128 devices in a mesh: sect: 8 (over z, core), blk: 16 (over x, y).
Axes of the slice: x: 4, y: 4, z: 4, core: 2. Of those that a mesh axis runs over, the one named last changes fastest.
Arguments:
- left_boundary: bfloat16 [8, 17, 64, 128, 128], P('sect', None, 'blk'), may hold values from -4 to 4, as said below
- right_boundary: bfloat16 [8, 17, 64, 128, 128], P('sect', None, 'blk'), may hold values from -4 to 4, as said below
- psi_start: float32 [8, 384, 128, 128], P('sect', 'blk'), may hold values from -6 to 6
- left_local: int32 [8, 384], P('sect'), may hold values from 0 to 3
- right_group: int32 [8, 384, 1], P('sect'), may hold values from 0 to 15; in each aligned block of 24 rows (0 to 23, 24 to 47, ..., all dimensions but the last counted through in order) at most 2 rows name the same one
- right_local: int32 [8, 384], P('sect'), may hold values from 0 to 3
- left_dims: int32 [8, 64], P('sect'), may hold values from 64 to 128
- right_dims: int32 [8, 64], P('sect'), may hold values from 64 to 128
- left_mix: float32 [17, 17], replicated, may hold values from -1.5 to 1.5
- right_mix: float32 [17, 17], replicated, may hold values from -1.5 to 1.5
Outputs:
- wave: bfloat16 [8, 384, 128, 128], P('sect', 'blk')
- energy: float32 [8], P('sect')
- left_grown: bfloat16 [8, 17, 64, 128, 128], P('sect', None, 'blk')
- right_grown: bfloat16 [8, 17, 64, 128, 128], P('sect', None, 'blk')
The draws below stay inside these ranges and needn't reach their ends.
Inputs may be any that keep to these rules, and one draw needn't show every extreme that they name: `right_group`: among the blocks e of each aligned run of 24 blocks of a section, at most 2 share one value, and some run reaches 2. `left_boundary`: every block of every channel and sector is symmetric. `right_boundary`: every block of every channel and sector is symmetric.
All inputs are finite; a program needn't handle non-finite values.
Results may differ from the reference program's by a relative error of at most 0.012.
Values may be sent and summed in bfloat16 or wider, within the bound.
A program may use at most 256 MiB of HBM per device.

```python
import math
import jax
import jax.numpy as jnp
import numpy as np
from jax import lax

P_SIZE = 128
K = 17
SEC_DEV = 4
E_DEV = 24
ITERS = 2
SECTORS = 64
ENTRIES = 384
CAP = 2
N_SECT = 8
N_BLK = 16


def env_blocks(key, spread):
    first, second = jax.random.split(key, 2)
    raw = jax.random.normal(first, (N_SECT, K, SECTORS, P_SIZE, P_SIZE), jnp.float32) * (spread / math.sqrt(P_SIZE))
    symmetric = (raw + jnp.swapaxes(raw, -1, -2)) * 0.5
    rows = jnp.arange(P_SIZE)[:, None]
    cols = jnp.arange(P_SIZE)[None, :]
    diagonal = jax.random.uniform(second, (N_SECT, K, SECTORS, 1, P_SIZE), jnp.float32, -0.5, 1.5)
    blocks = symmetric + jnp.where(rows == cols, 1.0, 0.0) * diagonal
    return jnp.clip(blocks, -4.0, 4.0).astype(jnp.bfloat16)


def draw_left_boundary(key, part):
    key = jax.random.fold_in(key, 11)
    return env_blocks(key, 1.0)


def draw_right_boundary(key, part):
    key = jax.random.fold_in(key, 23)
    return env_blocks(key, 1.0)


def plant(entries, rng, low, top_value):
    longest = entries.shape.index(max(entries.shape))
    spots = []
    for shift in (0, 1):
        where = [jax.random.randint(jax.random.fold_in(rng, axis), (), 0, length) for axis, length in enumerate(entries.shape)]
        where[longest] = (where[longest] + shift) % entries.shape[longest]
        spots.append(tuple(where))
    return entries.at[spots[0]].set(low).at[spots[1]].set(top_value)


def shard_levels(key, shape, cuts, least, largest):
    def one(position, parts):
        draws = jax.random.uniform(jax.random.fold_in(jax.random.fold_in(key, 6), position), (parts,), jnp.float32, least / len(cuts), largest / len(cuts))
        return jnp.repeat(jnp.exp(draws), shape[position] // parts).reshape((-1,) + (1,) * (len(shape) - position - 1))

    factor_of = one(*cuts[0])
    for cut in cuts[1:]:
        factor_of = factor_of * one(*cut)
    return factor_of


def routed_block(rng, own, number, rows, amount, top, bound, lean):
    sequence = jax.random.permutation(rng, amount)
    heavy_load, usual = shares(amount, rows * top, bound, lean, True), shares(amount, rows * top, bound, lean, False)
    places = jnp.arange(amount)

    def named(lengths, rotation):
        used = int((lengths > 0).sum())
        fixed = max(1, used // 4)
        moved = fixed + (places - fixed + rotation * (used - fixed)) % max(1, amount - fixed)
        return jnp.zeros((amount,), jnp.int32).at[sequence[jnp.where(places < fixed, places, moved)]].set(jnp.asarray(lengths, jnp.int32))

    lengths = jnp.where(number % 4 == 0, named(heavy_load, number // 4), named(usual, number - number // 4 - 1))
    mixed = jax.random.permutation(jax.random.fold_in(own, 3), amount)
    giver, receiver = mixed[0:amount // 2 * 2:2], mixed[1:amount // 2 * 2:2]
    margin = jnp.minimum(lengths[giver] - 1, bound - lengths[receiver]) // 2
    margin = jnp.where((giver == sequence[0]) | (receiver == sequence[0]) | (lengths[receiver] == 0), 0, jnp.maximum(margin, 0))
    moved = jax.random.randint(jax.random.fold_in(own, 4), (amount // 2,), 0, 1 << 20) % (margin + 1)
    lengths = lengths.at[giver].add(-moved).at[receiver].add(moved)
    members = jnp.searchsorted(jnp.cumsum(lengths), jnp.arange(rows * top), side="right").astype(jnp.int32)
    table = members.reshape(top, rows).T
    table = table[jax.random.permutation(jax.random.fold_in(own, 1), rows)]
    rotation = jax.random.randint(jax.random.fold_in(own, 2), (rows, 1), 0, top)
    return jnp.take_along_axis(table, (jnp.arange(top)[None, :] + rotation) % top, axis=1)


def shares(count, total, most, slope, full):
    weights = [(1 << 20) // math.isqrt(grade ** slope) + 1 for grade in range(1, count + 1)]
    largest = most if full else min(most, max(-(-total // count), total * weights[0] // sum(weights)))
    least = 1 if total - largest >= count - 1 else 0
    given, surplus = [largest] + [least] * (count - 1), total - largest - least * (count - 1)
    while surplus > 0:
        free = [i for i in range(1, count) if given[i] < largest] or [i for i in range(1, count) if given[i] < most]
        whole, left = sum([weights[i] for i in free]), surplus
        for i in free:
            addition = min(most - given[i], max(1, left * weights[i] // whole), surplus)
            given[i] = given[i] + addition
            surplus = surplus - addition
    return np.array(given)


def scatter_about(key, dims, scale, most, cuts=(), kind=jnp.bfloat16):
    result = jax.random.normal(key, dims, jnp.float32) * scale
    if len(cuts) > 0:
        result = shard_levels(key, dims, cuts, -0.22, 0.18) * result
    return jnp.clip(result, min=-most, max=most).astype(kind)


def setup_inputs(seed: int = 0) -> dict:
    arg_keys = jax.random.split(jax.random.key(seed), 11)
    left_boundary = draw_left_boundary(jax.random.fold_in(arg_keys[10], 71), 0)
    right_boundary = draw_right_boundary(jax.random.fold_in(arg_keys[10], 71), 0)
    psi_start = scatter_about(arg_keys[2], (N_SECT, ENTRIES, P_SIZE, P_SIZE), 1.0, 6.0, ((0, 8), (1, 16)), jnp.float32)
    left_local = plant(jax.random.randint(arg_keys[3], (N_SECT, ENTRIES), 0, SEC_DEV), jax.random.fold_in(arg_keys[3], 1), 0, SEC_DEV - 1).astype(jnp.int32)
    right_group_keys = jax.random.split(jax.random.fold_in(arg_keys[4], 1), N_SECT * ENTRIES // E_DEV)
    right_group_turns = jax.random.permutation(jax.random.fold_in(arg_keys[4], 3), N_SECT * ENTRIES // E_DEV)
    right_group = jax.vmap(lambda own, number: routed_block(jax.random.fold_in(arg_keys[4], 2), own, number, E_DEV, N_BLK, 1, CAP, 2))(right_group_keys, right_group_turns).reshape((N_SECT, ENTRIES, 1))
    right_local = plant(jax.random.randint(arg_keys[5], (N_SECT, ENTRIES), 0, SEC_DEV), jax.random.fold_in(arg_keys[5], 1), 0, SEC_DEV - 1).astype(jnp.int32)
    left_dims = plant(jax.random.randint(arg_keys[6], (N_SECT, SECTORS), P_SIZE // 2, P_SIZE + 1), jax.random.fold_in(arg_keys[6], 1), P_SIZE // 2, P_SIZE).astype(jnp.int32)
    right_dims = plant(jax.random.randint(arg_keys[7], (N_SECT, SECTORS), P_SIZE // 2, P_SIZE + 1), jax.random.fold_in(arg_keys[7], 1), P_SIZE // 2, P_SIZE).astype(jnp.int32)
    left_mix = scatter_about(arg_keys[8], (K, K), K ** -0.5, 1.5, (), jnp.float32)
    right_mix = scatter_about(arg_keys[9], (K, K), K ** -0.5, 1.5, (), jnp.float32)
    return dict(left_boundary=left_boundary, right_boundary=right_boundary, psi_start=psi_start, left_local=left_local, right_group=right_group, right_local=right_local, left_dims=left_dims, right_dims=right_dims, left_mix=left_mix, right_mix=right_mix)


EPSILON = 1e-06

def vacuum(channel):
    eye = jnp.eye(P_SIZE, dtype=jnp.float32)
    chan = (jnp.arange(K) == channel).astype(jnp.float32)
    blocks = chan[:, None, None, None] * eye[None, None, :, :] * jnp.ones((1, SECTORS, 1, 1), jnp.float32)
    return blocks.astype(jnp.bfloat16)

def reference(left_boundary, right_boundary, psi_start, left_local, right_group, right_local, left_dims, right_dims, left_mix, right_mix):
    hi = lax.Precision.HIGHEST
    waves, energies, lefts, rights = ([], [], [], [])
    inv_root = 1.0 / math.sqrt(P_SIZE)
    for section in range(N_SECT):
        lenv = left_boundary[section - 1] if section > 0 else vacuum(0)
        renv = right_boundary[section + 1] if section < N_SECT - 1 else vacuum(K - 1)
        lsec = (jnp.arange(ENTRIES, dtype=jnp.int32) // E_DEV * SEC_DEV + left_local[section]).astype(jnp.int32)
        rsec = (right_group[section, :, 0] * SEC_DEV + right_local[section]).astype(jnp.int32)
        lsel = jnp.take(lenv, lsec, axis=1).astype(jnp.float32)
        rsel = jnp.take(renv, rsec, axis=1).astype(jnp.float32)
        rows = jnp.arange(P_SIZE, dtype=jnp.int32)[None, :] < jnp.take(left_dims[section], lsec)[:, None]
        cols = jnp.arange(P_SIZE, dtype=jnp.int32)[None, :] < jnp.take(right_dims[section], rsec)[:, None]
        mask = jnp.logical_and(rows[:, :, None], cols[:, None, :]).astype(jnp.float32)

        def hamiltonian(vector):
            rounded = lax.optimization_barrier(vector.astype(jnp.bfloat16)).astype(jnp.float32)
            inner = jnp.einsum('kexa,eab->kexb', lsel, rounded, precision=hi)
            inner = lax.optimization_barrier(inner.astype(jnp.bfloat16)).astype(jnp.float32)
            return jnp.einsum('kexb,kedb->exd', inner, rsel, precision=hi) * mask
        start = psi_start[section] * mask
        vector = start / jnp.sqrt(jnp.sum(start * start))
        image = hamiltonian(vector)
        ritz_value = jnp.float32(0.0)
        for iteration in range(ITERS):
            rayleigh = jnp.sum(vector * image)
            resid = image - rayleigh * vector
            coupling = jnp.sqrt(jnp.sum(resid * resid) + EPSILON)
            correction = resid / coupling
            corr_image = hamiltonian(correction)
            curvature = jnp.sum(correction * corr_image)
            ritz_value = 0.5 * (rayleigh + curvature) - jnp.sqrt(0.25 * (rayleigh - curvature) ** 2 + coupling * coupling)
            coef_old = curvature - ritz_value
            coef_new = -coupling
            length = jnp.sqrt(coef_old * coef_old + coef_new * coef_new)
            vector = (coef_old * vector + coef_new * correction) / length
            image = (coef_old * image + coef_new * corr_image) / length
        wave = (vector * (P_SIZE * math.sqrt(ENTRIES))).astype(jnp.bfloat16)
        wave_f = wave.astype(jnp.float32)
        first = jnp.einsum('kexa,eab->kexb', lsel, wave_f, precision=hi)
        first = lax.optimization_barrier(first.astype(jnp.bfloat16)).astype(jnp.float32)
        lterm = (jnp.einsum('eax,keab->kexb', wave_f, first, precision=hi) * inv_root).astype(jnp.bfloat16).astype(jnp.float32)
        right_hot = (rsec[:, None] == jnp.arange(SECTORS, dtype=jnp.int32)[None, :]).astype(jnp.float32)
        lsum = jnp.einsum('ej,kexb->kjxb', right_hot, lterm, precision=hi)
        left_new = jnp.einsum('kv,kjxb->vjxb', left_mix, lsum, precision=hi).astype(jnp.bfloat16)
        second = jnp.einsum('eab,kebd->kead', wave_f, rsel, precision=hi)
        second = lax.optimization_barrier(second.astype(jnp.bfloat16)).astype(jnp.float32)
        rterm = jnp.einsum('kead,ecd->keac', second, wave_f, precision=hi) * inv_root
        left_hot = (lsec[:, None] == jnp.arange(SECTORS, dtype=jnp.int32)[None, :]).astype(jnp.float32)
        rsum = jnp.einsum('ej,keac->kjac', left_hot, rterm, precision=hi)
        right_new = jnp.einsum('kv,kjac->vjac', right_mix, rsum, precision=hi).astype(jnp.bfloat16)
        waves.append(wave)
        energies.append(ritz_value)
        lefts.append(left_new)
        rights.append(right_new)
    return (jnp.stack(waves), jnp.stack(energies).astype(jnp.float32), jnp.stack(lefts), jnp.stack(rights))
```

```python
import math

import jax
import jax.numpy as jnp
from jax import lax
from jax.experimental import pallas as pl
from jax.experimental.pallas import tpu as pltpu
from jax.sharding import PartitionSpec as P

MESH = pl.DeviceIdType.MESH
F32 = jnp.float32
BF16 = jnp.bfloat16
EPSILON = 1e-06

N = 128
HALF = 64
SIDE = 4
SEC = 4
RANKS = 2
SLOTS = SIDE * SIDE * RANKS
RUN = 24
PACK = SEC * HALF + 16
UNROLL = 4
LAG = 2

SEND, SLOT_OF, LSEC, RSEC, LDIM, RDIM = 0, 32, 64, 96, 128, 160
ORD_R, KEEP_R, LAST_R, LIVE_R = 192, 224, 256, 272
ORD_L, KEEP_L, LAST_L, LIVE_L = 288, 320, 352, 368
TABLE = 384


def router(left_local, right_group, right_local, left_dims, right_dims, table, count):
    me = lax.axis_index("blk")
    my_x, my_y = me >> 2, me & 3

    def clear(i, _):
        table[SEND + i] = 0
        table[SLOT_OF + i] = 0
        table[LSEC + i] = (i >> 3) * SEC
        table[RSEC + i] = ((i & 7) >> 1) * SEC
        table[LDIM + i] = 0
        table[RDIM + i] = 0
        return 0

    lax.fori_loop(0, SLOTS, clear, 0)

    def zero_counts():
        for i in range(SIDE * SIDE):
            count[i] = 0

    zero_counts()

    def own(e, _):
        group = right_group[me * RUN + e]
        rank = jnp.minimum(count[group], RANKS - 1)
        count[group] = rank + 1
        slot = (group & 3) * 8 + (group >> 2) * 2 + rank
        table[SLOT_OF + e] = slot
        table[SEND + slot] = e
        return 0

    lax.fori_loop(0, RUN, own, 0)
    for source in range(SIDE):
        run = my_x * SIDE + source
        zero_counts()

        def other(e, _):
            at = run * RUN + e
            group = right_group[at]
            rank = jnp.minimum(count[group], RANKS - 1)
            count[group] = rank + 1

            @pl.when((group & 3) == my_y)
            def _():
                slot = source * 8 + (group >> 2) * 2 + rank
                left, right = left_local[at], right_local[at]
                table[LSEC + slot] = source * SEC + left
                table[RSEC + slot] = (group >> 2) * SEC + right
                table[LDIM + slot] = left_dims[run * SEC + left]
                table[RDIM + slot] = right_dims[group * SEC + right]

            return 0

        lax.fori_loop(0, RUN, other, 0)
    for key, order, keep, last, live in (
        (LSEC, ORD_R, KEEP_R, LAST_R, LIVE_R),
        (RSEC, ORD_L, KEEP_L, LAST_L, LIVE_L),
    ):
        zero_counts()

        def tally(s, _):
            sector = table[key + s]
            count[sector] = count[sector] + 1
            return 0

        lax.fori_loop(0, SLOTS, tally, 0)
        for g in range(SIDE):
            begin = jnp.int32(0)
            for j in range(SEC):
                sector = g * SEC + j
                amount = count[sector]
                count[sector] = g * 8 + begin
                table[live + sector] = jnp.minimum(amount, 1)
                begin = begin + amount
                table[last + sector] = jnp.maximum(begin - 1, 0)

        def place(s, _):
            sector = table[key + s]
            at = count[sector]
            count[sector] = at + 1
            table[order + at] = s
            return 0

        lax.fori_loop(0, SLOTS, place, 0)

        def compare(p, _):
            before = table[order + jnp.maximum(p - 1, 0)]
            same = table[key + table[order + p]] == table[key + before]
            table[keep + p] = jnp.where(jnp.logical_and((p & 7) != 0, same), 1, 0)
            return 0

        lax.fori_loop(0, SLOTS, compare, 0)


def dot(a, b):
    return jnp.dot(a, b, preferred_element_type=F32)


def triangle_masks():
    row = lax.broadcasted_iota(jnp.int32, (HALF, N), 0)
    col = lax.broadcasted_iota(jnp.int32, (HALF, N), 1)
    left = col < HALF
    below = jnp.logical_and(left, row > col)
    low = jnp.logical_and(col >= HALF, row > col - HALF)
    high = jnp.logical_and(col >= HALF, row < col - HALF)
    diag = row == col - HALF
    return below, left, low, high, diag


def pack(block, masks):
    below, _, _, _, diag = masks
    corner = block[HALF:]
    upper = jnp.where(below, pltpu.roll(corner, HALF, 1), block[:HALF])
    row = jnp.sum(jnp.where(diag, corner, 0.0), axis=0, keepdims=True)
    return upper, row


def unpack(packed, row, masks):
    below, above, left, low, high, diag = masks
    turned = jnp.concatenate([packed, packed], axis=0).T
    rolled = pltpu.roll(packed.astype(F32), HALF, 1).astype(BF16)
    top = packed * above + turned[:HALF] * below
    bottom = (
        turned[HALF:] * left
        + rolled * low
        + turned[:HALF] * high
        + jnp.broadcast_to(row, (HALF, N)).astype(BF16) * diag
    )
    return jnp.concatenate([top, bottom], axis=0)


def kernel(
    channels,
    table,
    left_mix,
    right_mix,
    left_hbm,
    right_hbm,
    psi,
    wave,
    energy,
    left_out,
    right_out,
    bound,
    cat,
    gath,
    outb,
    work,
    vec,
    vect,
    ret,
    stack,
    red,
    mine,
    local_sem,
    psi_send,
    psi_recv,
    z_send,
    z_recv,
    ring_send,
    ring_recv,
    red_send,
    red_recv,
    grow_send,
    grow_recv,
):
    n_sect = lax.axis_size("sect")
    sect = lax.axis_index("sect")
    me = lax.axis_index("blk")
    my_x, my_y = me // SIDE, me % SIDE
    up, down = (sect + 1) % n_sect, (sect + n_sect - 1) % n_sect
    half = channels // 2

    def along_y(step):
        return my_x * SIDE + (my_y + step) % SIDE

    def along_x(step):
        return ((my_x + step) % SIDE) * SIDE + my_y

    barrier = pltpu.get_barrier_semaphore()

    def greet(d, _):
        pl.semaphore_signal(
            barrier, inc=1, device_id={"blk": (me + d) % (SIDE * SIDE)}, device_id_type=MESH
        )
        return 0

    lax.fori_loop(1, SIDE * SIDE, greet, 0)
    pl.semaphore_signal(barrier, inc=1, device_id={"sect": up}, device_id_type=MESH)
    pl.semaphore_signal(barrier, inc=1, device_id={"sect": down}, device_id_type=MESH)

    loads = [
        pltpu.make_async_copy(left_hbm, bound.at[0], local_sem.at[0]),
        pltpu.make_async_copy(right_hbm, bound.at[1], local_sem.at[1]),
    ]
    for load in loads:
        load.start()

    def fill(i, _):
        ret[i] = psi[table[SEND + i]].astype(BF16)
        return 0

    lax.fori_loop(0, SLOTS, fill, 0)
    pl.semaphore_wait(barrier, SIDE * SIDE + 1)

    def psi_copy(step):
        to_y = (my_y + step) % SIDE
        return pltpu.make_async_remote_copy(
            src_ref=ret.at[pl.ds(to_y * 8, 8)],
            dst_ref=vec.at[pl.ds(my_y * 8, 8)],
            send_sem=psi_send.at[step - 1],
            recv_sem=psi_recv.at[step - 1],
            device_id={"blk": along_y(step)},
            device_id_type=MESH,
        )

    for step in (1, 3, 2):
        psi_copy(step).start()

    masks = triangle_masks()
    below, left, low, high, diag = masks
    ones = [jnp.where(m, 1.0, 0.0).astype(BF16) for m in (below, left, low, high, diag)]
    bits = (ones[0], jnp.where(below, 0.0, 1.0).astype(BF16), ones[1], ones[2], ones[3], ones[4])
    row16 = lax.broadcasted_iota(jnp.int32, (16, N), 0)
    eye_packed = jnp.where(
        lax.broadcasted_iota(jnp.int32, (HALF, N), 0) == lax.broadcasted_iota(jnp.int32, (HALF, N), 1),
        1.0,
        0.0,
    )
    eye_row = jnp.where(lax.broadcasted_iota(jnp.int32, (1, N), 1) >= HALF, 1.0, 0.0)

    def place(side):
        return my_y if side == 0 else my_x

    def z_copy(side, k):
        return pltpu.make_async_remote_copy(
            src_ref=outb.at[side, 3, k],
            dst_ref=gath.at[side, place(side), k],
            send_sem=z_send.at[side, k],
            recv_sem=z_recv.at[side, k],
            device_id={"sect": up if side == 0 else down},
            device_id_type=MESH,
        )

    for load in loads:
        load.wait()

    def pack_bound(k, _):
        for side in range(2):
            edge = sect == (n_sect - 1 if side == 0 else 0)
            here = k == (0 if side == 0 else channels - 1)
            rows = jnp.zeros((16, N), F32)
            for j in range(SEC):
                upper, row = pack(bound[side, k, j].astype(F32), masks)
                one = jnp.where(here, 1.0, 0.0)
                upper = jnp.where(edge, eye_packed * one, upper)
                row = jnp.where(edge, eye_row * one, row)
                outb[side, 3, k, pl.ds(j * HALF, HALF)] = upper.astype(BF16)
                rows = jnp.where(row16 == j, jnp.broadcast_to(row, (16, N)), rows)
            outb[side, 3, k, pl.ds(SEC * HALF, 16)] = rows.astype(BF16)
            z_copy(side, k).start()
        return 0

    lax.fori_loop(0, channels, pack_bound, 0)

    def ring_copy(side, which, k, back):
        at = place(side)
        if which == 2:
            at = (at + (1 if back else SIDE - 1)) % SIDE
        step = SIDE - 1 if back else 1
        return pltpu.make_async_remote_copy(
            src_ref=gath.at[side, at, k],
            dst_ref=gath.at[side, at, k],
            send_sem=ring_send.at[side, which, k],
            recv_sem=ring_recv.at[side, which, k],
            device_id={"blk": along_y(step) if side == 0 else along_x(step)},
            device_id_type=MESH,
        )

    def dims_mask(slot):
        rows = lax.broadcasted_iota(jnp.int32, (N, N), 0) < table[LDIM + slot]
        cols = lax.broadcasted_iota(jnp.int32, (N, N), 1) < table[RDIM + slot]
        return jnp.logical_and(rows, cols)

    X, HX, T, HT = 0, SLOTS, 2 * SLOTS, 3 * SLOTS

    def gather_step(t, _):
        @pl.when(t < channels)
        def _():
            for side in range(2):
                z_copy(side, t).wait_recv()
                ring_copy(side, 0, t, False).start()
                ring_copy(side, 1, t, True).start()

        @pl.when(jnp.logical_and(t >= 1, t < channels + 1))
        def _():
            k = t - 1
            for side in range(2):
                ring_copy(side, 0, k, False).wait_recv()
                ring_copy(side, 1, k, True).wait_recv()

            @pl.when(k % 2 == 0)
            def _():
                for side in range(2):
                    ring_copy(side, 2, k, False).start()

            @pl.when(k % 2 == 1)
            def _():
                for side in range(2):
                    ring_copy(side, 2, k, True).start()

        @pl.when(t == LAG)
        def _():
            for step in (1, 3, 2):
                psi_copy(step).wait_recv()
            for i in range(8):
                vec[my_y * 8 + i] = ret[my_y * 8 + i]

            def start(i, _):
                vec[i] = jnp.where(dims_mask(i), vec[i].astype(F32), 0.0).astype(BF16)
                work[HX + i] = jnp.zeros((N, N), F32)
                return 0

            lax.fori_loop(0, SLOTS, start, 0)

        @pl.when(t >= LAG)
        def _():
            k = t - LAG
            for side in range(2):
                ring_copy(side, 2, k, False).wait_recv()

            def open_group(g, _):
                for side in range(2):
                    rows = gath[side, g, k, pl.ds(SEC * HALF, 16)].astype(F32)
                    for j in range(SEC):
                        row = jnp.sum(jnp.where(row16 == j, rows, 0.0), axis=0, keepdims=True)
                        packed = gath[side, g, k, pl.ds(j * HALF, HALF)]
                        cat[side, g * SEC + j, k] = unpack(packed, row, bits)
                return 0

            lax.fori_loop(0, SIDE, open_group, 0)

            def apply(i, _):
                slots = [i * UNROLL + u for u in range(UNROLL)]
                inner = [dot(vec[s], cat[1, table[RSEC + s], k]).astype(BF16) for s in slots]
                for s, z in zip(slots, inner):
                    work[HX + s] += dot(cat[0, table[LSEC + s], k], z)
                return 0

            lax.fori_loop(0, SLOTS // UNROLL, apply, 0)

        return 0

    lax.fori_loop(0, channels + LAG, gather_step, 0)

    for step in (1, 3, 2):
        psi_copy(step).wait_send()

    def settle(k, _):
        for side in range(2):
            z_copy(side, k).wait_send()
            for which in range(3):
                ring_copy(side, which, k, False).wait_send()
        return 0

    lax.fori_loop(0, channels, settle, 0)

    def fold(block):
        return jnp.sum(block.reshape(N // 8, 8, N), axis=0)

    def exchange(number, parts):
        rows = [jnp.sum(p, axis=0, keepdims=True) for p in parts]
        rows += [jnp.zeros((1, N), F32)] * (8 - len(rows))
        mine[number] = jnp.concatenate(rows, axis=0)

        def copy(d):
            return pltpu.make_async_remote_copy(
                src_ref=mine.at[number],
                dst_ref=red.at[number, me],
                send_sem=red_send.at[number, d],
                recv_sem=red_recv.at[number, d],
                device_id={"blk": (me + d) % (SIDE * SIDE)},
                device_id_type=MESH,
            )

        def begin(d, _):
            copy(d).start()
            return 0

        lax.fori_loop(1, SIDE * SIDE, begin, 0)
        red[number, me] = mine[number]

        def end(d, _):
            copy(d).wait()
            return 0

        lax.fori_loop(1, SIDE * SIDE, end, 0)
        total = jnp.sum(red[number], axis=0)
        total = jnp.broadcast_to(jnp.sum(total, axis=1, keepdims=True), (8, N))
        return [total[i : i + 1] for i in range(len(parts))]

    zero8 = jnp.zeros((8, N), F32)

    def first_sums(s, sums):
        ss, sh, hh = sums
        start = vec[s].astype(F32)
        image = jnp.where(dims_mask(s), work[HX + s], 0.0)
        work[HX + s] = image
        return ss + fold(start * start), sh + fold(start * image), hh + fold(image * image)

    ss, sh, hh = exchange(0, lax.fori_loop(0, SLOTS, first_sums, (zero8,) * 3))
    norm = jnp.sqrt(ss)
    xx = ss / (norm * norm)
    a = sh / (norm * norm)
    hxhx = hh / (norm * norm)
    b = jnp.sqrt(jnp.maximum(hxhx - 2.0 * a * a + a * a * xx, 0.0) + EPSILON)

    def first_residual(s, _):
        x = vec[s].astype(F32) / norm
        hx = work[HX + s] / norm
        t = (hx - a * x) / b
        work[X + s] = x
        work[HX + s] = hx
        work[T + s] = t
        vec[s] = t.astype(BF16)
        return 0

    lax.fori_loop(0, SLOTS, first_residual, 0)

    def beside(side, sector):
        return jnp.concatenate([cat[side, sector, k] for k in range(channels)], axis=1)

    def hamiltonian(i, _):
        slots = [i * UNROLL + u for u in range(UNROLL)]
        inner = []
        for s in slots:
            z = dot(vec[s], beside(1, table[RSEC + s])).astype(BF16)
            inner.append(jnp.concatenate([z[:, k * N : (k + 1) * N] for k in range(channels)], axis=0))
        for s, z in zip(slots, inner):
            work[HT + s] = jnp.where(dims_mask(s), dot(beside(0, table[LSEC + s]), z), 0.0)
        return 0

    lax.fori_loop(0, SLOTS // UNROLL, hamiltonian, 0)

    def second_sums(s, sums):
        x, hx, t, ht = work[X + s], work[HX + s], work[T + s], work[HT + s]
        terms = (x * t, t * t, x * ht, t * hx, t * ht, hx * ht, ht * ht)
        return tuple(old + fold(term) for old, term in zip(sums, terms))

    xt, tt, xht, thx, c, hxht, htht = exchange(
        1, lax.fori_loop(0, SLOTS, second_sums, (zero8,) * 7)
    )

    def ritz(a, b, c):
        value = 0.5 * (a + c) - jnp.sqrt(0.25 * (a - c) * (a - c) + b * b)
        old, new = c - value, -b
        length = jnp.sqrt(old * old + new * new)
        return value, old / length, new / length

    _, p, q = ritz(a, b, c)
    a2 = p * p * a + p * q * (xht + thx) + q * q * c
    xx2 = p * p * xx + 2.0 * p * q * xt + q * q * tt
    hxhx2 = p * p * hxhx + 2.0 * p * q * hxht + q * q * htht
    b2 = jnp.sqrt(jnp.maximum(hxhx2 - 2.0 * a2 * a2 + a2 * a2 * xx2, 0.0) + EPSILON)

    def second_residual(s, _):
        x = p * work[X + s] + q * work[T + s]
        hx = p * work[HX + s] + q * work[HT + s]
        t = (hx - a2 * x) / b2
        work[X + s] = x
        work[T + s] = t
        vec[s] = t.astype(BF16)
        return 0

    lax.fori_loop(0, SLOTS, second_residual, 0)
    lax.fori_loop(0, SLOTS // UNROLL, hamiltonian, 0)

    def third_sums(s, total):
        return total + fold(work[T + s] * work[HT + s])

    (c2,) = exchange(2, [lax.fori_loop(0, SLOTS, third_sums, zero8)])
    value, p2, q2 = ritz(a2, b2, c2)
    energy[...] = jnp.broadcast_to(value, (8, N))
    scale = N * math.sqrt(RUN * SIDE * SIDE)

    def final_vector(s, _):
        w = ((p2 * work[X + s] + q2 * work[T + s]) * scale).astype(BF16)
        vec[s] = w
        vect[s] = w.T
        return 0

    lax.fori_loop(0, SLOTS, final_vector, 0)

    def wave_copy(step):
        to_y = (my_y + step) % SIDE
        return pltpu.make_async_remote_copy(
            src_ref=vec.at[pl.ds(to_y * 8, 8)],
            dst_ref=ret.at[pl.ds(my_y * 8, 8)],
            send_sem=psi_send.at[step + 2],
            recv_sem=psi_recv.at[step + 2],
            device_id={"blk": along_y(step)},
            device_id_type=MESH,
        )

    def grow(kind, group, to):
        order, keep, last, live = (
            (ORD_L, KEEP_L, LAST_L, LIVE_L) if kind == 0 else (ORD_R, KEEP_R, LAST_R, LIVE_R)
        )
        outer, sector_at = (vect, LSEC) if kind == 0 else (vec, RSEC)
        closing = vec if kind == 0 else vect

        def term(i, _):
            spots = [i * 2 + u for u in range(2)]
            for u, spot in enumerate(spots):
                slot = table[order + group * 8 + spot]
                z = dot(outer[slot], beside(kind, table[sector_at + slot])).astype(BF16)
                for k in range(channels):
                    stack[u, k] = z[:, k * N : (k + 1) * N]
            for u, spot in enumerate(spots):
                slot = table[order + group * 8 + spot]
                stay = table[keep + group * 8 + spot] > 0
                right = closing[slot]
                for k in range(channels):
                    before = work[jnp.maximum(spot - 1, 0) * channels + k]
                    work[spot * channels + k] = dot(stack[u, k], right) + jnp.where(stay, before, 0.0)
            return 0

        lax.fori_loop(0, 4, term, 0)

        def close(k, _):
            rows = jnp.zeros((16, N), F32)
            for j in range(SEC):
                spot = table[last + group * SEC + j]
                has = table[live + group * SEC + j] > 0
                upper, row = pack(work[spot * channels + k], masks)
                outb[kind, to, k, pl.ds(j * HALF, HALF)] = jnp.where(has, upper, 0.0).astype(BF16)
                row = jnp.where(has, row, 0.0)
                rows = jnp.where(row16 == j, jnp.broadcast_to(row, (16, N)), rows)
            outb[kind, to, k, pl.ds(SEC * HALF, 16)] = rows.astype(BF16)
            return 0

        lax.fori_loop(0, channels, close, 0)

    first, second = pl.ds(0, half), pl.ds(half, channels - half)

    def grow_copy(kind, number):
        source, target, part, back = (
            (0, 0, first, False),
            (0, 0, second, True),
            (1, 1, second, False),
            (1, 1, first, False),
            (2, 2, first, True),
            (2, 2, second, True),
        )[number]
        step = SIDE - 1 if back else 1
        return pltpu.make_async_remote_copy(
            src_ref=outb.at[kind, source, part],
            dst_ref=gath.at[kind, target, part],
            send_sem=grow_send.at[kind, number],
            recv_sem=grow_recv.at[kind, number],
            device_id={"blk": along_x(step) if kind == 0 else along_y(step)},
            device_id_type=MESH,
        )

    def my_group(kind, step):
        return ((my_x if kind == 0 else my_y) + step) % SIDE

    for kind in range(2):
        grow(kind, my_group(kind, 2), 0)
        grow_copy(kind, 0).start()
        grow_copy(kind, 1).start()
    for kind in range(2):
        grow(kind, my_group(kind, 1), 1)
        grow_copy(kind, 2).start()
    for step in (1, 3, 2):
        wave_copy(step).start()
    for kind in range(2):
        grow(kind, my_group(kind, SIDE - 1), 2)
        grow_copy(kind, 4).start()
    for kind in range(2):
        grow_copy(kind, 0).wait_recv()

        def add_first(k, _):
            outb[kind, 1, k] = (outb[kind, 1, k].astype(F32) + gath[kind, 0, k].astype(F32)).astype(BF16)
            return 0

        lax.fori_loop(0, half, add_first, 0)
        grow_copy(kind, 3).start()
        grow_copy(kind, 1).wait_recv()

        def add_second(k, _):
            outb[kind, 2, k] = (outb[kind, 2, k].astype(F32) + gath[kind, 0, k].astype(F32)).astype(BF16)
            return 0

        lax.fori_loop(half, channels, add_second, 0)
        grow_copy(kind, 5).start()
    for kind in range(2):
        grow(kind, my_group(kind, 0), 3)

    for step in (1, 3, 2):
        wave_copy(step).wait_recv()
    for i in range(8):
        ret[my_y * 8 + i] = vec[my_y * 8 + i]

    def take(e, _):
        wave[e] = ret[table[SLOT_OF + e]]
        return 0

    lax.fori_loop(0, RUN, take, 0)

    shrink = 1.0 / math.sqrt(N)
    stores = []
    for kind in range(2):
        mix = left_mix if kind == 0 else right_mix
        for number in (2, 3, 4, 5):
            grow_copy(kind, number).wait_recv()

        def add_all(k, _):
            for j in range(SEC):
                part = pl.ds(j * HALF, HALF)
                total = (
                    outb[kind, 3, k, part].astype(F32)
                    + gath[kind, 1, k, part].astype(F32)
                    + gath[kind, 2, k, part].astype(F32)
                )
                work[j * channels + k, pl.ds(0, HALF)] = total * shrink
            part = pl.ds(SEC * HALF, 16)
            rows = (
                outb[kind, 3, k, part].astype(F32)
                + gath[kind, 1, k, part].astype(F32)
                + gath[kind, 2, k, part].astype(F32)
            )
            work[SEC * channels + k, pl.ds(0, 16)] = rows * shrink
            return 0

        lax.fori_loop(0, channels, add_all, 0)

        def blend(v, _):
            factors = [mix[k * channels + v] for k in range(channels)]
            rows = factors[0] * work[SEC * channels, pl.ds(0, 16)]
            for k in range(1, channels):
                rows = rows + factors[k] * work[SEC * channels + k, pl.ds(0, 16)]
            for j in range(SEC):
                upper = factors[0] * work[j * channels, pl.ds(0, HALF)]
                for k in range(1, channels):
                    upper = upper + factors[k] * work[j * channels + k, pl.ds(0, HALF)]
                row = jnp.sum(jnp.where(row16 == j, rows, 0.0), axis=0, keepdims=True)
                bound[kind, v, j] = unpack(upper.astype(BF16), row, bits)
            return 0

        lax.fori_loop(0, channels, blend, 0)
        store = pltpu.make_async_copy(
            bound.at[kind], left_out if kind == 0 else right_out, local_sem.at[kind]
        )
        store.start()
        stores.append(store)
    for store in stores:
        store.wait()
    for step in (1, 3, 2):
        wave_copy(step).wait_send()
    for kind in range(2):
        for number in range(6):
            grow_copy(kind, number).wait_send()


def body(
    left_boundary,
    right_boundary,
    psi_start,
    left_local,
    right_group,
    right_local,
    left_dims,
    right_dims,
    left_mix,
    right_mix,
):
    channels = left_boundary.shape[1]
    smem = pl.BlockSpec(memory_space=pltpu.SMEM)
    vmem = pl.BlockSpec(memory_space=pltpu.VMEM)
    hbm = pl.BlockSpec(memory_space=pl.ANY)
    table = pl.pallas_call(
        router,
        out_shape=jax.ShapeDtypeStruct((TABLE,), jnp.int32),
        in_specs=[smem] * 5,
        out_specs=smem,
        scratch_shapes=[pltpu.SMEM((16,), jnp.int32)],
        name="router",
    )(
        left_local.reshape(-1),
        right_group.reshape(-1),
        right_local.reshape(-1),
        left_dims.reshape(-1),
        right_dims.reshape(-1),
    )
    dma = pltpu.SemaphoreType.DMA
    env = (channels, SEC, N, N)
    wave, energy, left_grown, right_grown = pl.pallas_call(
        lambda *refs: kernel(channels, *refs),
        out_shape=(
            jax.ShapeDtypeStruct((RUN, N, N), BF16),
            jax.ShapeDtypeStruct((8, N), F32),
            jax.ShapeDtypeStruct(env, BF16),
            jax.ShapeDtypeStruct(env, BF16),
        ),
        in_specs=[smem, smem, smem, hbm, hbm, vmem],
        out_specs=(vmem, vmem, hbm, hbm),
        scratch_shapes=[
            pltpu.VMEM((2,) + env, BF16),
            pltpu.VMEM((2, SIDE * SEC, channels, N, N), BF16),
            pltpu.VMEM((2, SIDE, channels, PACK, N), BF16),
            pltpu.VMEM((2, SIDE, channels, PACK, N), BF16),
            pltpu.VMEM((max(4 * SLOTS, 8 * channels), N, N), F32),
            pltpu.VMEM((SLOTS, N, N), BF16),
            pltpu.VMEM((SLOTS, N, N), BF16),
            pltpu.VMEM((SLOTS, N, N), BF16),
            pltpu.VMEM((2, channels, N, N), BF16),
            pltpu.VMEM((3, SIDE * SIDE, 8, N), F32),
            pltpu.VMEM((3, 8, N), F32),
            dma((2,)),
            dma((6,)),
            dma((6,)),
            dma((2, channels)),
            dma((2, channels)),
            dma((2, 3, channels)),
            dma((2, 3, channels)),
            dma((3, SIDE * SIDE)),
            dma((3, SIDE * SIDE)),
            dma((2, 6)),
            dma((2, 6)),
        ],
        compiler_params=pltpu.CompilerParams(
            collective_id=0, has_side_effects=True, vmem_limit_bytes=62 * 2**20
        ),
        name="davidson",
    )(
        table,
        left_mix.reshape(-1),
        right_mix.reshape(-1),
        left_boundary[0],
        right_boundary[0],
        psi_start[0],
    )
    return wave[None], energy[0, :1], left_grown[None], right_grown[None]


def solution(mesh):
    return jax.shard_map(
        body,
        mesh=mesh,
        in_specs=(
            P("sect", None, "blk", None, None),
            P("sect", None, "blk", None, None),
            P("sect", "blk", None, None),
            P("sect", None),
            P("sect", None, None),
            P("sect", None),
            P("sect", None),
            P("sect", None),
            P(),
            P(),
        ),
        out_specs=(
            P("sect", "blk", None, None),
            P("sect"),
            P("sect", None, "blk", None, None),
            P("sect", None, "blk", None, None),
        ),
        check_vma=False,
    )
```

```python
import math

import jax
import jax.numpy as jnp
from jax import lax
from jax.experimental import pallas as pl
from jax.experimental.pallas import tpu as pltpu
from jax.sharding import PartitionSpec as P

MESH = pl.DeviceIdType.MESH
F32 = jnp.float32
BF16 = jnp.bfloat16
EPSILON = 1e-06

N = 128
HALF = 64
SIDE = 4
SEC = 4
RANKS = 2
SLOTS = SIDE * SIDE * RANKS
RUN = 24
PACK = SEC * HALF + 16
UNROLL = 4
AHEAD = 3

SEND, SLOT_OF, LSEC, RSEC, LDIM, RDIM = 0, 32, 64, 96, 128, 160
ORD_R, KEEP_R, LAST_R, LIVE_R = 192, 224, 256, 272
ORD_L, KEEP_L, LAST_L, LIVE_L = 288, 320, 352, 368
SPARE = 384 - LSEC
TABLE = 512


def places(me, swap):
    x, y = me // SIDE, me % SIDE
    return x * (1 - swap) + y * swap, y * (1 - swap) + x * swap


def device_at(u, w, swap):
    return (u * SIDE + w) * (1 - swap) + (w * SIDE + u) * swap


def router(left_local, right_group, right_local, left_dims, right_dims, table, count):
    me = lax.axis_index("blk")
    swap = lax.axis_index("sect") & 1
    my_u, my_w = places(me, swap)
    for i in range(SLOTS):
        table[SEND + i] = 0
        table[LSEC + i] = (i // 8) * SEC
        table[RSEC + i] = (i % 8 // 2) * SEC
        table[LDIM + i] = 0
        table[RDIM + i] = 0

    def zero_counts():
        for i in range(SIDE * SIDE):
            count[i] = 0

    def split(group):
        x, y = group >> 2, group & 3
        return x * (1 - swap) + y * swap, y * (1 - swap) + x * swap

    zero_counts()
    for e in range(RUN):
        group = right_group[0, me * RUN + e]
        rank = jnp.minimum(count[group], RANKS - 1)
        count[group] = rank + 1
        u, w = split(group)
        slot = w * 8 + u * 2 + rank
        table[SLOT_OF + e] = slot
        table[SEND + slot] = e
    for source in range(SIDE):
        run = device_at(my_u, source, swap)
        zero_counts()
        for e in range(RUN):
            at = run * RUN + e
            group = right_group[0, at]
            rank = jnp.minimum(count[group], RANKS - 1)
            count[group] = rank + 1
            u, w = split(group)
            slot = jnp.where(w == my_w, source * 8 + u * 2 + rank, SPARE)
            left, right = left_local[0, at], right_local[0, at]
            table[LSEC + slot] = source * SEC + left
            table[RSEC + slot] = u * SEC + right
            table[LDIM + slot] = left_dims[0, run * SEC + left]
            table[RDIM + slot] = right_dims[0, group * SEC + right]
    for key, order, keep, last, live in (
        (LSEC, ORD_R, KEEP_R, LAST_R, LIVE_R),
        (RSEC, ORD_L, KEEP_L, LAST_L, LIVE_L),
    ):
        zero_counts()
        for s in range(SLOTS):
            sector = table[key + s]
            count[sector] = count[sector] + 1
        for g in range(SIDE):
            begin = jnp.int32(0)
            for j in range(SEC):
                sector = g * SEC + j
                amount = count[sector]
                count[sector] = g * 8 + begin
                table[live + sector] = jnp.minimum(amount, 1)
                begin = begin + amount
                table[last + sector] = jnp.maximum(begin - 1, 0)
        for s in range(SLOTS):
            sector = table[key + s]
            at = count[sector]
            count[sector] = at + 1
            table[order + at] = s
        for g in range(SIDE):
            before = jnp.int32(-1)
            for p in range(g * 8, g * 8 + 8):
                sector = table[key + table[order + p]]
                table[keep + p] = jnp.where(sector == before, 1, 0)
                before = sector


def dot(a, b):
    return jnp.dot(a, b, preferred_element_type=F32)


def triangle_masks():
    row = lax.broadcasted_iota(jnp.int32, (HALF, N), 0)
    col = lax.broadcasted_iota(jnp.int32, (HALF, N), 1)
    left = col < HALF
    below = jnp.logical_and(left, row > col)
    low = jnp.logical_and(col >= HALF, row > col - HALF)
    high = jnp.logical_and(col >= HALF, row < col - HALF)
    diag = row == col - HALF
    return below, left, low, high, diag


def pack(block, masks):
    below, _, _, _, diag = masks
    corner = block[HALF:]
    upper = jnp.where(below, pltpu.roll(corner, HALF, 1), block[:HALF])
    row = jnp.sum(jnp.where(diag, corner, 0.0), axis=0, keepdims=True)
    return upper, row


def unpack(packed, row, masks):
    below, above, left, low, high, diag = masks
    turned = jnp.concatenate([packed, packed], axis=0).T
    rolled = pltpu.roll(packed.astype(F32), HALF, 1).astype(BF16)
    top = packed * above + turned[:HALF] * below
    bottom = (
        turned[HALF:] * left
        + rolled * low
        + turned[:HALF] * high
        + jnp.broadcast_to(row, (HALF, N)).astype(BF16) * diag
    )
    return jnp.concatenate([top, bottom], axis=0)


def kernel(
    channels,
    table,
    left_mix,
    right_mix,
    left_hbm,
    right_hbm,
    psi,
    wave,
    energy,
    left_out,
    right_out,
    bound,
    cat,
    gath,
    outb,
    work,
    vec,
    vect,
    ret,
    stack,
    red,
    mine,
    local_sem,
    store_sem,
    psi_send,
    psi_recv,
    z_send,
    z_recv,
    ring_send,
    ring_recv,
    red_send,
    red_recv,
    grow_send,
    grow_recv,
):
    n_sect = lax.axis_size("sect")
    sect = lax.axis_index("sect")
    me = lax.axis_index("blk")
    swap = sect % 2
    my_u, my_w = places(me, swap)
    up, down = (sect + 1) % n_sect, (sect + n_sect - 1) % n_sect
    deep = channels * HALF + 32
    region = max(channels * PACK, SEC * deep)

    def along(side, step):
        if side == 0:
            return device_at(my_u, (my_w + step) % SIDE, swap)
        return device_at((my_u + step) % SIDE, my_w, swap)

    def rows_of(group, k):
        return pl.ds(pl.multiple_of(group * region + k * PACK, 16), PACK)

    def sector_rows(place, j):
        return pl.ds(pl.multiple_of(place * region + j * deep, 16), deep)

    barrier = pltpu.get_barrier_semaphore()

    def greet(d, _):
        pl.semaphore_signal(
            barrier, inc=1, device_id={"blk": (me + d) % (SIDE * SIDE)}, device_id_type=MESH
        )
        return 0

    lax.fori_loop(1, SIDE * SIDE, greet, 0)
    pl.semaphore_signal(barrier, inc=1, device_id={"sect": up}, device_id_type=MESH)
    pl.semaphore_signal(barrier, inc=1, device_id={"sect": down}, device_id_type=MESH)

    loads = [
        pltpu.make_async_copy(left_hbm, bound.at[0], local_sem.at[0]),
        pltpu.make_async_copy(right_hbm, bound.at[1], local_sem.at[1]),
    ]
    for load in loads:
        load.start()

    def fill(i, _):
        ret[i] = psi[table[SEND + i]].astype(BF16)
        return 0

    lax.fori_loop(0, SLOTS, fill, 0)
    pl.semaphore_wait(barrier, SIDE * SIDE + 1)

    def psi_copy(step):
        to_w = (my_w + step) % SIDE
        return pltpu.make_async_remote_copy(
            src_ref=ret.at[pl.ds(to_w * 8, 8)],
            dst_ref=vec.at[pl.ds(my_w * 8, 8)],
            send_sem=psi_send.at[step - 1],
            recv_sem=psi_recv.at[step - 1],
            device_id={"blk": along(0, step)},
            device_id_type=MESH,
        )

    for step in (1, 3, 2):
        psi_copy(step).start()

    masks = triangle_masks()
    below, left, low, high, diag = masks
    ones = [jnp.where(m, 1.0, 0.0).astype(BF16) for m in (below, left, low, high, diag)]
    bits = (ones[0], jnp.where(below, 0.0, 1.0).astype(BF16), ones[1], ones[2], ones[3], ones[4])
    row32 = lax.broadcasted_iota(jnp.int32, (32, N), 0)
    row16 = lax.broadcasted_iota(jnp.int32, (16, N), 0)
    eye_packed = jnp.where(
        lax.broadcasted_iota(jnp.int32, (HALF, N), 0) == lax.broadcasted_iota(jnp.int32, (HALF, N), 1),
        1.0,
        0.0,
    )
    eye_row = jnp.where(lax.broadcasted_iota(jnp.int32, (1, N), 1) >= HALF, 1.0, 0.0)

    def place(side):
        return my_w if side == 0 else my_u

    def z_copy(side, k):
        return pltpu.make_async_remote_copy(
            src_ref=outb.at[side, rows_of(3, k)],
            dst_ref=gath.at[side, rows_of(place(1 - side), k)],
            send_sem=z_send.at[side, k],
            recv_sem=z_recv.at[side, k],
            device_id={"sect": up if side == 0 else down},
            device_id_type=MESH,
        )

    def pack_bound(k):
        for side in range(2):
            edge = sect == (n_sect - 1 if side == 0 else 0)
            here = k == (0 if side == 0 else channels - 1)
            one = jnp.where(here, 1.0, 0.0)
            rows = jnp.zeros((16, N), F32)
            base = 3 * region + k * PACK
            for j in range(SEC):
                upper, row = pack(bound[side, k, j].astype(F32), masks)
                upper = jnp.where(edge, eye_packed * one, upper)
                row = jnp.where(edge, eye_row * one, row)
                outb[side, pl.ds(pl.multiple_of(base + j * HALF, 16), HALF)] = upper.astype(BF16)
                rows = jnp.where(row16 == j, jnp.broadcast_to(row, (16, N)), rows)
            outb[side, pl.ds(pl.multiple_of(base + SEC * HALF, 16), 16)] = rows.astype(BF16)
            z_copy(side, k).start()

    def ring_copy(side, which, k, back):
        at = place(side)
        if which == 2:
            at = (at + (1 if back else SIDE - 1)) % SIDE
        step = SIDE - 1 if back else 1
        return pltpu.make_async_remote_copy(
            src_ref=gath.at[side, rows_of(at, k)],
            dst_ref=gath.at[side, rows_of(at, k)],
            send_sem=ring_send.at[side, which, k],
            recv_sem=ring_recv.at[side, which, k],
            device_id={"blk": along(side, step)},
            device_id_type=MESH,
        )

    def dims_mask(slot):
        rows = lax.broadcasted_iota(jnp.int32, (N, N), 0) < table[LDIM + slot]
        cols = lax.broadcasted_iota(jnp.int32, (N, N), 1) < table[RDIM + slot]
        return jnp.logical_and(rows, cols)

    X, HX, T, HT = 0, SLOTS, 2 * SLOTS, 3 * SLOTS

    for load in loads:
        load.wait()

    def gather_step(t, _):
        @pl.when(t < channels)
        def _():
            pack_bound(t)

        @pl.when(jnp.logical_and(t >= AHEAD, t < channels + AHEAD))
        def _():
            k = t - AHEAD
            for side in range(2):
                z_copy(side, k).wait_recv()
                ring_copy(side, 0, k, False).start()
                ring_copy(side, 1, k, True).start()

        @pl.when(jnp.logical_and(t >= 2 * AHEAD, t < channels + 2 * AHEAD))
        def _():
            k = t - 2 * AHEAD
            for side in range(2):
                ring_copy(side, 0, k, False).wait_recv()
                ring_copy(side, 1, k, True).wait_recv()

            @pl.when(k % 2 == 0)
            def _():
                for side in range(2):
                    ring_copy(side, 2, k, False).start()

            @pl.when(k % 2 == 1)
            def _():
                for side in range(2):
                    ring_copy(side, 2, k, True).start()

        @pl.when(t == 3 * AHEAD)
        def _():
            for step in (1, 3, 2):
                psi_copy(step).wait_recv()
            for i in range(8):
                vec[my_w * 8 + i] = ret[my_w * 8 + i]

            def start(i, _):
                vec[i] = jnp.where(dims_mask(i), vec[i].astype(F32), 0.0).astype(BF16)
                work[HX + i] = jnp.zeros((N, N), F32)
                return 0

            lax.fori_loop(0, SLOTS, start, 0)

        @pl.when(t >= 3 * AHEAD)
        def _():
            k = t - 3 * AHEAD
            for side in range(2):
                ring_copy(side, 2, k, False).wait_recv()

            def open_group(g, _):
                base = g * region + k * PACK
                for side in range(2):
                    rows = gath[side, pl.ds(pl.multiple_of(base + SEC * HALF, 16), 16)].astype(F32)
                    for j in range(SEC):
                        row = jnp.sum(jnp.where(row16 == j, rows, 0.0), axis=0, keepdims=True)
                        packed = gath[side, pl.ds(pl.multiple_of(base + j * HALF, 16), HALF)]
                        cat[side, g * SEC + j, k] = unpack(packed, row, bits)
                return 0

            lax.fori_loop(0, SIDE, open_group, 0)

            def apply(i, _):
                slots = [i * UNROLL + u for u in range(UNROLL)]
                inner = [dot(vec[s], cat[1, table[RSEC + s], k]).astype(BF16) for s in slots]
                for s, z in zip(slots, inner):
                    work[HX + s] += dot(cat[0, table[LSEC + s], k], z)
                return 0

            lax.fori_loop(0, SLOTS // UNROLL, apply, 0)

        return 0

    lax.fori_loop(0, channels + 3 * AHEAD, gather_step, 0)

    for step in (1, 3, 2):
        psi_copy(step).wait_send()

    def settle(k, _):
        for side in range(2):
            z_copy(side, k).wait_send()
            for which in range(3):
                ring_copy(side, which, k, False).wait_send()
        return 0

    lax.fori_loop(0, channels, settle, 0)

    def fold(block):
        return jnp.sum(block.reshape(N // 8, 8, N), axis=0)

    def exchange(number, parts):
        rows = [jnp.sum(p, axis=0, keepdims=True) for p in parts]
        rows += [jnp.zeros((1, N), F32)] * (8 - len(rows))
        mine[number] = jnp.concatenate(rows, axis=0)

        def copy(d):
            return pltpu.make_async_remote_copy(
                src_ref=mine.at[number],
                dst_ref=red.at[number, me],
                send_sem=red_send.at[number, d],
                recv_sem=red_recv.at[number, d],
                device_id={"blk": (me + d) % (SIDE * SIDE)},
                device_id_type=MESH,
            )

        def begin(d, _):
            copy(d).start()
            return 0

        lax.fori_loop(1, SIDE * SIDE, begin, 0)
        red[number, me] = mine[number]

        def end(d, _):
            copy(d).wait()
            return 0

        lax.fori_loop(1, SIDE * SIDE, end, 0)
        total = jnp.sum(red[number], axis=0)
        total = jnp.broadcast_to(jnp.sum(total, axis=1, keepdims=True), (8, N))
        return [total[i : i + 1] for i in range(len(parts))]

    zero8 = jnp.zeros((8, N), F32)

    def first_sums(s, sums):
        ss, sh, hh = sums
        start = vec[s].astype(F32)
        image = jnp.where(dims_mask(s), work[HX + s], 0.0)
        work[HX + s] = image
        return ss + fold(start * start), sh + fold(start * image), hh + fold(image * image)

    ss, sh, hh = exchange(0, lax.fori_loop(0, SLOTS, first_sums, (zero8,) * 3))
    norm = jnp.sqrt(ss)
    xx = ss / (norm * norm)
    a = sh / (norm * norm)
    hxhx = hh / (norm * norm)
    b = jnp.sqrt(jnp.maximum(hxhx - 2.0 * a * a + a * a * xx, 0.0) + EPSILON)

    def first_residual(s, _):
        x = vec[s].astype(F32) / norm
        hx = work[HX + s] / norm
        t = (hx - a * x) / b
        work[X + s] = x
        work[HX + s] = hx
        work[T + s] = t
        vec[s] = t.astype(BF16)
        return 0

    lax.fori_loop(0, SLOTS, first_residual, 0)

    def beside(side, sector):
        return jnp.concatenate([cat[side, sector, k] for k in range(channels)], axis=1)

    def hamiltonian(i, _):
        slots = [i * UNROLL + u for u in range(UNROLL)]
        inner = []
        for s in slots:
            z = dot(vec[s], beside(1, table[RSEC + s])).astype(BF16)
            inner.append(jnp.concatenate([z[:, k * N : (k + 1) * N] for k in range(channels)], axis=0))
        for s, z in zip(slots, inner):
            work[HT + s] = jnp.where(dims_mask(s), dot(beside(0, table[LSEC + s]), z), 0.0)
        return 0

    lax.fori_loop(0, SLOTS // UNROLL, hamiltonian, 0)

    def second_sums(s, sums):
        x, hx, t, ht = work[X + s], work[HX + s], work[T + s], work[HT + s]
        terms = (x * t, t * t, x * ht, t * hx, t * ht, hx * ht, ht * ht)
        return tuple(old + fold(term) for old, term in zip(sums, terms))

    xt, tt, xht, thx, c, hxht, htht = exchange(
        1, lax.fori_loop(0, SLOTS, second_sums, (zero8,) * 7)
    )

    def ritz(a, b, c):
        value = 0.5 * (a + c) - jnp.sqrt(0.25 * (a - c) * (a - c) + b * b)
        old, new = c - value, -b
        length = jnp.sqrt(old * old + new * new)
        return value, old / length, new / length

    _, p, q = ritz(a, b, c)
    a2 = p * p * a + p * q * (xht + thx) + q * q * c
    xx2 = p * p * xx + 2.0 * p * q * xt + q * q * tt
    hxhx2 = p * p * hxhx + 2.0 * p * q * hxht + q * q * htht
    b2 = jnp.sqrt(jnp.maximum(hxhx2 - 2.0 * a2 * a2 + a2 * a2 * xx2, 0.0) + EPSILON)

    def second_residual(s, _):
        x = p * work[X + s] + q * work[T + s]
        hx = p * work[HX + s] + q * work[HT + s]
        t = (hx - a2 * x) / b2
        work[X + s] = x
        work[T + s] = t
        vec[s] = t.astype(BF16)
        return 0

    lax.fori_loop(0, SLOTS, second_residual, 0)
    lax.fori_loop(0, SLOTS // UNROLL, hamiltonian, 0)

    def third_sums(s, total):
        return total + fold(work[T + s] * work[HT + s])

    (c2,) = exchange(2, [lax.fori_loop(0, SLOTS, third_sums, zero8)])
    value, p2, q2 = ritz(a2, b2, c2)
    energy[...] = jnp.broadcast_to(value, (8, N))
    scale = N * math.sqrt(RUN * SIDE * SIDE)

    def final_vector(s, _):
        w = ((p2 * work[X + s] + q2 * work[T + s]) * scale).astype(BF16)
        vec[s] = w
        vect[s] = w.T
        return 0

    lax.fori_loop(0, SLOTS, final_vector, 0)

    def wave_copy(step):
        to_w = (my_w + step) % SIDE
        return pltpu.make_async_remote_copy(
            src_ref=vec.at[pl.ds(to_w * 8, 8)],
            dst_ref=ret.at[pl.ds(my_w * 8, 8)],
            send_sem=psi_send.at[step + 2],
            recv_sem=psi_recv.at[step + 2],
            device_id={"blk": along(0, step)},
            device_id_type=MESH,
        )

    def grow(kind, group, to):
        order, keep, last, live = (
            (ORD_L, KEEP_L, LAST_L, LIVE_L) if kind == 0 else (ORD_R, KEEP_R, LAST_R, LIVE_R)
        )
        outer, sector_at = (vect, LSEC) if kind == 0 else (vec, RSEC)
        closing = vec if kind == 0 else vect

        def term(i, _):
            spots = [i * 2 + u for u in range(2)]
            for u, spot in enumerate(spots):
                slot = table[order + group * 8 + spot]
                z = dot(outer[slot], beside(kind, table[sector_at + slot])).astype(BF16)
                for k in range(channels):
                    stack[u, k] = z[:, k * N : (k + 1) * N]
            for u, spot in enumerate(spots):
                slot = table[order + group * 8 + spot]
                stay = table[keep + group * 8 + spot] > 0
                right = closing[slot]
                for k in range(channels):
                    before = work[jnp.maximum(spot - 1, 0) * channels + k]
                    work[spot * channels + k] = dot(stack[u, k], right) + jnp.where(stay, before, 0.0)
            return 0

        lax.fori_loop(0, 4, term, 0)

        def close(k, diagonals):
            after = []
            for j in range(SEC):
                spot = table[last + group * SEC + j]
                upper, row = pack(work[spot * channels + k], masks)
                at = pl.multiple_of(to * region + j * deep + k * HALF, 16)
                has = table[live + group * SEC + j] > 0
                outb[kind, pl.ds(at, HALF)] = jnp.where(has, upper, 0.0).astype(BF16)
                after.append(jnp.where(row32 == k, jnp.broadcast_to(row, (32, N)), diagonals[j]))
            return tuple(after)

        diagonals = lax.fori_loop(0, channels, close, (jnp.zeros((32, N), F32),) * SEC)
        for j in range(SEC):
            has = table[live + group * SEC + j] > 0
            at = to * region + j * deep + channels * HALF
            outb[kind, pl.ds(at, 32)] = jnp.where(has, diagonals[j], 0.0).astype(BF16)

    def grow_copy(kind, target, j):
        back = target == 2 or (target == 0 and j >= 2)
        return pltpu.make_async_remote_copy(
            src_ref=outb.at[kind, sector_rows(target, j)],
            dst_ref=gath.at[kind, sector_rows(target, j)],
            send_sem=grow_send.at[kind, target, j],
            recv_sem=grow_recv.at[kind, target, j],
            device_id={"blk": along(1 - kind, SIDE - 1 if back else 1)},
            device_id_type=MESH,
        )

    def my_group(kind, step):
        return ((my_u if kind == 0 else my_w) + step) % SIDE

    for step in (1, 3, 2):
        wave_copy(step).start()
    for kind in range(2):
        grow(kind, my_group(kind, 2), 0)
        for j in (0, 2, 1, 3):
            grow_copy(kind, 0, j).start()
    for kind in range(2):
        grow(kind, my_group(kind, 1), 1)
        for j in (2, 3):
            grow_copy(kind, 1, j).start()
    for kind in range(2):
        grow(kind, my_group(kind, SIDE - 1), 2)
        for j in (0, 1):
            grow_copy(kind, 2, j).start()
    for j in (0, 2, 1, 3):
        target = 1 if j < 2 else 2
        for kind in range(2):
            grow_copy(kind, 0, j).wait_recv()

            def add(i, _):
                there = pl.ds(pl.multiple_of(target * region + j * deep + i * 32, 16), 32)
                here = pl.ds(pl.multiple_of(j * deep + i * 32, 16), 32)
                total = outb[kind, there].astype(F32) + gath[kind, here].astype(F32)
                outb[kind, there] = total.astype(BF16)
                return 0

            lax.fori_loop(0, deep // 32, add, 0)
            grow_copy(kind, target, j).start()
    for kind in range(2):
        grow(kind, my_group(kind, 0), 3)

    for step in (1, 3, 2):
        wave_copy(step).wait_recv()
    for i in range(8):
        ret[my_w * 8 + i] = vec[my_w * 8 + i]

    def take(e, _):
        wave[e] = ret[table[SLOT_OF + e]]
        return 0

    lax.fori_loop(0, RUN, take, 0)

    shrink = 1.0 / math.sqrt(N)

    def store(kind, j):
        out = left_out if kind == 0 else right_out
        return pltpu.make_async_copy(bound.at[kind, :, j], out.at[:, j], store_sem.at[kind, j])

    for j, kind in [(j, kind) for j in (0, 2, 1, 3) for kind in range(2)]:
        mix = left_mix if kind == 0 else right_mix
        for target in (1, 2):
            grow_copy(kind, target, j).wait_recv()

        def total(at, size):
            own, before, after = (
                pl.ds(pl.multiple_of(spot * region + j * deep + at, 16), size) for spot in (3, 1, 2)
            )
            parts = outb[kind, own].astype(F32) + gath[kind, before].astype(F32)
            return (parts + gath[kind, after].astype(F32)) * shrink

        def add_all(k, _):
            work[k, pl.ds(0, HALF)] = total(k * HALF, HALF)
            return 0

        lax.fori_loop(0, channels, add_all, 0)
        work[channels, pl.ds(0, 32)] = total(channels * HALF, 32)

        def blend(v, _):
            factors = [mix[k, v] for k in range(channels)]
            row = factors[0] * work[channels, pl.ds(0, 1)]
            upper = factors[0] * work[0, pl.ds(0, HALF)]
            for k in range(1, channels):
                row = row + factors[k] * work[channels, pl.ds(k, 1)]
                upper = upper + factors[k] * work[k, pl.ds(0, HALF)]
            bound[kind, v, j] = unpack(upper.astype(BF16), row, bits)
            return 0

        lax.fori_loop(0, channels, blend, 0)
        store(kind, j).start()
    for kind in range(2):
        for j in range(SEC):
            store(kind, j).wait()
            for target in range(3):
                grow_copy(kind, target, j).wait_send()
    for step in (1, 3, 2):
        wave_copy(step).wait_send()


def body(
    left_boundary,
    right_boundary,
    psi_start,
    left_local,
    right_group,
    right_local,
    left_dims,
    right_dims,
    left_mix,
    right_mix,
):
    channels = left_boundary.shape[1]
    smem = pl.BlockSpec(memory_space=pltpu.SMEM)
    vmem = pl.BlockSpec(memory_space=pltpu.VMEM)
    hbm = pl.BlockSpec(memory_space=pl.ANY)
    table = pl.pallas_call(
        router,
        out_shape=jax.ShapeDtypeStruct((TABLE,), jnp.int32),
        in_specs=[smem] * 5,
        out_specs=smem,
        scratch_shapes=[pltpu.SMEM((16,), jnp.int32)],
        name="router",
    )(
        left_local,
        right_group[:, :, 0],
        right_local,
        left_dims,
        right_dims,
    )
    dma = pltpu.SemaphoreType.DMA
    env = (channels, SEC, N, N)
    region = max(channels * PACK, SEC * (channels * HALF + 32))
    wave, energy, left_grown, right_grown = pl.pallas_call(
        lambda *refs: kernel(channels, *refs),
        out_shape=(
            jax.ShapeDtypeStruct((RUN, N, N), BF16),
            jax.ShapeDtypeStruct((8, N), F32),
            jax.ShapeDtypeStruct(env, BF16),
            jax.ShapeDtypeStruct(env, BF16),
        ),
        in_specs=[smem, smem, smem, hbm, hbm, vmem],
        out_specs=(vmem, vmem, hbm, hbm),
        scratch_shapes=[
            pltpu.VMEM((2,) + env, BF16),
            pltpu.VMEM((2, SIDE * SEC, channels, N, N), BF16),
            pltpu.VMEM((2, SIDE * region, N), BF16),
            pltpu.VMEM((2, SIDE * region, N), BF16),
            pltpu.VMEM((max(4 * SLOTS, 8 * channels), N, N), F32),
            pltpu.VMEM((SLOTS, N, N), BF16),
            pltpu.VMEM((SLOTS, N, N), BF16),
            pltpu.VMEM((SLOTS, N, N), BF16),
            pltpu.VMEM((2, channels, N, N), BF16),
            pltpu.VMEM((3, SIDE * SIDE, 8, N), F32),
            pltpu.VMEM((3, 8, N), F32),
            dma((2,)),
            dma((2, SEC)),
            dma((6,)),
            dma((6,)),
            dma((2, channels)),
            dma((2, channels)),
            dma((2, 3, channels)),
            dma((2, 3, channels)),
            dma((3, SIDE * SIDE)),
            dma((3, SIDE * SIDE)),
            dma((2, 3, SEC)),
            dma((2, 3, SEC)),
        ],
        compiler_params=pltpu.CompilerParams(
            collective_id=0, has_side_effects=True, vmem_limit_bytes=62 * 2**20
        ),
        name="davidson",
    )(
        table,
        left_mix,
        right_mix,
        left_boundary[0],
        right_boundary[0],
        psi_start[0],
    )
    return wave[None], energy[0, :1], left_grown[None], right_grown[None]


def solution(mesh):
    return jax.shard_map(
        body,
        mesh=mesh,
        in_specs=(
            P("sect", None, "blk", None, None),
            P("sect", None, "blk", None, None),
            P("sect", "blk", None, None),
            P("sect", None),
            P("sect", None, None),
            P("sect", None),
            P("sect", None),
            P("sect", None),
            P(),
            P(),
        ),
        out_specs=(
            P("sect", "blk", None, None),
            P("sect"),
            P("sect", None, "blk", None, None),
            P("sect", None, "blk", None, None),
        ),
        check_vma=False,
    )
```

```python
import math

import jax
import jax.numpy as jnp
from jax import lax
from jax.experimental import pallas as pl
from jax.experimental.pallas import tpu as pltpu
from jax.sharding import PartitionSpec as P

MESH = pl.DeviceIdType.MESH
F32 = jnp.float32
BF16 = jnp.bfloat16
EPSILON = 1e-06

N = 128
HALF = 64
SIDE = 4
SEC = 4
RANKS = 2
SLOTS = SIDE * SIDE * RANKS
RUN = 24
PACK = SEC * HALF + 16
UNROLL = 4
TERMS = 4
AHEAD = 3

SEND, SLOT_OF, LSEC, RSEC, LDIM, RDIM = 0, 32, 64, 96, 128, 160
ORD_R, KEEP_R, LAST_R, LIVE_R = 192, 224, 256, 272
ORD_L, KEEP_L, LAST_L, LIVE_L = 288, 320, 352, 368
SPARE = 384 - LSEC
TABLE = 512


def places(me, swap):
    x, y = me // SIDE, me % SIDE
    return x * (1 - swap) + y * swap, y * (1 - swap) + x * swap


def device_at(u, w, swap):
    return (u * SIDE + w) * (1 - swap) + (w * SIDE + u) * swap


def router(left_local, right_group, right_local, left_dims, right_dims, table, count):
    me = lax.axis_index("blk")
    swap = lax.axis_index("sect") & 1
    my_u, my_w = places(me, swap)
    for i in range(SLOTS):
        table[SEND + i] = 0
        table[LSEC + i] = (i // 8) * SEC
        table[RSEC + i] = (i % 8 // 2) * SEC
        table[LDIM + i] = 0
        table[RDIM + i] = 0

    def zero_counts():
        for i in range(SIDE * SIDE):
            count[i] = 0

    def split(group):
        x, y = group >> 2, group & 3
        return x * (1 - swap) + y * swap, y * (1 - swap) + x * swap

    zero_counts()
    for e in range(RUN):
        group = right_group[0, me * RUN + e]
        rank = jnp.minimum(count[group], RANKS - 1)
        count[group] = rank + 1
        u, w = split(group)
        slot = w * 8 + u * 2 + rank
        table[SLOT_OF + e] = slot
        table[SEND + slot] = e
    for source in range(SIDE):
        run = device_at(my_u, source, swap)
        zero_counts()
        for e in range(RUN):
            at = run * RUN + e
            group = right_group[0, at]
            rank = jnp.minimum(count[group], RANKS - 1)
            count[group] = rank + 1
            u, w = split(group)
            slot = jnp.where(w == my_w, source * 8 + u * 2 + rank, SPARE)
            left, right = left_local[0, at], right_local[0, at]
            table[LSEC + slot] = source * SEC + left
            table[RSEC + slot] = u * SEC + right
            table[LDIM + slot] = left_dims[0, run * SEC + left]
            table[RDIM + slot] = right_dims[0, group * SEC + right]
    for key, order, keep, last, live in (
        (LSEC, ORD_R, KEEP_R, LAST_R, LIVE_R),
        (RSEC, ORD_L, KEEP_L, LAST_L, LIVE_L),
    ):
        zero_counts()
        for s in range(SLOTS):
            sector = table[key + s]
            count[sector] = count[sector] + 1
        for g in range(SIDE):
            begin = jnp.int32(0)
            for j in range(SEC):
                sector = g * SEC + j
                amount = count[sector]
                count[sector] = g * 8 + begin
                table[live + sector] = jnp.minimum(amount, 1)
                begin = begin + amount
                table[last + sector] = jnp.maximum(begin - 1, 0)
        for s in range(SLOTS):
            sector = table[key + s]
            at = count[sector]
            count[sector] = at + 1
            table[order + at] = s
        for g in range(SIDE):
            before = jnp.int32(-1)
            for p in range(g * 8, g * 8 + 8):
                sector = table[key + table[order + p]]
                table[keep + p] = jnp.where(sector == before, 1, 0)
                before = sector


def dot(a, b):
    return jnp.dot(a, b, preferred_element_type=F32)


def triangle_masks():
    row = lax.broadcasted_iota(jnp.int32, (HALF, N), 0)
    col = lax.broadcasted_iota(jnp.int32, (HALF, N), 1)
    left = col < HALF
    below = jnp.logical_and(left, row > col)
    low = jnp.logical_and(col >= HALF, row > col - HALF)
    high = jnp.logical_and(col >= HALF, row < col - HALF)
    diag = row == col - HALF
    return below, left, low, high, diag


def pack(block, masks):
    below, _, _, _, diag = masks
    corner = block[HALF:]
    upper = jnp.where(below, pltpu.roll(corner, HALF, 1), block[:HALF])
    row = jnp.sum(jnp.where(diag, corner, 0.0), axis=0, keepdims=True)
    return upper, row


def unpack(packed, row, masks):
    below, above, left, low, high, diag = masks
    turned = jnp.concatenate([packed, packed], axis=0).T
    rolled = pltpu.roll(packed.astype(F32), HALF, 1).astype(BF16)
    top = packed * above + turned[:HALF] * below
    bottom = (
        turned[HALF:] * left
        + rolled * low
        + turned[:HALF] * high
        + jnp.broadcast_to(row, (HALF, N)).astype(BF16) * diag
    )
    return jnp.concatenate([top, bottom], axis=0)


def kernel(
    channels,
    table,
    left_mix,
    right_mix,
    left_hbm,
    right_hbm,
    psi,
    wave,
    energy,
    left_out,
    right_out,
    bound,
    cat,
    gath,
    outb,
    work,
    vec,
    vect,
    vecr,
    vectr,
    ret,
    stack,
    red,
    mine,
    local_sem,
    store_sem,
    psi_send,
    psi_recv,
    z_send,
    z_recv,
    ring_send,
    ring_recv,
    red_send,
    red_recv,
    grow_send,
    grow_recv,
):
    n_sect = lax.axis_size("sect")
    sect = lax.axis_index("sect")
    me = lax.axis_index("blk")
    swap = sect % 2
    my_u, my_w = places(me, swap)
    up, down = (sect + 1) % n_sect, (sect + n_sect - 1) % n_sect
    deep = channels * HALF + 32
    region = max(channels * PACK, SEC * deep)

    def along(side, step):
        if side == 0:
            return device_at(my_u, (my_w + step) % SIDE, swap)
        return device_at((my_u + step) % SIDE, my_w, swap)

    def rows_of(group, k):
        return pl.ds(pl.multiple_of(group * region + k * PACK, 16), PACK)

    def sector_rows(place, j):
        return pl.ds(pl.multiple_of(place * region + j * deep, 16), deep)

    barrier = pltpu.get_barrier_semaphore()

    def greet(d, _):
        pl.semaphore_signal(
            barrier, inc=1, device_id={"blk": (me + d) % (SIDE * SIDE)}, device_id_type=MESH
        )
        return 0

    lax.fori_loop(1, SIDE * SIDE, greet, 0)
    pl.semaphore_signal(barrier, inc=1, device_id={"sect": up}, device_id_type=MESH)
    pl.semaphore_signal(barrier, inc=1, device_id={"sect": down}, device_id_type=MESH)

    loads = [
        pltpu.make_async_copy(left_hbm, bound.at[0], local_sem.at[0]),
        pltpu.make_async_copy(right_hbm, bound.at[1], local_sem.at[1]),
    ]
    for load in loads:
        load.start()

    def fill(i, _):
        ret[i] = psi[table[SEND + i]].astype(BF16)
        return 0

    lax.fori_loop(0, SLOTS, fill, 0)
    pl.semaphore_wait(barrier, SIDE * SIDE + 1)

    def psi_copy(step):
        to_w = (my_w + step) % SIDE
        return pltpu.make_async_remote_copy(
            src_ref=ret.at[pl.ds(to_w * 8, 8)],
            dst_ref=vec.at[pl.ds(my_w * 8, 8)],
            send_sem=psi_send.at[step - 1],
            recv_sem=psi_recv.at[step - 1],
            device_id={"blk": along(0, step)},
            device_id_type=MESH,
        )

    for step in (1, 3, 2):
        psi_copy(step).start()

    masks = triangle_masks()
    below, left, low, high, diag = masks
    diag_low = lax.broadcasted_iota(jnp.int32, (HALF, N), 0) == lax.broadcasted_iota(jnp.int32, (HALF, N), 1)
    ones = [jnp.where(m, 1.0, 0.0).astype(BF16) for m in (below, left, low, high, diag)]
    bits = (ones[0], jnp.where(below, 0.0, 1.0).astype(BF16), ones[1], ones[2], ones[3], ones[4])
    row32 = lax.broadcasted_iota(jnp.int32, (32, N), 0)
    row16 = lax.broadcasted_iota(jnp.int32, (16, N), 0)
    eye_packed = jnp.where(
        lax.broadcasted_iota(jnp.int32, (HALF, N), 0) == lax.broadcasted_iota(jnp.int32, (HALF, N), 1),
        1.0,
        0.0,
    )
    eye_row = jnp.where(lax.broadcasted_iota(jnp.int32, (1, N), 1) >= HALF, 1.0, 0.0)

    def place(side):
        return my_w if side == 0 else my_u

    def z_copy(side, k):
        return pltpu.make_async_remote_copy(
            src_ref=outb.at[side, rows_of(3, k)],
            dst_ref=gath.at[side, rows_of(place(1 - side), k)],
            send_sem=z_send.at[side, k],
            recv_sem=z_recv.at[side, k],
            device_id={"sect": up if side == 0 else down},
            device_id_type=MESH,
        )

    def pack_bound(k):
        for side in range(2):
            edge = sect == (n_sect - 1 if side == 0 else 0)
            here = k == (0 if side == 0 else channels - 1)
            one = jnp.where(here, 1.0, 0.0)
            rows = jnp.zeros((16, N), F32)
            base = 3 * region + k * PACK
            for j in range(SEC):
                upper, row = pack(bound[side, k, j].astype(F32), masks)
                upper = jnp.where(edge, eye_packed * one, upper)
                row = jnp.where(edge, eye_row * one, row)
                outb[side, pl.ds(pl.multiple_of(base + j * HALF, 16), HALF)] = upper.astype(BF16)
                rows = jnp.where(row16 == j, jnp.broadcast_to(row, (16, N)), rows)
            outb[side, pl.ds(pl.multiple_of(base + SEC * HALF, 16), 16)] = rows.astype(BF16)
            z_copy(side, k).start()

    def ring_copy(side, which, k, back):
        at = place(side)
        if which == 2:
            at = (at + (1 if back else SIDE - 1)) % SIDE
        step = SIDE - 1 if back else 1
        return pltpu.make_async_remote_copy(
            src_ref=gath.at[side, rows_of(at, k)],
            dst_ref=gath.at[side, rows_of(at, k)],
            send_sem=ring_send.at[side, which, k],
            recv_sem=ring_recv.at[side, which, k],
            device_id={"blk": along(side, step)},
            device_id_type=MESH,
        )

    def dims_mask(slot):
        rows = lax.broadcasted_iota(jnp.int32, (N, N), 0) < table[LDIM + slot]
        cols = lax.broadcasted_iota(jnp.int32, (N, N), 1) < table[RDIM + slot]
        return jnp.logical_and(rows, cols)

    X, HX, T, HT = 0, SLOTS, 2 * SLOTS, 3 * SLOTS

    for load in loads:
        load.wait()

    def beside(side, sector, lo=0, hi=channels):
        return jnp.concatenate([cat[side, sector, k] for k in range(lo, hi)], axis=1)

    def product(blocks, slots, lo=0, hi=channels):
        inner = []
        for block, s in zip(blocks, slots):
            z = dot(block, beside(1, table[RSEC + s], lo, hi)).astype(BF16)
            inner.append(jnp.concatenate([z[:, k * N : (k + 1) * N] for k in range(hi - lo)], axis=0))
        return [dot(beside(0, table[LSEC + s], lo, hi), z) for s, z in zip(slots, inner)]

    def gather_step(t, _):
        @pl.when(t < channels)
        def _():
            pack_bound(t)

        @pl.when(jnp.logical_and(t >= AHEAD, t < channels + AHEAD))
        def _():
            k = t - AHEAD
            for side in range(2):
                z_copy(side, k).wait_recv()
                ring_copy(side, 0, k, False).start()
                ring_copy(side, 1, k, True).start()

        @pl.when(jnp.logical_and(t >= 2 * AHEAD, t < channels + 2 * AHEAD))
        def _():
            k = t - 2 * AHEAD
            for side in range(2):
                ring_copy(side, 0, k, False).wait_recv()
                ring_copy(side, 1, k, True).wait_recv()

            @pl.when(k % 2 == 0)
            def _():
                for side in range(2):
                    ring_copy(side, 2, k, False).start()

            @pl.when(k % 2 == 1)
            def _():
                for side in range(2):
                    ring_copy(side, 2, k, True).start()

        @pl.when(t == 3 * AHEAD)
        def _():
            for step in (1, 3, 2):
                psi_copy(step).wait_recv()
            for i in range(8):
                vec[my_w * 8 + i] = ret[my_w * 8 + i]

            def start(i, _):
                vec[i] = jnp.where(dims_mask(i), vec[i].astype(F32), 0.0).astype(BF16)
                return 0

            lax.fori_loop(0, SLOTS, start, 0)

        @pl.when(t >= 3 * AHEAD)
        def _():
            k = t - 3 * AHEAD
            for side in range(2):
                ring_copy(side, 2, k, False).wait_recv()

            def open_group(g, _):
                base = g * region + k * PACK
                for side in range(2):
                    rows = gath[side, pl.ds(pl.multiple_of(base + SEC * HALF, 16), 16)].astype(F32)
                    for j in range(SEC):
                        row = jnp.sum(jnp.where(row16 == j, rows, 0.0), axis=0, keepdims=True)
                        packed = gath[side, pl.ds(pl.multiple_of(base + j * HALF, 16), HALF)]
                        cat[side, g * SEC + j, k] = unpack(packed, row, bits)
                return 0

            lax.fori_loop(0, SIDE, open_group, 0)

            bounds = [4 * n for n in range(max(channels // 4, 1))] + [channels]
            for lo, hi in zip(bounds[:-1], bounds[1:]):

                @pl.when(k == hi - 1)
                def _():
                    def apply(i, _):
                        slots = [i * UNROLL + u for u in range(UNROLL)]
                        images = product([vec[s] for s in slots], slots, lo, hi)
                        for s, image in zip(slots, images):
                            work[HX + s] = image if lo == 0 else work[HX + s] + image
                        return 0

                    lax.fori_loop(0, SLOTS // UNROLL, apply, 0)

        return 0

    lax.fori_loop(0, channels + 3 * AHEAD, gather_step, 0)

    for step in (1, 3, 2):
        psi_copy(step).wait_send()

    def settle(k, _):
        for side in range(2):
            z_copy(side, k).wait_send()
            for which in range(3):
                ring_copy(side, which, k, False).wait_send()
        return 0

    lax.fori_loop(0, channels, settle, 0)

    def fold(block):
        return jnp.sum(block.reshape(N // 8, 8, N), axis=0)

    def exchange(number, parts):
        rows = [jnp.sum(p, axis=0, keepdims=True) for p in parts]
        rows += [jnp.zeros((1, N), F32)] * (8 - len(rows))
        mine[number] = jnp.concatenate(rows, axis=0)

        def copy(d):
            return pltpu.make_async_remote_copy(
                src_ref=mine.at[number],
                dst_ref=red.at[number, me],
                send_sem=red_send.at[number, d],
                recv_sem=red_recv.at[number, d],
                device_id={"blk": (me + d) % (SIDE * SIDE)},
                device_id_type=MESH,
            )

        def begin(d, _):
            copy(d).start()
            return 0

        lax.fori_loop(1, SIDE * SIDE, begin, 0)
        red[number, me] = mine[number]

        def end(d, _):
            copy(d).wait()
            return 0

        lax.fori_loop(1, SIDE * SIDE, end, 0)
        total = jnp.sum(red[number], axis=0)
        total = jnp.broadcast_to(jnp.sum(total, axis=1, keepdims=True), (8, N))
        return [total[i : i + 1] for i in range(len(parts))]

    zero8 = jnp.zeros((8, N), F32)

    def first_sums(s, sums):
        ss, sh, hh = sums
        start = vec[s].astype(F32)
        image = jnp.where(dims_mask(s), work[HX + s], 0.0)
        work[HX + s] = image
        return ss + fold(start * start), sh + fold(start * image), hh + fold(image * image)

    ss, sh, hh = exchange(0, lax.fori_loop(0, SLOTS, first_sums, (zero8,) * 3))
    norm = jnp.sqrt(ss)
    xx = ss / (norm * norm)
    a = sh / (norm * norm)
    hxhx = hh / (norm * norm)
    b = jnp.sqrt(jnp.maximum(hxhx - 2.0 * a * a + a * a * xx, 0.0) + EPSILON)

    per_norm, per_b = 1.0 / norm, 1.0 / b

    def first_correction(i, sums):
        slots = [i * UNROLL + u for u in range(UNROLL)]
        blocks = []
        for s in slots:
            x = vec[s].astype(F32) * per_norm
            hx = work[HX + s] * per_norm
            t = (hx - a * x) * per_b
            work[X + s] = x
            work[HX + s] = hx
            work[T + s] = t
            blocks.append(t.astype(BF16))
        for s, image in zip(slots, product(blocks, slots)):
            ht = jnp.where(dims_mask(s), image, 0.0)
            work[HT + s] = ht
            x, hx, t = work[X + s], work[HX + s], work[T + s]
            terms = (x * t, t * t, x * ht, t * hx, t * ht, hx * ht, ht * ht)
            sums = tuple(old + fold(term) for old, term in zip(sums, terms))
        return sums

    xt, tt, xht, thx, c, hxht, htht = exchange(
        1, lax.fori_loop(0, SLOTS // UNROLL, first_correction, (zero8,) * 7)
    )

    def ritz(a, b, c):
        value = 0.5 * (a + c) - jnp.sqrt(0.25 * (a - c) * (a - c) + b * b)
        old, new = c - value, -b
        length = jnp.sqrt(old * old + new * new)
        return value, old / length, new / length

    _, p, q = ritz(a, b, c)
    a2 = p * p * a + p * q * (xht + thx) + q * q * c
    xx2 = p * p * xx + 2.0 * p * q * xt + q * q * tt
    hxhx2 = p * p * hxhx + 2.0 * p * q * hxht + q * q * htht
    b2 = jnp.sqrt(jnp.maximum(hxhx2 - 2.0 * a2 * a2 + a2 * a2 * xx2, 0.0) + EPSILON)

    per_b2 = 1.0 / b2

    def second_correction(i, total):
        slots = [i * UNROLL + u for u in range(UNROLL)]
        blocks = []
        for s in slots:
            x = p * work[X + s] + q * work[T + s]
            hx = p * work[HX + s] + q * work[HT + s]
            t = (hx - a2 * x) * per_b2
            work[X + s] = x
            work[T + s] = t
            blocks.append(t.astype(BF16))
        for s, image in zip(slots, product(blocks, slots)):
            total = total + fold(work[T + s] * jnp.where(dims_mask(s), image, 0.0))
        return total

    (c2,) = exchange(2, [lax.fori_loop(0, SLOTS // UNROLL, second_correction, zero8)])
    value, p2, q2 = ritz(a2, b2, c2)
    energy[...] = jnp.broadcast_to(value, (8, N))
    scale = N * math.sqrt(RUN * SIDE * SIDE)

    def final_vector(s, _):
        w = ((p2 * work[X + s] + q2 * work[T + s]) * scale).astype(BF16)
        turned = w.T
        vec[s] = w
        vect[s] = turned
        vecr[s] = pltpu.roll(w.astype(F32), HALF, 1).astype(BF16)
        vectr[s] = pltpu.roll(turned.astype(F32), HALF, 1).astype(BF16)
        return 0

    lax.fori_loop(0, SLOTS, final_vector, 0)

    def wave_copy(step):
        to_w = (my_w + step) % SIDE
        return pltpu.make_async_remote_copy(
            src_ref=vec.at[pl.ds(to_w * 8, 8)],
            dst_ref=ret.at[pl.ds(my_w * 8, 8)],
            send_sem=psi_send.at[step + 2],
            recv_sem=psi_recv.at[step + 2],
            device_id={"blk": along(0, step)},
            device_id_type=MESH,
        )

    def grow(kind, group, to):
        order, keep, last, live = (
            (ORD_L, KEEP_L, LAST_L, LIVE_L) if kind == 0 else (ORD_R, KEEP_R, LAST_R, LIVE_R)
        )
        outer, sector_at = (vect, LSEC) if kind == 0 else (vec, RSEC)
        closing, closing_rolled = (vec, vecr) if kind == 0 else (vect, vectr)
        nothing = jnp.zeros((N, N), BF16)

        def term(i, _):
            spots = [i * TERMS + u for u in range(TERMS)]
            slots = [table[order + group * 8 + spot] for spot in spots]
            for u, slot in enumerate(slots):
                z = dot(outer[slot], beside(kind, table[sector_at + slot])).astype(BF16)
                for k in range(channels):
                    part = z[:, k * N : (k + 1) * N]
                    stack[u, pl.ds(k * HALF, HALF), pl.ds(0, N)] = part[:HALF]
                    stack[u, pl.ds(k * HALF, HALF), pl.ds(N, N)] = part[HALF:]
            for u, (spot, slot) in enumerate(zip(spots, slots)):
                square = jnp.concatenate(
                    [
                        jnp.concatenate([closing[slot], nothing], axis=1),
                        jnp.concatenate([nothing, closing_rolled[slot]], axis=1),
                    ],
                    axis=0,
                )
                both = dot(stack[u], square)
                stay = table[keep + group * 8 + spot] > 0
                for k in range(channels):
                    rows = both[k * HALF : (k + 1) * HALF]
                    upper = jnp.where(below, rows[:, N:], rows[:, :N])
                    trace = jnp.where(diag_low, rows[:, N:], 0.0)
                    trace = jnp.sum(trace.reshape(HALF // 8, 8, N), axis=0)
                    before = jnp.maximum(spot - 1, 0) * channels + k
                    now = spot * channels + k
                    work[now, pl.ds(0, HALF)] = upper + jnp.where(stay, work[before, pl.ds(0, HALF)], 0.0)
                    work[now, pl.ds(HALF, 8)] = trace + jnp.where(stay, work[before, pl.ds(HALF, 8)], 0.0)
            return 0

        lax.fori_loop(0, 8 // TERMS, term, 0)

        def close(k, diagonals):
            after = []
            for j in range(SEC):
                spot = table[last + group * SEC + j]
                upper = work[spot * channels + k, pl.ds(0, HALF)]
                row = jnp.sum(work[spot * channels + k, pl.ds(HALF, 8)], axis=0, keepdims=True)
                at = pl.multiple_of(to * region + j * deep + k * HALF, 16)
                has = table[live + group * SEC + j] > 0
                outb[kind, pl.ds(at, HALF)] = jnp.where(has, upper, 0.0).astype(BF16)
                after.append(jnp.where(row32 == k, jnp.broadcast_to(row, (32, N)), diagonals[j]))
            return tuple(after)

        diagonals = lax.fori_loop(0, channels, close, (jnp.zeros((32, N), F32),) * SEC)
        for j in range(SEC):
            has = table[live + group * SEC + j] > 0
            at = to * region + j * deep + channels * HALF
            outb[kind, pl.ds(at, 32)] = jnp.where(has, diagonals[j], 0.0).astype(BF16)

    def grow_copy(kind, target, j):
        back = target == 2 or (target == 0 and j >= 2)
        return pltpu.make_async_remote_copy(
            src_ref=outb.at[kind, sector_rows(target, j)],
            dst_ref=gath.at[kind, sector_rows(target, j)],
            send_sem=grow_send.at[kind, target, j],
            recv_sem=grow_recv.at[kind, target, j],
            device_id={"blk": along(1 - kind, SIDE - 1 if back else 1)},
            device_id_type=MESH,
        )

    def my_group(kind, step):
        return ((my_u if kind == 0 else my_w) + step) % SIDE

    for step in (1, 3, 2):
        wave_copy(step).start()
    for kind in range(2):
        grow(kind, my_group(kind, 2), 0)
        for j in (0, 2, 1, 3):
            grow_copy(kind, 0, j).start()
    for kind in range(2):
        grow(kind, my_group(kind, 1), 1)
        for j in (2, 3):
            grow_copy(kind, 1, j).start()
    for kind in range(2):
        grow(kind, my_group(kind, SIDE - 1), 2)
        for j in (0, 1):
            grow_copy(kind, 2, j).start()
    for j in (0, 2, 1, 3):
        target = 1 if j < 2 else 2
        for kind in range(2):
            grow_copy(kind, 0, j).wait_recv()

            def add(i, _):
                there = pl.ds(pl.multiple_of(target * region + j * deep + i * 32, 16), 32)
                here = pl.ds(pl.multiple_of(j * deep + i * 32, 16), 32)
                total = outb[kind, there].astype(F32) + gath[kind, here].astype(F32)
                outb[kind, there] = total.astype(BF16)
                return 0

            lax.fori_loop(0, deep // 32, add, 0)
            grow_copy(kind, target, j).start()
    for kind in range(2):
        grow(kind, my_group(kind, 0), 3)

    for step in (1, 3, 2):
        wave_copy(step).wait_recv()
    for i in range(8):
        ret[my_w * 8 + i] = vec[my_w * 8 + i]

    def take(e, _):
        wave[e] = ret[table[SLOT_OF + e]]
        return 0

    lax.fori_loop(0, RUN, take, 0)

    shrink = 1.0 / math.sqrt(N)

    def store(kind, j):
        out = left_out if kind == 0 else right_out
        return pltpu.make_async_copy(bound.at[kind, :, j], out.at[:, j], store_sem.at[kind, j])

    for j, kind in [(j, kind) for j in (0, 2, 1, 3) for kind in range(2)]:
        mix = left_mix if kind == 0 else right_mix
        for target in (1, 2):
            grow_copy(kind, target, j).wait_recv()

        def total(at, size):
            own, before, after = (
                pl.ds(pl.multiple_of(spot * region + j * deep + at, 16), size) for spot in (3, 1, 2)
            )
            parts = outb[kind, own].astype(F32) + gath[kind, before].astype(F32)
            return (parts + gath[kind, after].astype(F32)) * shrink

        def add_all(k, _):
            work[k, pl.ds(0, HALF)] = total(k * HALF, HALF)
            return 0

        lax.fori_loop(0, channels, add_all, 0)
        work[channels, pl.ds(0, 32)] = pltpu.roll(total(channels * HALF, 32), HALF, 1)

        def blend(v, _):
            factors = [mix[k, v] for k in range(channels)]
            row = factors[0] * work[channels, pl.ds(0, 1)]
            upper = factors[0] * work[0, pl.ds(0, HALF)]
            for k in range(1, channels):
                row = row + factors[k] * work[channels, pl.ds(k, 1)]
                upper = upper + factors[k] * work[k, pl.ds(0, HALF)]
            bound[kind, v, j] = unpack(upper.astype(BF16), row, bits)
            return 0

        lax.fori_loop(0, channels, blend, 0)
        store(kind, j).start()
    for kind in range(2):
        for j in range(SEC):
            store(kind, j).wait()
            for target in range(3):
                grow_copy(kind, target, j).wait_send()
    for step in (1, 3, 2):
        wave_copy(step).wait_send()


def body(
    left_boundary,
    right_boundary,
    psi_start,
    left_local,
    right_group,
    right_local,
    left_dims,
    right_dims,
    left_mix,
    right_mix,
):
    channels = left_boundary.shape[1]
    smem = pl.BlockSpec(memory_space=pltpu.SMEM)
    vmem = pl.BlockSpec(memory_space=pltpu.VMEM)
    hbm = pl.BlockSpec(memory_space=pl.ANY)
    table = pl.pallas_call(
        router,
        out_shape=jax.ShapeDtypeStruct((TABLE,), jnp.int32),
        in_specs=[smem] * 5,
        out_specs=smem,
        scratch_shapes=[pltpu.SMEM((16,), jnp.int32)],
        name="router",
    )(
        left_local,
        right_group[:, :, 0],
        right_local,
        left_dims,
        right_dims,
    )
    dma = pltpu.SemaphoreType.DMA
    env = (channels, SEC, N, N)
    region = max(channels * PACK, SEC * (channels * HALF + 32))
    wave, energy, left_grown, right_grown = pl.pallas_call(
        lambda *refs: kernel(channels, *refs),
        out_shape=(
            jax.ShapeDtypeStruct((RUN, N, N), BF16),
            jax.ShapeDtypeStruct((8, N), F32),
            jax.ShapeDtypeStruct(env, BF16),
            jax.ShapeDtypeStruct(env, BF16),
        ),
        in_specs=[smem, smem, smem, hbm, hbm, vmem],
        out_specs=(vmem, vmem, hbm, hbm),
        scratch_shapes=[
            pltpu.VMEM((2,) + env, BF16),
            pltpu.VMEM((2, SIDE * SEC, channels, N, N), BF16),
            pltpu.VMEM((2, SIDE * region, N), BF16),
            pltpu.VMEM((2, SIDE * region, N), BF16),
            pltpu.VMEM((max(4 * SLOTS, 8 * channels), N, N), F32),
            pltpu.VMEM((SLOTS, N, N), BF16),
            pltpu.VMEM((SLOTS, N, N), BF16),
            pltpu.VMEM((SLOTS, N, N), BF16),
            pltpu.VMEM((SLOTS, N, N), BF16),
            pltpu.VMEM((SLOTS, N, N), BF16),
            pltpu.VMEM((TERMS, channels * HALF, 2 * N), BF16),
            pltpu.VMEM((3, SIDE * SIDE, 8, N), F32),
            pltpu.VMEM((3, 8, N), F32),
            dma((2,)),
            dma((2, SEC)),
            dma((6,)),
            dma((6,)),
            dma((2, channels)),
            dma((2, channels)),
            dma((2, 3, channels)),
            dma((2, 3, channels)),
            dma((3, SIDE * SIDE)),
            dma((3, SIDE * SIDE)),
            dma((2, 3, SEC)),
            dma((2, 3, SEC)),
        ],
        compiler_params=pltpu.CompilerParams(
            collective_id=0, has_side_effects=True, vmem_limit_bytes=62 * 2**20
        ),
        name="davidson",
    )(
        table,
        left_mix,
        right_mix,
        left_boundary[0],
        right_boundary[0],
        psi_start[0],
    )
    return wave[None], energy[0, :1], left_grown[None], right_grown[None]


def solution(mesh):
    return jax.shard_map(
        body,
        mesh=mesh,
        in_specs=(
            P("sect", None, "blk", None, None),
            P("sect", None, "blk", None, None),
            P("sect", "blk", None, None),
            P("sect", None),
            P("sect", None, None),
            P("sect", None),
            P("sect", None),
            P("sect", None),
            P(),
            P(),
        ),
        out_specs=(
            P("sect", "blk", None, None),
            P("sect"),
            P("sect", None, "blk", None, None),
            P("sect", None, "blk", None, None),
        ),
        check_vma=False,
    )
```

```python
import math

import jax
import jax.numpy as jnp
from jax import lax
from jax.experimental import pallas as pl
from jax.experimental.pallas import tpu as pltpu
from jax.sharding import PartitionSpec as P

MESH = pl.DeviceIdType.MESH
F32 = jnp.float32
BF16 = jnp.bfloat16
EPSILON = 1e-06

N = 128
HALF = 64
SIDE = 4
SEC = 4
RANKS = 2
SLOTS = SIDE * SIDE * RANKS
RUN = 24
PACK = SEC * HALF + 16
UNROLL = 4
TERMS = 4
RING, HAND, OPEN = 3, 7, 10

SEND, SLOT_OF, LSEC, RSEC, LDIM, RDIM = 0, 32, 64, 96, 128, 160
ORD_R, KEEP_R, LAST_R, LIVE_R = 192, 224, 256, 272
ORD_L, KEEP_L, LAST_L, LIVE_L = 288, 320, 352, 368
SPARE = 384 - LSEC
TABLE = 512


def places(me, swap):
    x, y = me // SIDE, me % SIDE
    return x * (1 - swap) + y * swap, y * (1 - swap) + x * swap


def device_at(u, w, swap):
    return (u * SIDE + w) * (1 - swap) + (w * SIDE + u) * swap


def router(left_local, right_group, right_local, left_dims, right_dims, table, count):
    me = lax.axis_index("blk")
    swap = lax.axis_index("sect") & 1
    my_u, my_w = places(me, swap)
    for i in range(SLOTS):
        table[SEND + i] = 0
        table[LSEC + i] = (i // 8) * SEC
        table[RSEC + i] = (i % 8 // 2) * SEC
        table[LDIM + i] = 0
        table[RDIM + i] = 0

    def zero_counts():
        for i in range(SIDE * SIDE):
            count[i] = 0

    def split(group):
        x, y = group >> 2, group & 3
        return x * (1 - swap) + y * swap, y * (1 - swap) + x * swap

    zero_counts()
    for e in range(RUN):
        group = right_group[0, me * RUN + e]
        rank = jnp.minimum(count[group], RANKS - 1)
        count[group] = rank + 1
        u, w = split(group)
        slot = w * 8 + u * 2 + rank
        table[SLOT_OF + e] = slot
        table[SEND + slot] = e
    for source in range(SIDE):
        run = device_at(my_u, source, swap)
        zero_counts()
        for e in range(RUN):
            at = run * RUN + e
            group = right_group[0, at]
            rank = jnp.minimum(count[group], RANKS - 1)
            count[group] = rank + 1
            u, w = split(group)
            slot = jnp.where(w == my_w, source * 8 + u * 2 + rank, SPARE)
            left, right = left_local[0, at], right_local[0, at]
            table[LSEC + slot] = source * SEC + left
            table[RSEC + slot] = u * SEC + right
            table[LDIM + slot] = left_dims[0, run * SEC + left]
            table[RDIM + slot] = right_dims[0, group * SEC + right]
    for key, order, keep, last, live in (
        (LSEC, ORD_R, KEEP_R, LAST_R, LIVE_R),
        (RSEC, ORD_L, KEEP_L, LAST_L, LIVE_L),
    ):
        zero_counts()
        for s in range(SLOTS):
            sector = table[key + s]
            count[sector] = count[sector] + 1
        for g in range(SIDE):
            begin = jnp.int32(0)
            for j in range(SEC):
                sector = g * SEC + j
                amount = count[sector]
                count[sector] = g * 8 + begin
                table[live + sector] = jnp.minimum(amount, 1)
                begin = begin + amount
                table[last + sector] = jnp.maximum(begin - 1, 0)
        for s in range(SLOTS):
            sector = table[key + s]
            at = count[sector]
            count[sector] = at + 1
            table[order + at] = s
        for g in range(SIDE):
            before = jnp.int32(-1)
            for p in range(g * 8, g * 8 + 8):
                sector = table[key + table[order + p]]
                table[keep + p] = jnp.where(sector == before, 1, 0)
                before = sector


def dot(a, b):
    return jnp.dot(a, b, preferred_element_type=F32)


def triangle_masks():
    row = lax.broadcasted_iota(jnp.int32, (HALF, N), 0)
    col = lax.broadcasted_iota(jnp.int32, (HALF, N), 1)
    left = col < HALF
    below = jnp.logical_and(left, row > col)
    low = jnp.logical_and(col >= HALF, row > col - HALF)
    high = jnp.logical_and(col >= HALF, row < col - HALF)
    diag = row == col - HALF
    return below, left, low, high, diag


def pack(block, masks):
    below, _, _, _, diag = masks
    corner = block[HALF:]
    upper = jnp.where(below, pltpu.roll(corner, HALF, 1), block[:HALF])
    row = jnp.sum(jnp.where(diag, corner, 0.0), axis=0, keepdims=True)
    return upper, row


def unpack(packed, row, masks):
    below, above, left, low, high, diag = masks
    turned = jnp.concatenate([packed, packed], axis=0).T
    rolled = pltpu.roll(packed.astype(F32), HALF, 1).astype(BF16)
    top = packed * above + turned[:HALF] * below
    bottom = (
        turned[HALF:] * left
        + rolled * low
        + turned[:HALF] * high
        + jnp.broadcast_to(row, (HALF, N)).astype(BF16) * diag
    )
    return jnp.concatenate([top, bottom], axis=0)


def kernel(
    channels,
    table,
    left_mix,
    right_mix,
    left_hbm,
    right_hbm,
    psi,
    wave,
    energy,
    left_out,
    right_out,
    bound,
    cat,
    gath,
    outb,
    work,
    vec,
    vect,
    vecr,
    vectr,
    ret,
    stack,
    spread,
    red,
    mine,
    local_sem,
    store_sem,
    psi_send,
    psi_recv,
    z_send,
    z_recv,
    ring_send,
    ring_recv,
    red_send,
    red_recv,
    grow_send,
    grow_recv,
):
    n_sect = lax.axis_size("sect")
    sect = lax.axis_index("sect")
    me = lax.axis_index("blk")
    swap = sect % 2
    my_u, my_w = places(me, swap)
    up, down = (sect + 1) % n_sect, (sect + n_sect - 1) % n_sect
    deep = channels * HALF + 32
    region = max(channels * PACK, SEC * deep)

    def along(side, step):
        if side == 0:
            return device_at(my_u, (my_w + step) % SIDE, swap)
        return device_at((my_u + step) % SIDE, my_w, swap)

    def rows_of(group, k):
        return pl.ds(pl.multiple_of(group * region + k * PACK, 16), PACK)

    def sector_rows(place, j):
        return pl.ds(pl.multiple_of(place * region + j * deep, 16), deep)

    barrier = pltpu.get_barrier_semaphore()

    def greet(d, _):
        pl.semaphore_signal(
            barrier, inc=1, device_id={"blk": (me + d) % (SIDE * SIDE)}, device_id_type=MESH
        )
        return 0

    lax.fori_loop(1, SIDE * SIDE, greet, 0)
    pl.semaphore_signal(barrier, inc=1, device_id={"sect": up}, device_id_type=MESH)
    pl.semaphore_signal(barrier, inc=1, device_id={"sect": down}, device_id_type=MESH)

    loads = [
        pltpu.make_async_copy(left_hbm, bound.at[0], local_sem.at[0]),
        pltpu.make_async_copy(right_hbm, bound.at[1], local_sem.at[1]),
    ]
    for load in loads:
        load.start()

    def fill(i, _):
        ret[i] = psi[table[SEND + i]].astype(BF16)
        return 0

    lax.fori_loop(0, SLOTS, fill, 0)
    pl.semaphore_wait(barrier, SIDE * SIDE + 1)

    def psi_copy(step):
        to_w = (my_w + step) % SIDE
        return pltpu.make_async_remote_copy(
            src_ref=ret.at[pl.ds(to_w * 8, 8)],
            dst_ref=vec.at[pl.ds(my_w * 8, 8)],
            send_sem=psi_send.at[step - 1],
            recv_sem=psi_recv.at[step - 1],
            device_id={"blk": along(0, step)},
            device_id_type=MESH,
        )

    for step in (1, 3, 2):
        psi_copy(step).start()

    masks = triangle_masks()
    below, left, low, high, diag = masks
    diag_low = lax.broadcasted_iota(jnp.int32, (HALF, N), 0) == lax.broadcasted_iota(jnp.int32, (HALF, N), 1)
    ones = [jnp.where(m, 1.0, 0.0).astype(BF16) for m in (below, left, low, high, diag)]
    bits = (ones[0], jnp.where(below, 0.0, 1.0).astype(BF16), ones[1], ones[2], ones[3], ones[4])
    row32 = lax.broadcasted_iota(jnp.int32, (32, N), 0)
    row16 = lax.broadcasted_iota(jnp.int32, (16, N), 0)
    eye_packed = jnp.where(
        lax.broadcasted_iota(jnp.int32, (HALF, N), 0) == lax.broadcasted_iota(jnp.int32, (HALF, N), 1),
        1.0,
        0.0,
    )
    eye_row = jnp.where(lax.broadcasted_iota(jnp.int32, (1, N), 1) >= HALF, 1.0, 0.0)

    lane = lax.broadcasted_iota(jnp.int32, (8, 2 * N), 1) - lax.broadcasted_iota(jnp.int32, (8, 2 * N), 0)
    spread[...] = jnp.zeros_like(spread)

    def spread_mix(v, _):
        for kind, mix in enumerate((left_mix, right_mix)):
            rows = jnp.zeros((8, 2 * N), F32)
            for k in range(channels):
                rows = jnp.where(lane == 8 * k, mix[k, v], rows)
            spread[kind, pl.ds(pl.multiple_of(v * 8, 8), 8)] = rows
        return 0

    lax.fori_loop(0, channels, spread_mix, 0)

    def place(side):
        return my_w if side == 0 else my_u

    def z_copy(side, k):
        return pltpu.make_async_remote_copy(
            src_ref=outb.at[side, rows_of(3, k)],
            dst_ref=gath.at[side, rows_of(place(1 - side), k)],
            send_sem=z_send.at[side, k],
            recv_sem=z_recv.at[side, k],
            device_id={"sect": up if side == 0 else down},
            device_id_type=MESH,
        )

    def pack_bound(k):
        for side in range(2):
            edge = sect == (n_sect - 1 if side == 0 else 0)
            here = k == (0 if side == 0 else channels - 1)
            one = jnp.where(here, 1.0, 0.0)
            rows = jnp.zeros((16, N), F32)
            base = 3 * region + k * PACK
            for j in range(SEC):
                upper, row = pack(bound[side, k, j].astype(F32), masks)
                upper = jnp.where(edge, eye_packed * one, upper)
                row = jnp.where(edge, eye_row * one, row)
                outb[side, pl.ds(pl.multiple_of(base + j * HALF, 16), HALF)] = upper.astype(BF16)
                rows = jnp.where(row16 == j, jnp.broadcast_to(row, (16, N)), rows)
            outb[side, pl.ds(pl.multiple_of(base + SEC * HALF, 16), 16)] = rows.astype(BF16)
            z_copy(side, k).start()

    def ring_copy(side, which, k, back):
        at = place(side)
        if which == 2:
            at = (at + (1 if back else SIDE - 1)) % SIDE
        step = SIDE - 1 if back else 1
        return pltpu.make_async_remote_copy(
            src_ref=gath.at[side, rows_of(at, k)],
            dst_ref=gath.at[side, rows_of(at, k)],
            send_sem=ring_send.at[side, which, k],
            recv_sem=ring_recv.at[side, which, k],
            device_id={"blk": along(side, step)},
            device_id_type=MESH,
        )

    def dims_mask(slot):
        rows = lax.broadcasted_iota(jnp.int32, (N, N), 0) < table[LDIM + slot]
        cols = lax.broadcasted_iota(jnp.int32, (N, N), 1) < table[RDIM + slot]
        return jnp.logical_and(rows, cols)

    X, HX, T, HT = 0, SLOTS, 2 * SLOTS, 3 * SLOTS

    for load in loads:
        load.wait()

    def beside(side, sector, lo=0, hi=channels):
        return jnp.concatenate([cat[side, sector, k] for k in range(lo, hi)], axis=1)

    def product(blocks, slots, lo=0, hi=channels):
        inner = []
        for block, s in zip(blocks, slots):
            z = dot(block, beside(1, table[RSEC + s], lo, hi)).astype(BF16)
            inner.append(jnp.concatenate([z[:, k * N : (k + 1) * N] for k in range(hi - lo)], axis=0))
        return [dot(beside(0, table[LSEC + s], lo, hi), z) for s, z in zip(slots, inner)]

    def gather_step(t, _):
        @pl.when(t < channels)
        def _():
            pack_bound(t)

        @pl.when(jnp.logical_and(t >= RING, t < channels + RING))
        def _():
            k = t - RING
            for side in range(2):
                z_copy(side, k).wait_recv()
                ring_copy(side, 0, k, False).start()
                ring_copy(side, 1, k, True).start()

        @pl.when(jnp.logical_and(t >= HAND, t < channels + HAND))
        def _():
            k = t - HAND
            for side in range(2):
                ring_copy(side, 0, k, False).wait_recv()
                ring_copy(side, 1, k, True).wait_recv()

            @pl.when(k % 2 == 0)
            def _():
                for side in range(2):
                    ring_copy(side, 2, k, False).start()

            @pl.when(k % 2 == 1)
            def _():
                for side in range(2):
                    ring_copy(side, 2, k, True).start()

        @pl.when(t == OPEN)
        def _():
            for step in (1, 3, 2):
                psi_copy(step).wait_recv()
            for i in range(8):
                vec[my_w * 8 + i] = ret[my_w * 8 + i]

            def start(i, _):
                vec[i] = jnp.where(dims_mask(i), vec[i].astype(F32), 0.0).astype(BF16)
                return 0

            lax.fori_loop(0, SLOTS, start, 0)

        @pl.when(t >= OPEN)
        def _():
            k = t - OPEN
            for side in range(2):
                ring_copy(side, 2, k, False).wait_recv()

            def open_group(g, _):
                base = g * region + k * PACK
                for side in range(2):
                    rows = gath[side, pl.ds(pl.multiple_of(base + SEC * HALF, 16), 16)].astype(F32)
                    for j in range(SEC):
                        row = jnp.sum(jnp.where(row16 == j, rows, 0.0), axis=0, keepdims=True)
                        packed = gath[side, pl.ds(pl.multiple_of(base + j * HALF, 16), HALF)]
                        cat[side, g * SEC + j, k] = unpack(packed, row, bits)
                return 0

            lax.fori_loop(0, SIDE, open_group, 0)

            bounds = list(range(0, channels, 5)) + [channels]
            for lo, hi in zip(bounds[:-1], bounds[1:]):

                @pl.when(k == hi - 1)
                def _():
                    def apply(i, _):
                        slots = [i * UNROLL + u for u in range(UNROLL)]
                        images = product([vec[s] for s in slots], slots, lo, hi)
                        for s, image in zip(slots, images):
                            work[HX + s] = image if lo == 0 else work[HX + s] + image
                        return 0

                    lax.fori_loop(0, SLOTS // UNROLL, apply, 0)

        return 0

    lax.fori_loop(0, channels + OPEN, gather_step, 0)

    for step in (1, 3, 2):
        psi_copy(step).wait_send()

    def settle(k, _):
        for side in range(2):
            z_copy(side, k).wait_send()
            for which in range(3):
                ring_copy(side, which, k, False).wait_send()
        return 0

    lax.fori_loop(0, channels, settle, 0)

    def fold(block):
        return jnp.sum(block.reshape(N // 8, 8, N), axis=0)

    def exchange(number, parts):
        rows = [jnp.sum(p, axis=0, keepdims=True) for p in parts]
        rows += [jnp.zeros((1, N), F32)] * (8 - len(rows))
        mine[number] = jnp.concatenate(rows, axis=0)

        def copy(d):
            return pltpu.make_async_remote_copy(
                src_ref=mine.at[number],
                dst_ref=red.at[number, me],
                send_sem=red_send.at[number, d],
                recv_sem=red_recv.at[number, d],
                device_id={"blk": (me + d) % (SIDE * SIDE)},
                device_id_type=MESH,
            )

        def begin(d, _):
            copy(d).start()
            return 0

        lax.fori_loop(1, SIDE * SIDE, begin, 0)
        red[number, me] = mine[number]

        def end(d, _):
            copy(d).wait()
            return 0

        lax.fori_loop(1, SIDE * SIDE, end, 0)
        total = jnp.sum(red[number], axis=0)
        total = jnp.broadcast_to(jnp.sum(total, axis=1, keepdims=True), (8, N))
        return [total[i : i + 1] for i in range(len(parts))]

    zero8 = jnp.zeros((8, N), F32)

    def first_sums(s, sums):
        ss, sh, hh = sums
        start = vec[s].astype(F32)
        image = jnp.where(dims_mask(s), work[HX + s], 0.0)
        work[HX + s] = image
        return ss + fold(start * start), sh + fold(start * image), hh + fold(image * image)

    ss, sh, hh = exchange(0, lax.fori_loop(0, SLOTS, first_sums, (zero8,) * 3))
    norm = jnp.sqrt(ss)
    xx = ss / (norm * norm)
    a = sh / (norm * norm)
    hxhx = hh / (norm * norm)
    b = jnp.sqrt(jnp.maximum(hxhx - 2.0 * a * a + a * a * xx, 0.0) + EPSILON)

    per_norm, per_b = 1.0 / norm, 1.0 / b

    def first_correction(i, sums):
        slots = [i * UNROLL + u for u in range(UNROLL)]
        blocks = []
        for s in slots:
            x = vec[s].astype(F32) * per_norm
            hx = work[HX + s] * per_norm
            t = (hx - a * x) * per_b
            work[X + s] = x
            work[HX + s] = hx
            work[T + s] = t
            blocks.append(t.astype(BF16))
        for s, image in zip(slots, product(blocks, slots)):
            ht = jnp.where(dims_mask(s), image, 0.0)
            work[HT + s] = ht
            x, hx, t = work[X + s], work[HX + s], work[T + s]
            terms = (x * t, t * t, x * ht, t * hx, t * ht, hx * ht, ht * ht)
            sums = tuple(old + fold(term) for old, term in zip(sums, terms))
        return sums

    xt, tt, xht, thx, c, hxht, htht = exchange(
        1, lax.fori_loop(0, SLOTS // UNROLL, first_correction, (zero8,) * 7)
    )

    def ritz(a, b, c):
        value = 0.5 * (a + c) - jnp.sqrt(0.25 * (a - c) * (a - c) + b * b)
        old, new = c - value, -b
        length = jnp.sqrt(old * old + new * new)
        return value, old / length, new / length

    _, p, q = ritz(a, b, c)
    a2 = p * p * a + p * q * (xht + thx) + q * q * c
    xx2 = p * p * xx + 2.0 * p * q * xt + q * q * tt
    hxhx2 = p * p * hxhx + 2.0 * p * q * hxht + q * q * htht
    b2 = jnp.sqrt(jnp.maximum(hxhx2 - 2.0 * a2 * a2 + a2 * a2 * xx2, 0.0) + EPSILON)

    per_b2 = 1.0 / b2

    def second_correction(i, total):
        slots = [i * UNROLL + u for u in range(UNROLL)]
        blocks = []
        for s in slots:
            x = p * work[X + s] + q * work[T + s]
            hx = p * work[HX + s] + q * work[HT + s]
            t = (hx - a2 * x) * per_b2
            work[X + s] = x
            work[T + s] = t
            blocks.append(t.astype(BF16))
        for s, image in zip(slots, product(blocks, slots)):
            total = total + fold(work[T + s] * jnp.where(dims_mask(s), image, 0.0))
        return total

    (c2,) = exchange(2, [lax.fori_loop(0, SLOTS // UNROLL, second_correction, zero8)])
    value, p2, q2 = ritz(a2, b2, c2)
    energy[...] = jnp.broadcast_to(value, (8, N))
    scale = N * math.sqrt(RUN * SIDE * SIDE)

    def final_vector(s, _):
        w = ((p2 * work[X + s] + q2 * work[T + s]) * scale).astype(BF16)
        turned = w.T
        vec[s] = w
        vect[s] = turned
        vecr[s] = pltpu.roll(w.astype(F32), HALF, 1).astype(BF16)
        vectr[s] = pltpu.roll(turned.astype(F32), HALF, 1).astype(BF16)
        return 0

    lax.fori_loop(0, SLOTS, final_vector, 0)

    def wave_copy(step):
        to_w = (my_w + step) % SIDE
        return pltpu.make_async_remote_copy(
            src_ref=vec.at[pl.ds(to_w * 8, 8)],
            dst_ref=ret.at[pl.ds(my_w * 8, 8)],
            send_sem=psi_send.at[step + 2],
            recv_sem=psi_recv.at[step + 2],
            device_id={"blk": along(0, step)},
            device_id_type=MESH,
        )

    def grow(kind, group, to):
        order, keep, last, live = (
            (ORD_L, KEEP_L, LAST_L, LIVE_L) if kind == 0 else (ORD_R, KEEP_R, LAST_R, LIVE_R)
        )
        outer, sector_at = (vect, LSEC) if kind == 0 else (vec, RSEC)
        closing, closing_rolled = (vec, vecr) if kind == 0 else (vect, vectr)
        nothing = jnp.zeros((N, N), BF16)

        def term(i, _):
            spots = [i * TERMS + u for u in range(TERMS)]
            slots = [table[order + group * 8 + spot] for spot in spots]
            for u, slot in enumerate(slots):
                z = dot(outer[slot], beside(kind, table[sector_at + slot])).astype(BF16)
                for k in range(channels):
                    part = z[:, k * N : (k + 1) * N]
                    stack[u, pl.ds(k * HALF, HALF), pl.ds(0, N)] = part[:HALF]
                    stack[u, pl.ds(k * HALF, HALF), pl.ds(N, N)] = part[HALF:]
            for u, (spot, slot) in enumerate(zip(spots, slots)):
                square = jnp.concatenate(
                    [
                        jnp.concatenate([closing[slot], nothing], axis=1),
                        jnp.concatenate([nothing, closing_rolled[slot]], axis=1),
                    ],
                    axis=0,
                )
                both = dot(stack[u], square)
                stay = table[keep + group * 8 + spot] > 0
                for k in range(channels):
                    rows = both[k * HALF : (k + 1) * HALF]
                    upper = jnp.where(below, rows[:, N:], rows[:, :N])
                    trace = jnp.where(diag_low, rows[:, N:], 0.0)
                    trace = jnp.sum(trace.reshape(HALF // 8, 8, N), axis=0)
                    before = jnp.maximum(spot - 1, 0) * channels + k
                    now = spot * channels + k
                    work[now, pl.ds(0, HALF)] = upper + jnp.where(stay, work[before, pl.ds(0, HALF)], 0.0)
                    work[now, pl.ds(HALF, 8)] = trace + jnp.where(stay, work[before, pl.ds(HALF, 8)], 0.0)
            return 0

        lax.fori_loop(0, 8 // TERMS, term, 0)

        def close(k, diagonals):
            after = []
            for j in range(SEC):
                spot = table[last + group * SEC + j]
                upper = work[spot * channels + k, pl.ds(0, HALF)]
                row = jnp.sum(work[spot * channels + k, pl.ds(HALF, 8)], axis=0, keepdims=True)
                at = pl.multiple_of(to * region + j * deep + k * HALF, 16)
                has = table[live + group * SEC + j] > 0
                outb[kind, pl.ds(at, HALF)] = jnp.where(has, upper, 0.0).astype(BF16)
                after.append(jnp.where(row32 == k, jnp.broadcast_to(row, (32, N)), diagonals[j]))
            return tuple(after)

        diagonals = lax.fori_loop(0, channels, close, (jnp.zeros((32, N), F32),) * SEC)
        for j in range(SEC):
            has = table[live + group * SEC + j] > 0
            at = to * region + j * deep + channels * HALF
            outb[kind, pl.ds(at, 32)] = jnp.where(has, diagonals[j], 0.0).astype(BF16)

    def grow_copy(kind, target, j):
        back = target == 2 or (target == 0 and j >= 2)
        return pltpu.make_async_remote_copy(
            src_ref=outb.at[kind, sector_rows(target, j)],
            dst_ref=gath.at[kind, sector_rows(target, j)],
            send_sem=grow_send.at[kind, target, j],
            recv_sem=grow_recv.at[kind, target, j],
            device_id={"blk": along(1 - kind, SIDE - 1 if back else 1)},
            device_id_type=MESH,
        )

    def my_group(kind, step):
        return ((my_u if kind == 0 else my_w) + step) % SIDE

    for step in (1, 3, 2):
        wave_copy(step).start()
    for kind in range(2):
        grow(kind, my_group(kind, 2), 0)
        for j in (0, 2, 1, 3):
            grow_copy(kind, 0, j).start()
    for kind in range(2):
        grow(kind, my_group(kind, 1), 1)
        for j in (2, 3):
            grow_copy(kind, 1, j).start()
    for kind in range(2):
        grow(kind, my_group(kind, SIDE - 1), 2)
        for j in (0, 1):
            grow_copy(kind, 2, j).start()
    for j in (0, 2, 1, 3):
        target = 1 if j < 2 else 2
        for kind in range(2):
            grow_copy(kind, 0, j).wait_recv()

            def add(i, _):
                there = pl.ds(pl.multiple_of(target * region + j * deep + i * 32, 16), 32)
                here = pl.ds(pl.multiple_of(j * deep + i * 32, 16), 32)
                total = outb[kind, there].astype(F32) + gath[kind, here].astype(F32)
                outb[kind, there] = total.astype(BF16)
                return 0

            lax.fori_loop(0, deep // 32, add, 0)
            grow_copy(kind, target, j).start()
    for kind in range(2):
        grow(kind, my_group(kind, 0), 3)

    for step in (1, 3, 2):
        wave_copy(step).wait_recv()
    for i in range(8):
        ret[my_w * 8 + i] = vec[my_w * 8 + i]

    def take(e, _):
        wave[e] = ret[table[SLOT_OF + e]]
        return 0

    lax.fori_loop(0, RUN, take, 0)

    shrink = 1.0 / math.sqrt(N)

    def store(kind, j):
        out = left_out if kind == 0 else right_out
        return pltpu.make_async_copy(bound.at[kind, :, j], out.at[:, j], store_sem.at[kind, j])

    for j, kind in [(j, kind) for j in (0, 2, 1, 3) for kind in range(2)]:
        for target in (1, 2):
            grow_copy(kind, target, j).wait_recv()

        def total(at, size):
            own, before, after = (
                pl.ds(pl.multiple_of(spot * region + j * deep + at, 16), size) for spot in (3, 1, 2)
            )
            parts = outb[kind, own].astype(F32) + gath[kind, before].astype(F32)
            return (parts + gath[kind, after].astype(F32)) * shrink

        diagonals = pltpu.roll(total(channels * HALF, 32), HALF, 1)
        for k in range(channels):
            work[k, pl.ds(0, HALF)] = total(k * HALF, HALF)
            work[k, pl.ds(HALF, 8)] = jnp.broadcast_to(diagonals[k : k + 1], (8, N))

        factor = spread[kind]
        high_part = factor.astype(BF16)
        low_part = (factor - high_part.astype(F32)).astype(BF16)

        def eight(r):
            rows = [work[k, pl.ds(r * 8, 8)] for k in range(channels)]
            rows.append(jnp.zeros((2 * N - 8 * channels, N), F32))
            return jnp.concatenate(rows, axis=0).astype(BF16)

        for start in range(0, 9, 2):
            count = min(2, 9 - start)
            rows = jnp.concatenate([eight(start + n) for n in range(count)], axis=1)
            mixed = dot(high_part, rows) + dot(low_part, rows)
            for v in range(channels):
                for n in range(count):
                    work[32 + v, pl.ds((start + n) * 8, 8)] = mixed[v * 8 : v * 8 + 8, n * N : n * N + N]

        def grown(v):
            upper = work[32 + v, pl.ds(0, HALF)].astype(BF16)
            bound[kind, v, j] = unpack(upper, work[32 + v, pl.ds(HALF, 1)], bits)

        def several(i, _):
            for n in range(4):
                grown(i * 4 + n)
            return 0

        lax.fori_loop(0, channels // 4, several, 0)
        for v in range(channels // 4 * 4, channels):
            grown(v)
        store(kind, j).start()
    for kind in range(2):
        for j in range(SEC):
            store(kind, j).wait()
            for target in range(3):
                grow_copy(kind, target, j).wait_send()
    for step in (1, 3, 2):
        wave_copy(step).wait_send()


def finish(wave_in, energy_in, left_in, right_in, wave, energy, left, right, wave_held, left_held, right_held, load_sem, store_sem):
    channels = left_in.shape[0]
    cuts = [channels * n // 4 for n in range(5)]
    loads, stores = [], []

    def through(source, held, target, part):
        n = len(loads)
        loads.append(pltpu.make_async_copy(source.at[part], held.at[part], load_sem.at[n]))
        stores.append(pltpu.make_async_copy(held.at[part], target.at[part], store_sem.at[n]))

    for lo, hi in zip(cuts[:-1], cuts[1:]):
        through(left_in, left_held, left, pl.ds(lo, hi - lo))
        through(right_in, right_held, right, pl.ds(lo, hi - lo))
    through(wave_in, wave_held, wave, pl.ds(0, RUN))
    for load in loads:
        load.start()
    energy[0] = energy_in[0, 0]
    for load, store in zip(loads, stores):
        load.wait()
        store.start()
    for store in stores:
        store.wait()


def body(
    left_boundary,
    right_boundary,
    psi_start,
    left_local,
    right_group,
    right_local,
    left_dims,
    right_dims,
    left_mix,
    right_mix,
):
    channels = left_boundary.shape[1]
    smem = pl.BlockSpec(memory_space=pltpu.SMEM)
    vmem = pl.BlockSpec(memory_space=pltpu.VMEM)
    hbm = pl.BlockSpec(memory_space=pl.ANY)
    table = pl.pallas_call(
        router,
        out_shape=jax.ShapeDtypeStruct((TABLE,), jnp.int32),
        in_specs=[smem] * 5,
        out_specs=smem,
        scratch_shapes=[pltpu.SMEM((16,), jnp.int32)],
        name="router",
    )(
        left_local,
        right_group[:, :, 0],
        right_local,
        left_dims,
        right_dims,
    )
    dma = pltpu.SemaphoreType.DMA
    env = (channels, SEC, N, N)
    region = max(channels * PACK, SEC * (channels * HALF + 32))
    wave, energy, left_grown, right_grown = pl.pallas_call(
        lambda *refs: kernel(channels, *refs),
        out_shape=(
            jax.ShapeDtypeStruct((RUN, N, N), BF16),
            jax.ShapeDtypeStruct((8, N), F32),
            jax.ShapeDtypeStruct(env, BF16),
            jax.ShapeDtypeStruct(env, BF16),
        ),
        in_specs=[smem, smem, smem, hbm, hbm, vmem],
        out_specs=(vmem, vmem, hbm, hbm),
        scratch_shapes=[
            pltpu.VMEM((2,) + env, BF16),
            pltpu.VMEM((2, SIDE * SEC, channels, N, N), BF16),
            pltpu.VMEM((2, SIDE * region, N), BF16),
            pltpu.VMEM((2, SIDE * region, N), BF16),
            pltpu.VMEM((max(4 * SLOTS, 8 * channels), N, N), F32),
            pltpu.VMEM((SLOTS, N, N), BF16),
            pltpu.VMEM((SLOTS, N, N), BF16),
            pltpu.VMEM((SLOTS, N, N), BF16),
            pltpu.VMEM((SLOTS, N, N), BF16),
            pltpu.VMEM((SLOTS, N, N), BF16),
            pltpu.VMEM((TERMS, channels * HALF, 2 * N), BF16),
            pltpu.VMEM((2, -(-channels // 2) * 16, 2 * N), F32),
            pltpu.VMEM((3, SIDE * SIDE, 8, N), F32),
            pltpu.VMEM((3, 8, N), F32),
            dma((2,)),
            dma((2, SEC)),
            dma((6,)),
            dma((6,)),
            dma((2, channels)),
            dma((2, channels)),
            dma((2, 3, channels)),
            dma((2, 3, channels)),
            dma((3, SIDE * SIDE)),
            dma((3, SIDE * SIDE)),
            dma((2, 3, SEC)),
            dma((2, 3, SEC)),
        ],
        compiler_params=pltpu.CompilerParams(
            collective_id=0, has_side_effects=True, vmem_limit_bytes=62 * 2**20
        ),
        name="davidson",
    )(
        table,
        left_mix,
        right_mix,
        left_boundary[0],
        right_boundary[0],
        psi_start[0],
    )
    wave, energy, left_grown, right_grown = pl.pallas_call(
        finish,
        out_shape=(
            jax.ShapeDtypeStruct(wave.shape, BF16),
            jax.ShapeDtypeStruct((1,), F32),
            jax.ShapeDtypeStruct(env, BF16),
            jax.ShapeDtypeStruct(env, BF16),
        ),
        in_specs=[hbm, vmem, hbm, hbm],
        out_specs=(hbm, smem, hbm, hbm),
        scratch_shapes=[
            pltpu.VMEM(wave.shape, BF16),
            pltpu.VMEM(env, BF16),
            pltpu.VMEM(env, BF16),
            dma((9,)),
            dma((9,)),
        ],
        compiler_params=pltpu.CompilerParams(vmem_limit_bytes=62 * 2**20),
        name="finish",
    )(wave, energy, left_grown, right_grown)
    return wave[None], energy, left_grown[None], right_grown[None]


def solution(mesh):
    return jax.shard_map(
        body,
        mesh=mesh,
        in_specs=(
            P("sect", None, "blk", None, None),
            P("sect", None, "blk", None, None),
            P("sect", "blk", None, None),
            P("sect", None),
            P("sect", None, None),
            P("sect", None),
            P("sect", None),
            P("sect", None),
            P(),
            P(),
        ),
        out_specs=(
            P("sect", "blk", None, None),
            P("sect"),
            P("sect", None, "blk", None, None),
            P("sect", None, "blk", None, None),
        ),
        check_vma=False,
    )
```

```python
import math

import jax
import jax.numpy as jnp
from jax import lax
from jax.experimental import pallas as pl
from jax.experimental.pallas import tpu as pltpu
from jax.sharding import PartitionSpec as P

MESH = pl.DeviceIdType.MESH
F32 = jnp.float32
BF16 = jnp.bfloat16
EPSILON = 1e-06

N = 128
HALF = 64
SIDE = 4
SEC = 4
RANKS = 2
SLOTS = SIDE * SIDE * RANKS
RUN = 24
PACK = SEC * HALF + 16
UNROLL = 4
TERMS = 4
PARTS = SLOTS // UNROLL
RING, HAND, OPEN = 3, 7, 10

SEND, SLOT_OF, LSEC, RSEC, LDIM, RDIM = 0, 32, 64, 96, 128, 160
ORD_R, KEEP_R, LAST_R, LIVE_R = 192, 224, 256, 272
ORD_L, KEEP_L, LAST_L, LIVE_L = 288, 320, 352, 368
SPARE = 384 - LSEC
TABLE = 512


def places(me, swap):
    x, y = me // SIDE, me % SIDE
    return x * (1 - swap) + y * swap, y * (1 - swap) + x * swap


def device_at(u, w, swap):
    return (u * SIDE + w) * (1 - swap) + (w * SIDE + u) * swap


def router(left_local, right_group, right_local, left_dims, right_dims, table, count):
    me = lax.axis_index("blk")
    swap = lax.axis_index("sect") & 1
    my_u, my_w = places(me, swap)
    for i in range(SLOTS):
        table[SEND + i] = 0
        table[LSEC + i] = (i // 8) * SEC
        table[RSEC + i] = (i % 8 // 2) * SEC
        table[LDIM + i] = 0
        table[RDIM + i] = 0

    def zero_counts():
        for i in range(SIDE * SIDE):
            count[i] = 0

    def split(group):
        x, y = group >> 2, group & 3
        return x * (1 - swap) + y * swap, y * (1 - swap) + x * swap

    zero_counts()
    for e in range(RUN):
        group = right_group[0, me * RUN + e]
        rank = jnp.minimum(count[group], RANKS - 1)
        count[group] = rank + 1
        u, w = split(group)
        slot = w * 8 + u * 2 + rank
        table[SLOT_OF + e] = slot
        table[SEND + slot] = e
    for source in range(SIDE):
        run = device_at(my_u, source, swap)
        zero_counts()
        for e in range(RUN):
            at = run * RUN + e
            group = right_group[0, at]
            rank = jnp.minimum(count[group], RANKS - 1)
            count[group] = rank + 1
            u, w = split(group)
            slot = jnp.where(w == my_w, source * 8 + u * 2 + rank, SPARE)
            left, right = left_local[0, at], right_local[0, at]
            table[LSEC + slot] = source * SEC + left
            table[RSEC + slot] = u * SEC + right
            table[LDIM + slot] = left_dims[0, run * SEC + left]
            table[RDIM + slot] = right_dims[0, group * SEC + right]
    for key, order, keep, last, live in (
        (LSEC, ORD_R, KEEP_R, LAST_R, LIVE_R),
        (RSEC, ORD_L, KEEP_L, LAST_L, LIVE_L),
    ):
        zero_counts()
        for s in range(SLOTS):
            sector = table[key + s]
            count[sector] = count[sector] + 1
        for g in range(SIDE):
            begin = jnp.int32(0)
            for j in range(SEC):
                sector = g * SEC + j
                amount = count[sector]
                count[sector] = g * 8 + begin
                table[live + sector] = jnp.minimum(amount, 1)
                begin = begin + amount
                table[last + sector] = jnp.maximum(begin - 1, 0)
        for s in range(SLOTS):
            sector = table[key + s]
            at = count[sector]
            count[sector] = at + 1
            table[order + at] = s
        for g in range(SIDE):
            before = jnp.int32(-1)
            for p in range(g * 8, g * 8 + 8):
                sector = table[key + table[order + p]]
                table[keep + p] = jnp.where(sector == before, 1, 0)
                before = sector


def dot(a, b):
    return jnp.dot(a, b, preferred_element_type=F32)


def triangle_masks():
    row = lax.broadcasted_iota(jnp.int32, (HALF, N), 0)
    col = lax.broadcasted_iota(jnp.int32, (HALF, N), 1)
    left = col < HALF
    below = jnp.logical_and(left, row > col)
    low = jnp.logical_and(col >= HALF, row > col - HALF)
    high = jnp.logical_and(col >= HALF, row < col - HALF)
    diag = row == col - HALF
    return below, left, low, high, diag, row == col


def triangle_bits(masks):
    below, left, low, high, diag = [jnp.where(m, 1.0, 0.0).astype(BF16) for m in masks[:5]]
    return below, jnp.where(masks[0], 0.0, 1.0).astype(BF16), left, low, high, diag


def pack(block, masks):
    below, diag = masks[0], masks[4]
    corner = block[HALF:]
    upper = jnp.where(below, pltpu.roll(corner, HALF, 1), block[:HALF])
    row = jnp.sum(jnp.where(diag, corner, 0.0), axis=0, keepdims=True)
    return upper, row


def unpack(packed, row, masks):
    below, above, left, low, high, diag = masks
    turned = jnp.concatenate([packed, packed], axis=0).T
    rolled = pltpu.roll(packed.astype(F32), HALF, 1).astype(BF16)
    top = packed * above + turned[:HALF] * below
    bottom = (
        turned[HALF:] * left
        + rolled * low
        + turned[:HALF] * high
        + jnp.broadcast_to(row, (HALF, N)).astype(BF16) * diag
    )
    return jnp.concatenate([top, bottom], axis=0)


def kernel(
    channels,
    table,
    left_mix,
    right_mix,
    left_hbm,
    right_hbm,
    psi,
    wave,
    energy,
    left_out,
    right_out,
    bound,
    cat,
    gath,
    outb,
    work,
    vec,
    vect,
    vecr,
    vectr,
    ret,
    stack,
    spread,
    red,
    mine,
    local_sem,
    store_sem,
    psi_send,
    psi_recv,
    z_send,
    z_recv,
    ring_send,
    ring_recv,
    red_send,
    red_recv,
    grow_send,
    grow_recv,
):
    n_sect = lax.axis_size("sect")
    sect = lax.axis_index("sect")
    me = lax.axis_index("blk")
    swap = sect % 2
    my_u, my_w = places(me, swap)
    up, down = (sect + 1) % n_sect, (sect + n_sect - 1) % n_sect
    deep = channels * HALF + 32
    region = max(channels * PACK, SEC * deep)

    def along(side, step):
        if side == 0:
            return device_at(my_u, (my_w + step) % SIDE, swap)
        return device_at((my_u + step) % SIDE, my_w, swap)

    def rows_of(group, k):
        return pl.ds(pl.multiple_of(group * region + k * PACK, 16), PACK)

    def sector_rows(place, j):
        return pl.ds(pl.multiple_of(place * region + j * deep, 16), deep)

    barrier = pltpu.get_barrier_semaphore()

    def greet(d, _):
        pl.semaphore_signal(
            barrier, inc=1, device_id={"blk": (me + d) % (SIDE * SIDE)}, device_id_type=MESH
        )
        return 0

    lax.fori_loop(1, SIDE * SIDE, greet, 0)
    pl.semaphore_signal(barrier, inc=1, device_id={"sect": up}, device_id_type=MESH)
    pl.semaphore_signal(barrier, inc=1, device_id={"sect": down}, device_id_type=MESH)

    loads = [
        pltpu.make_async_copy(left_hbm, bound.at[0], local_sem.at[0]),
        pltpu.make_async_copy(right_hbm, bound.at[1], local_sem.at[1]),
    ]
    for load in loads:
        load.start()

    def fill(i, _):
        ret[i] = psi[table[SEND + i]].astype(BF16)
        return 0

    lax.fori_loop(0, SLOTS, fill, 0)
    pl.semaphore_wait(barrier, SIDE * SIDE + 1)

    def psi_copy(step):
        to_w = (my_w + step) % SIDE
        return pltpu.make_async_remote_copy(
            src_ref=ret.at[pl.ds(to_w * 8, 8)],
            dst_ref=vec.at[pl.ds(my_w * 8, 8)],
            send_sem=psi_send.at[step - 1],
            recv_sem=psi_recv.at[step - 1],
            device_id={"blk": along(0, step)},
            device_id_type=MESH,
        )

    for step in (1, 3, 2):
        psi_copy(step).start()

    masks = triangle_masks()
    below, diag_low = masks[0], masks[5]
    bits = triangle_bits(masks)
    row32 = lax.broadcasted_iota(jnp.int32, (32, N), 0)
    row16 = lax.broadcasted_iota(jnp.int32, (16, N), 0)
    eye_packed = jnp.where(
        lax.broadcasted_iota(jnp.int32, (HALF, N), 0) == lax.broadcasted_iota(jnp.int32, (HALF, N), 1),
        1.0,
        0.0,
    )
    eye_row = jnp.where(lax.broadcasted_iota(jnp.int32, (1, N), 1) >= HALF, 1.0, 0.0)

    lane = lax.broadcasted_iota(jnp.int32, (8, 2 * N), 1) - lax.broadcasted_iota(jnp.int32, (8, 2 * N), 0)
    spread[...] = jnp.zeros_like(spread)

    def spread_mix(v, _):
        for kind, mix in enumerate((left_mix, right_mix)):
            rows = jnp.zeros((8, 2 * N), F32)
            for k in range(channels):
                rows = jnp.where(lane == 8 * k, mix[k, v], rows)
            spread[kind, pl.ds(pl.multiple_of(v * 8, 8), 8)] = rows
        return 0

    lax.fori_loop(0, channels, spread_mix, 0)

    def place(side):
        return my_w if side == 0 else my_u

    def z_copy(side, k):
        return pltpu.make_async_remote_copy(
            src_ref=outb.at[side, rows_of(3, k)],
            dst_ref=gath.at[side, rows_of(place(1 - side), k)],
            send_sem=z_send.at[side, k],
            recv_sem=z_recv.at[side, k],
            device_id={"sect": up if side == 0 else down},
            device_id_type=MESH,
        )

    def pack_bound(k):
        for side in range(2):
            edge = sect == (n_sect - 1 if side == 0 else 0)
            here = k == (0 if side == 0 else channels - 1)
            one = jnp.where(here, 1.0, 0.0)
            rows = jnp.zeros((16, N), F32)
            base = 3 * region + k * PACK
            for j in range(SEC):
                upper, row = pack(bound[side, k, j].astype(F32), masks)
                upper = jnp.where(edge, eye_packed * one, upper)
                row = jnp.where(edge, eye_row * one, row)
                outb[side, pl.ds(pl.multiple_of(base + j * HALF, 16), HALF)] = upper.astype(BF16)
                rows = jnp.where(row16 == j, jnp.broadcast_to(row, (16, N)), rows)
            outb[side, pl.ds(pl.multiple_of(base + SEC * HALF, 16), 16)] = rows.astype(BF16)
            z_copy(side, k).start()

    def ring_copy(side, which, k, back):
        at = place(side)
        if which == 2:
            at = (at + (1 if back else SIDE - 1)) % SIDE
        step = SIDE - 1 if back else 1
        return pltpu.make_async_remote_copy(
            src_ref=gath.at[side, rows_of(at, k)],
            dst_ref=gath.at[side, rows_of(at, k)],
            send_sem=ring_send.at[side, which, k],
            recv_sem=ring_recv.at[side, which, k],
            device_id={"blk": along(side, step)},
            device_id_type=MESH,
        )

    def dims_mask(slot):
        rows = lax.broadcasted_iota(jnp.int32, (N, N), 0) < table[LDIM + slot]
        cols = lax.broadcasted_iota(jnp.int32, (N, N), 1) < table[RDIM + slot]
        return jnp.logical_and(rows, cols)

    X, HX, T, HT = 0, SLOTS, 2 * SLOTS, 3 * SLOTS

    for load in loads:
        load.wait()

    def beside(side, sector, lo=0, hi=channels):
        return jnp.concatenate([cat[side, sector, k] for k in range(lo, hi)], axis=1)

    def product(blocks, slots, lo=0, hi=channels):
        inner = []
        for block, s in zip(blocks, slots):
            z = dot(block, beside(1, table[RSEC + s], lo, hi)).astype(BF16)
            inner.append(jnp.concatenate([z[:, k * N : (k + 1) * N] for k in range(hi - lo)], axis=0))
        return [dot(beside(0, table[LSEC + s], lo, hi), z) for s, z in zip(slots, inner)]

    bounds = list(range(0, channels, 5)) + [channels]
    groups = list(zip(bounds[:-1], bounds[1:]))

    def apply(lo, hi, i):
        slots = [i * UNROLL + u for u in range(UNROLL)]
        images = product([vec[s] for s in slots], slots, lo, hi)
        for s, image in zip(slots, images):
            work[HX + s] = image if lo == 0 else work[HX + s] + image

    def gather_step(t, _):
        @pl.when(t < channels)
        def _():
            pack_bound(t)

        @pl.when(jnp.logical_and(t >= RING, t < channels + RING))
        def _():
            k = t - RING
            for side in range(2):
                z_copy(side, k).wait_recv()
                ring_copy(side, 0, k, False).start()
                ring_copy(side, 1, k, True).start()

        @pl.when(jnp.logical_and(t >= HAND, t < channels + HAND))
        def _():
            k = t - HAND
            for side in range(2):
                ring_copy(side, 0, k, False).wait_recv()
                ring_copy(side, 1, k, True).wait_recv()

            @pl.when(k % 2 == 0)
            def _():
                for side in range(2):
                    ring_copy(side, 2, k, False).start()

            @pl.when(k % 2 == 1)
            def _():
                for side in range(2):
                    ring_copy(side, 2, k, True).start()

        @pl.when(t == OPEN)
        def _():
            for step in (1, 3, 2):
                psi_copy(step).wait_recv()
            for i in range(8):
                vec[my_w * 8 + i] = ret[my_w * 8 + i]

            def start(i, _):
                vec[i] = jnp.where(dims_mask(i), vec[i].astype(F32), 0.0).astype(BF16)
                return 0

            lax.fori_loop(0, SLOTS, start, 0)

        @pl.when(t >= OPEN)
        def _():
            k = t - OPEN
            for side in range(2):
                ring_copy(side, 2, k, False).wait_recv()

            def open_group(g, _):
                base = g * region + k * PACK
                for side in range(2):
                    rows = gath[side, pl.ds(pl.multiple_of(base + SEC * HALF, 16), 16)].astype(F32)
                    for j in range(SEC):
                        row = jnp.sum(jnp.where(row16 == j, rows, 0.0), axis=0, keepdims=True)
                        packed = gath[side, pl.ds(pl.multiple_of(base + j * HALF, 16), HALF)]
                        cat[side, g * SEC + j, k] = unpack(packed, row, bits)
                return 0

            lax.fori_loop(0, SIDE, open_group, 0)

            for lo, hi in groups[:-1]:

                @pl.when(jnp.logical_and(k >= hi, k < hi + PARTS // 2))
                def _():
                    for n in range(2):
                        apply(lo, hi, (k - hi) * 2 + n)

        return 0

    lax.fori_loop(0, channels + OPEN, gather_step, 0)
    for lo, hi in groups:
        done = min(max(channels - hi, 0) * 2, PARTS) if hi < channels else 0

        def rest(i, _):
            apply(lo, hi, i)
            return 0

        if done < PARTS:
            lax.fori_loop(done, PARTS, rest, 0)

    for step in (1, 3, 2):
        psi_copy(step).wait_send()

    def settle(k, _):
        for side in range(2):
            z_copy(side, k).wait_send()
            for which in range(3):
                ring_copy(side, which, k, False).wait_send()
        return 0

    lax.fori_loop(0, channels, settle, 0)

    def fold(block):
        return jnp.sum(block.reshape(N // 8, 8, N), axis=0)

    def exchange(number, parts):
        rows = [jnp.sum(p, axis=0, keepdims=True) for p in parts]
        rows += [jnp.zeros((1, N), F32)] * (8 - len(rows))
        mine[number] = jnp.concatenate(rows, axis=0)

        def copy(d):
            return pltpu.make_async_remote_copy(
                src_ref=mine.at[number],
                dst_ref=red.at[number, me],
                send_sem=red_send.at[number, d],
                recv_sem=red_recv.at[number, d],
                device_id={"blk": (me + d) % (SIDE * SIDE)},
                device_id_type=MESH,
            )

        for d in range(1, SIDE * SIDE):
            copy(d).start()
        red[number, me] = mine[number]

        for d in range(1, SIDE * SIDE):
            copy(d).wait()
        total = jnp.sum(red[number], axis=0)
        total = jnp.broadcast_to(jnp.sum(total, axis=1, keepdims=True), (8, N))
        return [total[i : i + 1] for i in range(len(parts))]

    zero8 = jnp.zeros((8, N), F32)

    def first_sums(s, sums):
        ss, sh, hh = sums
        start = vec[s].astype(F32)
        image = jnp.where(dims_mask(s), work[HX + s], 0.0)
        work[HX + s] = image
        return ss + fold(start * start), sh + fold(start * image), hh + fold(image * image)

    ss, sh, hh = exchange(0, lax.fori_loop(0, SLOTS, first_sums, (zero8,) * 3))
    norm = jnp.sqrt(ss)
    xx = ss / (norm * norm)
    a = sh / (norm * norm)
    hxhx = hh / (norm * norm)
    b = jnp.sqrt(jnp.maximum(hxhx - 2.0 * a * a + a * a * xx, 0.0) + EPSILON)

    per_norm, per_b = 1.0 / norm, 1.0 / b

    def first_correction(i, sums):
        slots = [i * UNROLL + u for u in range(UNROLL)]
        blocks = []
        for s in slots:
            x = vec[s].astype(F32) * per_norm
            hx = work[HX + s] * per_norm
            t = (hx - a * x) * per_b
            work[X + s] = x
            work[HX + s] = hx
            work[T + s] = t
            blocks.append(t.astype(BF16))
        for s, image in zip(slots, product(blocks, slots)):
            ht = jnp.where(dims_mask(s), image, 0.0)
            work[HT + s] = ht
            x, hx, t = work[X + s], work[HX + s], work[T + s]
            terms = (x * t, t * t, x * ht, t * hx, t * ht, hx * ht, ht * ht)
            sums = tuple(old + fold(term) for old, term in zip(sums, terms))
        return sums

    xt, tt, xht, thx, c, hxht, htht = exchange(
        1, lax.fori_loop(0, SLOTS // UNROLL, first_correction, (zero8,) * 7)
    )

    def ritz(a, b, c):
        value = 0.5 * (a + c) - jnp.sqrt(0.25 * (a - c) * (a - c) + b * b)
        old, new = c - value, -b
        length = jnp.sqrt(old * old + new * new)
        return value, old / length, new / length

    _, p, q = ritz(a, b, c)
    a2 = p * p * a + p * q * (xht + thx) + q * q * c
    xx2 = p * p * xx + 2.0 * p * q * xt + q * q * tt
    hxhx2 = p * p * hxhx + 2.0 * p * q * hxht + q * q * htht
    b2 = jnp.sqrt(jnp.maximum(hxhx2 - 2.0 * a2 * a2 + a2 * a2 * xx2, 0.0) + EPSILON)

    per_b2 = 1.0 / b2

    def second_correction(i, total):
        slots = [i * UNROLL + u for u in range(UNROLL)]
        blocks = []
        for s in slots:
            x = p * work[X + s] + q * work[T + s]
            hx = p * work[HX + s] + q * work[HT + s]
            t = (hx - a2 * x) * per_b2
            work[X + s] = x
            work[T + s] = t
            blocks.append(t.astype(BF16))
        for s, image in zip(slots, product(blocks, slots)):
            total = total + fold(work[T + s] * jnp.where(dims_mask(s), image, 0.0))
        return total

    (c2,) = exchange(2, [lax.fori_loop(0, SLOTS // UNROLL, second_correction, zero8)])
    value, p2, q2 = ritz(a2, b2, c2)
    energy[...] = jnp.broadcast_to(value, (8, N))
    scale = N * math.sqrt(RUN * SIDE * SIDE)

    def final_vector(s, _):
        w = ((p2 * work[X + s] + q2 * work[T + s]) * scale).astype(BF16)
        turned = w.T
        vec[s] = w
        vect[s] = turned
        vecr[s] = pltpu.roll(w.astype(F32), HALF, 1).astype(BF16)
        vectr[s] = pltpu.roll(turned.astype(F32), HALF, 1).astype(BF16)
        return 0

    lax.fori_loop(0, SLOTS, final_vector, 0)

    def wave_copy(step):
        to_w = (my_w + step) % SIDE
        return pltpu.make_async_remote_copy(
            src_ref=vec.at[pl.ds(to_w * 8, 8)],
            dst_ref=ret.at[pl.ds(my_w * 8, 8)],
            send_sem=psi_send.at[step + 2],
            recv_sem=psi_recv.at[step + 2],
            device_id={"blk": along(0, step)},
            device_id_type=MESH,
        )

    def grow(kind, group, to):
        order, keep, last, live = (
            (ORD_L, KEEP_L, LAST_L, LIVE_L) if kind == 0 else (ORD_R, KEEP_R, LAST_R, LIVE_R)
        )
        outer, sector_at = (vect, LSEC) if kind == 0 else (vec, RSEC)
        closing, closing_rolled = (vec, vecr) if kind == 0 else (vect, vectr)
        nothing = jnp.zeros((N, N), BF16)

        def term(i, _):
            spots = [i * TERMS + u for u in range(TERMS)]
            slots = [table[order + group * 8 + spot] for spot in spots]
            for u, slot in enumerate(slots):
                z = dot(outer[slot], beside(kind, table[sector_at + slot])).astype(BF16)
                for k in range(channels):
                    part = z[:, k * N : (k + 1) * N]
                    stack[u, pl.ds(k * HALF, HALF), pl.ds(0, N)] = part[:HALF]
                    stack[u, pl.ds(k * HALF, HALF), pl.ds(N, N)] = part[HALF:]
            for u, (spot, slot) in enumerate(zip(spots, slots)):
                square = jnp.concatenate(
                    [
                        jnp.concatenate([closing[slot], nothing], axis=1),
                        jnp.concatenate([nothing, closing_rolled[slot]], axis=1),
                    ],
                    axis=0,
                )
                both = dot(stack[u], square)
                stay = table[keep + group * 8 + spot] > 0
                for k in range(channels):
                    rows = both[k * HALF : (k + 1) * HALF]
                    upper = jnp.where(below, rows[:, N:], rows[:, :N])
                    trace = jnp.where(diag_low, rows[:, N:], 0.0)
                    trace = jnp.sum(trace.reshape(HALF // 8, 8, N), axis=0)
                    before = jnp.maximum(spot - 1, 0) * channels + k
                    now = spot * channels + k
                    work[now, pl.ds(0, HALF)] = upper + jnp.where(stay, work[before, pl.ds(0, HALF)], 0.0)
                    work[now, pl.ds(HALF, 8)] = trace + jnp.where(stay, work[before, pl.ds(HALF, 8)], 0.0)
            return 0

        lax.fori_loop(0, 8 // TERMS, term, 0)

        def close(k, diagonals):
            after = []
            for j in range(SEC):
                spot = table[last + group * SEC + j]
                upper = work[spot * channels + k, pl.ds(0, HALF)]
                row = jnp.sum(work[spot * channels + k, pl.ds(HALF, 8)], axis=0, keepdims=True)
                at = pl.multiple_of(to * region + j * deep + k * HALF, 16)
                has = table[live + group * SEC + j] > 0
                outb[kind, pl.ds(at, HALF)] = jnp.where(has, upper, 0.0).astype(BF16)
                after.append(jnp.where(row32 == k, jnp.broadcast_to(row, (32, N)), diagonals[j]))
            return tuple(after)

        diagonals = lax.fori_loop(0, channels, close, (jnp.zeros((32, N), F32),) * SEC)
        for j in range(SEC):
            has = table[live + group * SEC + j] > 0
            at = to * region + j * deep + channels * HALF
            outb[kind, pl.ds(at, 32)] = jnp.where(has, diagonals[j], 0.0).astype(BF16)

    def grow_copy(kind, target, j):
        back = target == 2 or (target == 0 and j >= 2)
        return pltpu.make_async_remote_copy(
            src_ref=outb.at[kind, sector_rows(target, j)],
            dst_ref=gath.at[kind, sector_rows(target, j)],
            send_sem=grow_send.at[kind, target, j],
            recv_sem=grow_recv.at[kind, target, j],
            device_id={"blk": along(1 - kind, SIDE - 1 if back else 1)},
            device_id_type=MESH,
        )

    def my_group(kind, step):
        return ((my_u if kind == 0 else my_w) + step) % SIDE

    for step in (1, 3, 2):
        wave_copy(step).start()
    for kind in range(2):
        grow(kind, my_group(kind, 2), 0)
        for j in (0, 2, 1, 3):
            grow_copy(kind, 0, j).start()
    for kind in range(2):
        grow(kind, my_group(kind, 1), 1)
        for j in (2, 3):
            grow_copy(kind, 1, j).start()
    for kind in range(2):
        grow(kind, my_group(kind, SIDE - 1), 2)
        for j in (0, 1):
            grow_copy(kind, 2, j).start()
    for j in (0, 2, 1, 3):
        target = 1 if j < 2 else 2
        for kind in range(2):
            grow_copy(kind, 0, j).wait_recv()

            def add(i, _):
                there = pl.ds(pl.multiple_of(target * region + j * deep + i * 32, 16), 32)
                here = pl.ds(pl.multiple_of(j * deep + i * 32, 16), 32)
                total = outb[kind, there].astype(F32) + gath[kind, here].astype(F32)
                outb[kind, there] = total.astype(BF16)
                return 0

            lax.fori_loop(0, deep // 32, add, 0)
            grow_copy(kind, target, j).start()
    for kind in range(2):
        grow(kind, my_group(kind, 0), 3)

    for step in (1, 3, 2):
        wave_copy(step).wait_recv()
    for i in range(8):
        ret[my_w * 8 + i] = vec[my_w * 8 + i]

    def take(e, _):
        wave[e] = ret[table[SLOT_OF + e]]
        return 0

    lax.fori_loop(0, RUN, take, 0)

    shrink = 1.0 / math.sqrt(N)

    def store(kind, j):
        out = left_out if kind == 0 else right_out
        return pltpu.make_async_copy(bound.at[kind, :, j, pl.ds(0, HALF + 16)], out.at[:, j], store_sem.at[kind, j])

    for j, kind in [(j, kind) for j in (0, 2, 1, 3) for kind in range(2)]:
        for target in (1, 2):
            grow_copy(kind, target, j).wait_recv()

        def total(at, size):
            own, before, after = (
                pl.ds(pl.multiple_of(spot * region + j * deep + at, 16), size) for spot in (3, 1, 2)
            )
            parts = outb[kind, own].astype(F32) + gath[kind, before].astype(F32)
            return (parts + gath[kind, after].astype(F32)) * shrink

        diagonals = pltpu.roll(total(channels * HALF, 32), HALF, 1)
        for k in range(channels):
            work[k, pl.ds(0, HALF)] = total(k * HALF, HALF)
            work[k, pl.ds(HALF, 8)] = jnp.broadcast_to(diagonals[k : k + 1], (8, N))

        factor = spread[kind]
        high_part = factor.astype(BF16)
        low_part = (factor - high_part.astype(F32)).astype(BF16)

        def eight(r):
            rows = [work[k, pl.ds(r * 8, 8)] for k in range(channels)]
            rows.append(jnp.zeros((2 * N - 8 * channels, N), F32))
            return jnp.concatenate(rows, axis=0).astype(BF16)

        for start in range(0, 9, 2):
            count = min(2, 9 - start)
            rows = jnp.concatenate([eight(start + n) for n in range(count)], axis=1)
            mixed = dot(high_part, rows) + dot(low_part, rows)
            for v in range(channels):
                for n in range(count):
                    work[32 + v, pl.ds((start + n) * 8, 8)] = mixed[v * 8 : v * 8 + 8, n * N : n * N + N]

        for v in range(channels):
            row = jnp.broadcast_to(work[32 + v, pl.ds(HALF, 1)], (16, N))
            bound[kind, v, j, pl.ds(0, HALF)] = work[32 + v, pl.ds(0, HALF)].astype(BF16)
            bound[kind, v, j, pl.ds(HALF, 16)] = row.astype(BF16)
        store(kind, j).start()
    for kind in range(2):
        for j in range(SEC):
            store(kind, j).wait()
            for target in range(3):
                grow_copy(kind, target, j).wait_send()
    for step in (1, 3, 2):
        wave_copy(step).wait_send()


def finish(wave_in, energy_in, left_in, right_in, wave, energy, left, right, wave_held, packed, whole, load_sem, store_sem):
    channels = left_in.shape[0]
    cuts = [channels * n // 6 for n in range(7)]
    parts = [(kind, lo, hi) for lo, hi in zip(cuts[:-1], cuts[1:]) for kind in range(2)]

    def load(n):
        kind, lo, hi = parts[n]
        source = (left_in, right_in)[kind]
        return pltpu.make_async_copy(
            source.at[pl.ds(lo, hi - lo)], packed.at[kind, pl.ds(lo, hi - lo)], load_sem.at[n]
        )

    def store(n):
        kind, lo, hi = parts[n]
        target = (left, right)[kind]
        return pltpu.make_async_copy(
            whole.at[kind, pl.ds(lo, hi - lo)], target.at[pl.ds(lo, hi - lo)], store_sem.at[n]
        )

    wave_load = pltpu.make_async_copy(wave_in, wave_held, load_sem.at[len(parts)])
    wave_store = pltpu.make_async_copy(wave_held, wave, store_sem.at[len(parts)])
    for n in range(len(parts)):
        load(n).start()
        if n == 1:
            wave_load.start()
    energy[0] = energy_in[0, 0]
    bits = triangle_bits(triangle_masks())
    for n, (kind, lo, hi) in enumerate(parts):
        load(n).wait()

        for k, j in [(k, j) for k in range(lo, hi) for j in range(SEC)]:
            row = packed[kind, k, j, pl.ds(HALF, 16)].astype(F32)[:1]
            whole[kind, k, j] = unpack(packed[kind, k, j, pl.ds(0, HALF)], row, bits)
        store(n).start()
        if n == 1:
            wave_load.wait()
            wave_store.start()
    for n in range(len(parts)):
        store(n).wait()
    wave_store.wait()


def body(
    left_boundary,
    right_boundary,
    psi_start,
    left_local,
    right_group,
    right_local,
    left_dims,
    right_dims,
    left_mix,
    right_mix,
):
    channels = left_boundary.shape[1]
    smem = pl.BlockSpec(memory_space=pltpu.SMEM)
    vmem = pl.BlockSpec(memory_space=pltpu.VMEM)
    hbm = pl.BlockSpec(memory_space=pl.ANY)
    table = pl.pallas_call(
        router,
        out_shape=jax.ShapeDtypeStruct((TABLE,), jnp.int32),
        in_specs=[smem] * 5,
        out_specs=smem,
        scratch_shapes=[pltpu.SMEM((16,), jnp.int32)],
        name="router",
    )(
        left_local,
        right_group[:, :, 0],
        right_local,
        left_dims,
        right_dims,
    )
    dma = pltpu.SemaphoreType.DMA
    env = (channels, SEC, N, N)
    region = max(channels * PACK, SEC * (channels * HALF + 32))
    wave, energy, left_grown, right_grown = pl.pallas_call(
        lambda *refs: kernel(channels, *refs),
        out_shape=(
            jax.ShapeDtypeStruct((RUN, N, N), BF16),
            jax.ShapeDtypeStruct((8, N), F32),
            jax.ShapeDtypeStruct((channels, SEC, HALF + 16, N), BF16),
            jax.ShapeDtypeStruct((channels, SEC, HALF + 16, N), BF16),
        ),
        in_specs=[smem, smem, smem, hbm, hbm, vmem],
        out_specs=(vmem, vmem, hbm, hbm),
        scratch_shapes=[
            pltpu.VMEM((2,) + env, BF16),
            pltpu.VMEM((2, SIDE * SEC, channels, N, N), BF16),
            pltpu.VMEM((2, SIDE * region, N), BF16),
            pltpu.VMEM((2, SIDE * region, N), BF16),
            pltpu.VMEM((max(4 * SLOTS, 8 * channels), N, N), F32),
            pltpu.VMEM((SLOTS, N, N), BF16),
            pltpu.VMEM((SLOTS, N, N), BF16),
            pltpu.VMEM((SLOTS, N, N), BF16),
            pltpu.VMEM((SLOTS, N, N), BF16),
            pltpu.VMEM((SLOTS, N, N), BF16),
            pltpu.VMEM((TERMS, channels * HALF, 2 * N), BF16),
            pltpu.VMEM((2, -(-channels // 2) * 16, 2 * N), F32),
            pltpu.VMEM((3, SIDE * SIDE, 8, N), F32),
            pltpu.VMEM((3, 8, N), F32),
            dma((2,)),
            dma((2, SEC)),
            dma((6,)),
            dma((6,)),
            dma((2, channels)),
            dma((2, channels)),
            dma((2, 3, channels)),
            dma((2, 3, channels)),
            dma((3, SIDE * SIDE)),
            dma((3, SIDE * SIDE)),
            dma((2, 3, SEC)),
            dma((2, 3, SEC)),
        ],
        compiler_params=pltpu.CompilerParams(
            collective_id=0, has_side_effects=True, vmem_limit_bytes=62 * 2**20
        ),
        name="davidson",
    )(
        table,
        left_mix,
        right_mix,
        left_boundary[0],
        right_boundary[0],
        psi_start[0],
    )
    wave, energy, left_grown, right_grown = pl.pallas_call(
        finish,
        out_shape=(
            jax.ShapeDtypeStruct(wave.shape, BF16),
            jax.ShapeDtypeStruct((1,), F32),
            jax.ShapeDtypeStruct(env, BF16),
            jax.ShapeDtypeStruct(env, BF16),
        ),
        in_specs=[hbm, vmem, hbm, hbm],
        out_specs=(hbm, smem, hbm, hbm),
        scratch_shapes=[
            pltpu.VMEM(wave.shape, BF16),
            pltpu.VMEM((2, channels, SEC, HALF + 16, N), BF16),
            pltpu.VMEM((2,) + env, BF16),
            dma((13,)),
            dma((13,)),
        ],
        compiler_params=pltpu.CompilerParams(vmem_limit_bytes=62 * 2**20),
        name="finish",
    )(wave, energy, left_grown, right_grown)
    return wave[None], energy, left_grown[None], right_grown[None]


def solution(mesh):
    return jax.shard_map(
        body,
        mesh=mesh,
        in_specs=(
            P("sect", None, "blk", None, None),
            P("sect", None, "blk", None, None),
            P("sect", "blk", None, None),
            P("sect", None),
            P("sect", None, None),
            P("sect", None),
            P("sect", None),
            P("sect", None),
            P(),
            P(),
        ),
        out_specs=(
            P("sect", "blk", None, None),
            P("sect"),
            P("sect", None, "blk", None, None),
            P("sect", None, "blk", None, None),
        ),
        check_vma=False,
    )
```

```python
import math

import jax
import jax.numpy as jnp
from jax import lax
from jax.experimental import pallas as pl
from jax.experimental.pallas import tpu as pltpu
from jax.sharding import PartitionSpec as P

MESH = pl.DeviceIdType.MESH
F32 = jnp.float32
BF16 = jnp.bfloat16
EPSILON = 1e-06

N = 128
HALF = 64
SIDE = 4
SEC = 4
RANKS = 2
SLOTS = SIDE * SIDE * RANKS
RUN = 24
PACK = SEC * HALF + 16
UNROLL = 4
TERMS = 4
PARTS = SLOTS // UNROLL
RING, HAND, OPEN = 3, 7, 10

SEND, SLOT_OF, LSEC, RSEC, LDIM, RDIM = 0, 32, 64, 96, 128, 160
ORD_R, KEEP_R, LAST_R, LIVE_R = 192, 224, 256, 272
ORD_L, KEEP_L, LAST_L, LIVE_L = 288, 320, 352, 368
SPARE = 384 - LSEC
TABLE = 512


def places(me, swap):
    x, y = me // SIDE, me % SIDE
    return x * (1 - swap) + y * swap, y * (1 - swap) + x * swap


def device_at(u, w, swap):
    return (u * SIDE + w) * (1 - swap) + (w * SIDE + u) * swap


def router(left_local, right_group, right_local, left_dims, right_dims, table, count):
    me = lax.axis_index("blk")
    swap = lax.axis_index("sect") & 1
    my_u, my_w = places(me, swap)
    for i in range(SLOTS):
        table[SEND + i] = 0
        table[LSEC + i] = (i // 8) * SEC
        table[RSEC + i] = (i % 8 // 2) * SEC
        table[LDIM + i] = 0
        table[RDIM + i] = 0

    def zero_counts():
        for i in range(SIDE * SIDE):
            count[i] = 0

    def split(group):
        x, y = group >> 2, group & 3
        return x * (1 - swap) + y * swap, y * (1 - swap) + x * swap

    zero_counts()
    for e in range(RUN):
        group = right_group[0, me * RUN + e]
        rank = jnp.minimum(count[group], RANKS - 1)
        count[group] = rank + 1
        u, w = split(group)
        slot = w * 8 + u * 2 + rank
        table[SLOT_OF + e] = slot
        table[SEND + slot] = e
    for source in range(SIDE):
        run = device_at(my_u, source, swap)
        zero_counts()
        for e in range(RUN):
            at = run * RUN + e
            group = right_group[0, at]
            rank = jnp.minimum(count[group], RANKS - 1)
            count[group] = rank + 1
            u, w = split(group)
            slot = jnp.where(w == my_w, source * 8 + u * 2 + rank, SPARE)
            left, right = left_local[0, at], right_local[0, at]
            table[LSEC + slot] = source * SEC + left
            table[RSEC + slot] = u * SEC + right
            table[LDIM + slot] = left_dims[0, run * SEC + left]
            table[RDIM + slot] = right_dims[0, group * SEC + right]
    for key, order, keep, last, live in (
        (LSEC, ORD_R, KEEP_R, LAST_R, LIVE_R),
        (RSEC, ORD_L, KEEP_L, LAST_L, LIVE_L),
    ):
        zero_counts()
        for s in range(SLOTS):
            sector = table[key + s]
            count[sector] = count[sector] + 1
        for g in range(SIDE):
            begin = jnp.int32(0)
            for j in range(SEC):
                sector = g * SEC + j
                amount = count[sector]
                count[sector] = g * 8 + begin
                table[live + sector] = jnp.minimum(amount, 1)
                begin = begin + amount
                table[last + sector] = jnp.maximum(begin - 1, 0)
        for s in range(SLOTS):
            sector = table[key + s]
            at = count[sector]
            count[sector] = at + 1
            table[order + at] = s
        for g in range(SIDE):
            before = jnp.int32(-1)
            for p in range(g * 8, g * 8 + 8):
                sector = table[key + table[order + p]]
                table[keep + p] = jnp.where(sector == before, 1, 0)
                before = sector


def dot(a, b):
    return jnp.dot(a, b, preferred_element_type=F32)


def triangle_masks():
    row = lax.broadcasted_iota(jnp.int32, (HALF, N), 0)
    col = lax.broadcasted_iota(jnp.int32, (HALF, N), 1)
    left = col < HALF
    below = jnp.logical_and(left, row > col)
    low = jnp.logical_and(col >= HALF, row > col - HALF)
    high = jnp.logical_and(col >= HALF, row < col - HALF)
    diag = row == col - HALF
    return below, left, low, high, diag, row == col


def triangle_bits(masks):
    below, left, low, high, diag = [jnp.where(m, 1.0, 0.0).astype(BF16) for m in masks[:5]]
    return below, jnp.where(masks[0], 0.0, 1.0).astype(BF16), left, low, high, diag


def pack(block, masks):
    below, diag = masks[0], masks[4]
    corner = block[HALF:]
    upper = jnp.where(below, pltpu.roll(corner, HALF, 1), block[:HALF])
    row = jnp.sum(jnp.where(diag, corner, 0.0), axis=0, keepdims=True)
    return upper, row


def unpack(packed, row, masks):
    below, above, left, low, high, diag = masks
    turned = jnp.concatenate([packed, packed], axis=0).T
    rolled = pltpu.roll(packed.astype(F32), HALF, 1).astype(BF16)
    top = packed * above + turned[:HALF] * below
    bottom = (
        turned[HALF:] * left
        + rolled * low
        + turned[:HALF] * high
        + jnp.broadcast_to(row, (HALF, N)).astype(BF16) * diag
    )
    return jnp.concatenate([top, bottom], axis=0)


def kernel(
    channels,
    table,
    left_mix,
    right_mix,
    left_hbm,
    right_hbm,
    psi,
    wave,
    energy,
    left_out,
    right_out,
    bound,
    cat,
    gath,
    outb,
    work,
    vec,
    vect,
    vecr,
    vectr,
    ret,
    stack,
    spread,
    red,
    mine,
    local_sem,
    store_sem,
    psi_send,
    psi_recv,
    z_send,
    z_recv,
    ring_send,
    ring_recv,
    red_send,
    red_recv,
    grow_send,
    grow_recv,
):
    n_sect = lax.axis_size("sect")
    sect = lax.axis_index("sect")
    me = lax.axis_index("blk")
    swap = sect % 2
    my_u, my_w = places(me, swap)
    up, down = (sect + 1) % n_sect, (sect + n_sect - 1) % n_sect
    deep = channels * HALF + 32
    region = max(channels * PACK, SEC * deep)

    def along(side, step):
        if side == 0:
            return device_at(my_u, (my_w + step) % SIDE, swap)
        return device_at((my_u + step) % SIDE, my_w, swap)

    def rows_of(group, k):
        return pl.ds(pl.multiple_of(group * region + k * PACK, 16), PACK)

    def sector_rows(place, j):
        return pl.ds(pl.multiple_of(place * region + j * deep, 16), deep)

    barrier = pltpu.get_barrier_semaphore()

    def greet(d, _):
        pl.semaphore_signal(
            barrier, inc=1, device_id={"blk": (me + d) % (SIDE * SIDE)}, device_id_type=MESH
        )
        return 0

    lax.fori_loop(1, SIDE * SIDE, greet, 0)
    pl.semaphore_signal(barrier, inc=1, device_id={"sect": up}, device_id_type=MESH)
    pl.semaphore_signal(barrier, inc=1, device_id={"sect": down}, device_id_type=MESH)

    loads = [
        pltpu.make_async_copy(left_hbm, bound.at[0], local_sem.at[0]),
        pltpu.make_async_copy(right_hbm, bound.at[1], local_sem.at[1]),
    ]
    for load in loads:
        load.start()

    def fill(i, _):
        ret[i] = psi[table[SEND + i]].astype(BF16)
        return 0

    lax.fori_loop(0, SLOTS, fill, 0)
    pl.semaphore_wait(barrier, SIDE * SIDE + 1)

    def psi_copy(step):
        to_w = (my_w + step) % SIDE
        return pltpu.make_async_remote_copy(
            src_ref=ret.at[pl.ds(to_w * 8, 8)],
            dst_ref=vec.at[pl.ds(my_w * 8, 8)],
            send_sem=psi_send.at[step - 1],
            recv_sem=psi_recv.at[step - 1],
            device_id={"blk": along(0, step)},
            device_id_type=MESH,
        )

    for step in (1, 3, 2):
        psi_copy(step).start()

    masks = triangle_masks()
    below, diag_low = masks[0], masks[5]
    bits = triangle_bits(masks)
    row32 = lax.broadcasted_iota(jnp.int32, (32, N), 0)
    row16 = lax.broadcasted_iota(jnp.int32, (16, N), 0)
    eye_packed = jnp.where(
        lax.broadcasted_iota(jnp.int32, (HALF, N), 0) == lax.broadcasted_iota(jnp.int32, (HALF, N), 1),
        1.0,
        0.0,
    )
    eye_row = jnp.where(lax.broadcasted_iota(jnp.int32, (1, N), 1) >= HALF, 1.0, 0.0)

    lane = lax.broadcasted_iota(jnp.int32, (8, 2 * N), 1) - lax.broadcasted_iota(jnp.int32, (8, 2 * N), 0)
    spread[...] = jnp.zeros_like(spread)

    def spread_mix(v, _):
        for kind, mix in enumerate((left_mix, right_mix)):
            rows = jnp.zeros((8, 2 * N), F32)
            for k in range(channels):
                rows = jnp.where(lane == 8 * k, mix[k, v], rows)
            spread[kind, pl.ds(pl.multiple_of(v * 8, 8), 8)] = rows
        return 0

    lax.fori_loop(0, channels, spread_mix, 0)

    def place(side):
        return my_w if side == 0 else my_u

    def z_copy(side, k):
        return pltpu.make_async_remote_copy(
            src_ref=outb.at[side, rows_of(3, k)],
            dst_ref=gath.at[side, rows_of(place(1 - side), k)],
            send_sem=z_send.at[side, k],
            recv_sem=z_recv.at[side, k],
            device_id={"sect": up if side == 0 else down},
            device_id_type=MESH,
        )

    def pack_bound(k):
        for side in range(2):
            edge = sect == (n_sect - 1 if side == 0 else 0)
            here = k == (0 if side == 0 else channels - 1)
            one = jnp.where(here, 1.0, 0.0)
            rows = jnp.zeros((16, N), F32)
            base = 3 * region + k * PACK
            for j in range(SEC):
                upper, row = pack(bound[side, k, j].astype(F32), masks)
                upper = jnp.where(edge, eye_packed * one, upper)
                row = jnp.where(edge, eye_row * one, row)
                outb[side, pl.ds(pl.multiple_of(base + j * HALF, 16), HALF)] = upper.astype(BF16)
                rows = jnp.where(row16 == j, jnp.broadcast_to(row, (16, N)), rows)
            outb[side, pl.ds(pl.multiple_of(base + SEC * HALF, 16), 16)] = rows.astype(BF16)
            z_copy(side, k).start()

    def ring_copy(side, which, k, back):
        at = place(side)
        if which == 2:
            at = (at + (1 if back else SIDE - 1)) % SIDE
        step = SIDE - 1 if back else 1
        return pltpu.make_async_remote_copy(
            src_ref=gath.at[side, rows_of(at, k)],
            dst_ref=gath.at[side, rows_of(at, k)],
            send_sem=ring_send.at[side, which, k],
            recv_sem=ring_recv.at[side, which, k],
            device_id={"blk": along(side, step)},
            device_id_type=MESH,
        )

    def dims_mask(slot):
        rows = lax.broadcasted_iota(jnp.int32, (N, N), 0) < table[LDIM + slot]
        cols = lax.broadcasted_iota(jnp.int32, (N, N), 1) < table[RDIM + slot]
        return jnp.logical_and(rows, cols)

    X, HX, T, HT = 0, SLOTS, 2 * SLOTS, 3 * SLOTS

    for load in loads:
        load.wait()

    def beside(side, sector, lo=0, hi=channels):
        return jnp.concatenate([cat[side, sector, k] for k in range(lo, hi)], axis=1)

    def product(blocks, slots, lo=0, hi=channels):
        inner = []
        for block, s in zip(blocks, slots):
            z = dot(block, beside(1, table[RSEC + s], lo, hi)).astype(BF16)
            inner.append(jnp.concatenate([z[:, k * N : (k + 1) * N] for k in range(hi - lo)], axis=0))
        return [dot(beside(0, table[LSEC + s], lo, hi), z) for s, z in zip(slots, inner)]

    bounds = list(range(0, channels, 5)) + [channels]
    groups = list(zip(bounds[:-1], bounds[1:]))

    def apply(lo, hi, i):
        slots = [i * UNROLL + u for u in range(UNROLL)]
        images = product([vec[s] for s in slots], slots, lo, hi)
        for s, image in zip(slots, images):
            work[HX + s] = image if lo == 0 else work[HX + s] + image

    def gather_step(t, _):
        @pl.when(t < channels)
        def _():
            pack_bound(t)

        @pl.when(jnp.logical_and(t >= RING, t < channels + RING))
        def _():
            k = t - RING
            for side in range(2):
                z_copy(side, k).wait_recv()
                ring_copy(side, 0, k, False).start()
                ring_copy(side, 1, k, True).start()

        @pl.when(jnp.logical_and(t >= HAND, t < channels + HAND))
        def _():
            k = t - HAND
            for side in range(2):
                ring_copy(side, 0, k, False).wait_recv()
                ring_copy(side, 1, k, True).wait_recv()

            @pl.when(k % 2 == 0)
            def _():
                for side in range(2):
                    ring_copy(side, 2, k, False).start()

            @pl.when(k % 2 == 1)
            def _():
                for side in range(2):
                    ring_copy(side, 2, k, True).start()

        @pl.when(t == OPEN)
        def _():
            for step in (1, 3, 2):
                psi_copy(step).wait_recv()
            for i in range(8):
                vec[my_w * 8 + i] = ret[my_w * 8 + i]

            def start(i, _):
                vec[i] = jnp.where(dims_mask(i), vec[i].astype(F32), 0.0).astype(BF16)
                return 0

            lax.fori_loop(0, SLOTS, start, 0)

        @pl.when(t >= OPEN)
        def _():
            k = t - OPEN
            for side in range(2):
                ring_copy(side, 2, k, False).wait_recv()

            def open_group(g, _):
                base = g * region + k * PACK
                for side in range(2):
                    rows = gath[side, pl.ds(pl.multiple_of(base + SEC * HALF, 16), 16)].astype(F32)
                    for j in range(SEC):
                        row = jnp.sum(jnp.where(row16 == j, rows, 0.0), axis=0, keepdims=True)
                        packed = gath[side, pl.ds(pl.multiple_of(base + j * HALF, 16), HALF)]
                        cat[side, g * SEC + j, k] = unpack(packed, row, bits)
                return 0

            lax.fori_loop(0, SIDE, open_group, 0)

            for lo, hi in groups[:-1]:

                @pl.when(jnp.logical_and(k >= hi, k < hi + PARTS // 2))
                def _():
                    for n in range(2):
                        apply(lo, hi, (k - hi) * 2 + n)

        return 0

    lax.fori_loop(0, channels + OPEN, gather_step, 0)
    for lo, hi in groups:
        done = min(max(channels - hi, 0) * 2, PARTS) if hi < channels else 0

        def rest(i, _):
            apply(lo, hi, i)
            return 0

        if done < PARTS:
            lax.fori_loop(done, PARTS, rest, 0)

    for step in (1, 3, 2):
        psi_copy(step).wait_send()

    def settle(k, _):
        for side in range(2):
            z_copy(side, k).wait_send()
            for which in range(3):
                ring_copy(side, which, k, False).wait_send()
        return 0

    lax.fori_loop(0, channels, settle, 0)

    def fold(block):
        return jnp.sum(block.reshape(N // 8, 8, N), axis=0)

    def exchange(number, parts):
        rows = [jnp.sum(p, axis=0, keepdims=True) for p in parts]
        rows += [jnp.zeros((1, N), F32)] * (8 - len(rows))
        mine[number] = jnp.concatenate(rows, axis=0)

        def copy(d):
            return pltpu.make_async_remote_copy(
                src_ref=mine.at[number],
                dst_ref=red.at[number, me],
                send_sem=red_send.at[number, d],
                recv_sem=red_recv.at[number, d],
                device_id={"blk": (me + d) % (SIDE * SIDE)},
                device_id_type=MESH,
            )

        for d in range(1, SIDE * SIDE):
            copy(d).start()
        red[number, me] = mine[number]

        for d in range(1, SIDE * SIDE):
            copy(d).wait()
        total = jnp.sum(red[number], axis=0)
        total = jnp.broadcast_to(jnp.sum(total, axis=1, keepdims=True), (8, N))
        return [total[i : i + 1] for i in range(len(parts))]

    zero8 = jnp.zeros((8, N), F32)

    def first_sums(s, sums):
        ss, sh, hh = sums
        start = vec[s].astype(F32)
        image = jnp.where(dims_mask(s), work[HX + s], 0.0)
        work[HX + s] = image
        return ss + fold(start * start), sh + fold(start * image), hh + fold(image * image)

    def several_sums(i, sums):
        for u in range(UNROLL):
            sums = first_sums(i * UNROLL + u, sums)
        return sums

    ss, sh, hh = exchange(0, lax.fori_loop(0, SLOTS // UNROLL, several_sums, (zero8,) * 3))
    norm = jnp.sqrt(ss)
    xx = ss / (norm * norm)
    a = sh / (norm * norm)
    hxhx = hh / (norm * norm)
    b = jnp.sqrt(jnp.maximum(hxhx - 2.0 * a * a + a * a * xx, 0.0) + EPSILON)

    per_norm, per_b = 1.0 / norm, 1.0 / b

    def first_correction(i, sums):
        slots = [i * UNROLL + u for u in range(UNROLL)]
        blocks = []
        for s in slots:
            x = vec[s].astype(F32) * per_norm
            hx = work[HX + s] * per_norm
            t = (hx - a * x) * per_b
            work[X + s] = x
            work[HX + s] = hx
            work[T + s] = t
            blocks.append(t.astype(BF16))
        for s, image in zip(slots, product(blocks, slots)):
            ht = jnp.where(dims_mask(s), image, 0.0)
            work[HT + s] = ht
            x, hx, t = work[X + s], work[HX + s], work[T + s]
            terms = (x * t, t * t, x * ht, t * hx, t * ht, hx * ht, ht * ht)
            sums = tuple(old + fold(term) for old, term in zip(sums, terms))
        return sums

    xt, tt, xht, thx, c, hxht, htht = exchange(
        1, lax.fori_loop(0, SLOTS // UNROLL, first_correction, (zero8,) * 7)
    )

    def ritz(a, b, c):
        value = 0.5 * (a + c) - jnp.sqrt(0.25 * (a - c) * (a - c) + b * b)
        old, new = c - value, -b
        length = jnp.sqrt(old * old + new * new)
        return value, old / length, new / length

    _, p, q = ritz(a, b, c)
    a2 = p * p * a + p * q * (xht + thx) + q * q * c
    xx2 = p * p * xx + 2.0 * p * q * xt + q * q * tt
    hxhx2 = p * p * hxhx + 2.0 * p * q * hxht + q * q * htht
    b2 = jnp.sqrt(jnp.maximum(hxhx2 - 2.0 * a2 * a2 + a2 * a2 * xx2, 0.0) + EPSILON)

    per_b2 = 1.0 / b2

    def second_correction(i, total):
        slots = [i * UNROLL + u for u in range(UNROLL)]
        blocks = []
        for s in slots:
            x = p * work[X + s] + q * work[T + s]
            hx = p * work[HX + s] + q * work[HT + s]
            t = (hx - a2 * x) * per_b2
            work[X + s] = x
            work[T + s] = t
            blocks.append(t.astype(BF16))
        for s, image in zip(slots, product(blocks, slots)):
            total = total + fold(work[T + s] * jnp.where(dims_mask(s), image, 0.0))
        return total

    (c2,) = exchange(2, [lax.fori_loop(0, SLOTS // UNROLL, second_correction, zero8)])
    value, p2, q2 = ritz(a2, b2, c2)
    energy[...] = jnp.broadcast_to(value, (8, N))
    scale = N * math.sqrt(RUN * SIDE * SIDE)

    def final_vector(s, _):
        w = ((p2 * work[X + s] + q2 * work[T + s]) * scale).astype(BF16)
        turned = w.T
        vec[s] = w
        vect[s] = turned
        vecr[s] = pltpu.roll(w.astype(F32), HALF, 1).astype(BF16)
        vectr[s] = pltpu.roll(turned.astype(F32), HALF, 1).astype(BF16)
        return 0

    def final_vectors(i, _):
        for u in range(UNROLL):
            final_vector(i * UNROLL + u, 0)
        return 0

    lax.fori_loop(0, SLOTS // UNROLL, final_vectors, 0)

    def wave_copy(step):
        to_w = (my_w + step) % SIDE
        return pltpu.make_async_remote_copy(
            src_ref=vec.at[pl.ds(to_w * 8, 8)],
            dst_ref=ret.at[pl.ds(my_w * 8, 8)],
            send_sem=psi_send.at[step + 2],
            recv_sem=psi_recv.at[step + 2],
            device_id={"blk": along(0, step)},
            device_id_type=MESH,
        )

    def grow(kind, group, to):
        order, keep, last, live = (
            (ORD_L, KEEP_L, LAST_L, LIVE_L) if kind == 0 else (ORD_R, KEEP_R, LAST_R, LIVE_R)
        )
        outer, sector_at = (vect, LSEC) if kind == 0 else (vec, RSEC)
        closing, closing_rolled = (vec, vecr) if kind == 0 else (vect, vectr)
        nothing = jnp.zeros((N, N), BF16)

        def term(i, _):
            spots = [i * TERMS + u for u in range(TERMS)]
            slots = [table[order + group * 8 + spot] for spot in spots]
            for u, slot in enumerate(slots):
                z = dot(outer[slot], beside(kind, table[sector_at + slot])).astype(BF16)
                for k in range(channels):
                    part = z[:, k * N : (k + 1) * N]
                    stack[u, pl.ds(k * HALF, HALF), pl.ds(0, N)] = part[:HALF]
                    stack[u, pl.ds(k * HALF, HALF), pl.ds(N, N)] = part[HALF:]
            for u, (spot, slot) in enumerate(zip(spots, slots)):
                square = jnp.concatenate(
                    [
                        jnp.concatenate([closing[slot], nothing], axis=1),
                        jnp.concatenate([nothing, closing_rolled[slot]], axis=1),
                    ],
                    axis=0,
                )
                both = dot(stack[u], square)
                stay = table[keep + group * 8 + spot] > 0
                for k in range(channels):
                    rows = both[k * HALF : (k + 1) * HALF]
                    upper = jnp.where(below, rows[:, N:], rows[:, :N])
                    trace = jnp.where(diag_low, rows[:, N:], 0.0)
                    trace = jnp.sum(trace.reshape(HALF // 8, 8, N), axis=0)
                    before = jnp.maximum(spot - 1, 0) * channels + k
                    now = spot * channels + k
                    work[now, pl.ds(0, HALF)] = upper + jnp.where(stay, work[before, pl.ds(0, HALF)], 0.0)
                    work[now, pl.ds(HALF, 8)] = trace + jnp.where(stay, work[before, pl.ds(HALF, 8)], 0.0)
            return 0

        lax.fori_loop(0, 8 // TERMS, term, 0)

        def close(k, diagonals):
            after = []
            for j in range(SEC):
                spot = table[last + group * SEC + j]
                upper = work[spot * channels + k, pl.ds(0, HALF)]
                row = jnp.sum(work[spot * channels + k, pl.ds(HALF, 8)], axis=0, keepdims=True)
                at = pl.multiple_of(to * region + j * deep + k * HALF, 16)
                has = table[live + group * SEC + j] > 0
                outb[kind, pl.ds(at, HALF)] = jnp.where(has, upper, 0.0).astype(BF16)
                after.append(jnp.where(row32 == k, jnp.broadcast_to(row, (32, N)), diagonals[j]))
            return tuple(after)

        diagonals = lax.fori_loop(0, channels, close, (jnp.zeros((32, N), F32),) * SEC)
        for j in range(SEC):
            has = table[live + group * SEC + j] > 0
            at = to * region + j * deep + channels * HALF
            outb[kind, pl.ds(at, 32)] = jnp.where(has, diagonals[j], 0.0).astype(BF16)

    def grow_copy(kind, target, j):
        back = target == 2 or (target == 0 and j >= 2)
        return pltpu.make_async_remote_copy(
            src_ref=outb.at[kind, sector_rows(target, j)],
            dst_ref=gath.at[kind, sector_rows(target, j)],
            send_sem=grow_send.at[kind, target, j],
            recv_sem=grow_recv.at[kind, target, j],
            device_id={"blk": along(1 - kind, SIDE - 1 if back else 1)},
            device_id_type=MESH,
        )

    def my_group(kind, step):
        return ((my_u if kind == 0 else my_w) + step) % SIDE

    for step in (1, 3, 2):
        wave_copy(step).start()
    for kind in range(2):
        grow(kind, my_group(kind, 2), 0)
        for j in (0, 2, 1, 3):
            grow_copy(kind, 0, j).start()
    for kind in range(2):
        grow(kind, my_group(kind, 1), 1)
        for j in (2, 3):
            grow_copy(kind, 1, j).start()
    for kind in range(2):
        grow(kind, my_group(kind, SIDE - 1), 2)
        for j in (0, 1):
            grow_copy(kind, 2, j).start()
    rows = 160 if deep % 160 == 0 else 32
    for j in (0, 2, 1, 3):
        target = 1 if j < 2 else 2
        for kind in range(2):
            grow_copy(kind, 0, j).wait_recv()

            def add(i, _):
                there = pl.ds(pl.multiple_of(target * region + j * deep + i * rows, 16), rows)
                here = pl.ds(pl.multiple_of(j * deep + i * rows, 16), rows)
                total = outb[kind, there].astype(F32) + gath[kind, here].astype(F32)
                outb[kind, there] = total.astype(BF16)
                return 0

            lax.fori_loop(0, deep // rows, add, 0)
            grow_copy(kind, target, j).start()
    for kind in range(2):
        grow(kind, my_group(kind, 0), 3)

    for step in (1, 3, 2):
        wave_copy(step).wait_recv()
    for i in range(8):
        ret[my_w * 8 + i] = vec[my_w * 8 + i]

    def take(e, _):
        wave[e] = ret[table[SLOT_OF + e]]
        return 0

    lax.fori_loop(0, RUN, take, 0)

    shrink = 1.0 / math.sqrt(N)

    def store(kind, j):
        out = left_out if kind == 0 else right_out
        return pltpu.make_async_copy(bound.at[kind, :, j, pl.ds(0, HALF + 16)], out.at[:, j], store_sem.at[kind, j])

    for j, kind in [(j, kind) for j in (0, 2, 1, 3) for kind in range(2)]:
        for target in (1, 2):
            grow_copy(kind, target, j).wait_recv()

        def total(at, size):
            own, before, after = (
                pl.ds(pl.multiple_of(spot * region + j * deep + at, 16), size) for spot in (3, 1, 2)
            )
            parts = outb[kind, own].astype(F32) + gath[kind, before].astype(F32)
            return (parts + gath[kind, after].astype(F32)) * shrink

        diagonals = pltpu.roll(total(channels * HALF, 32), HALF, 1)
        for k in range(channels):
            work[k, pl.ds(0, HALF)] = total(k * HALF, HALF)
            work[k, pl.ds(HALF, 8)] = jnp.broadcast_to(diagonals[k : k + 1], (8, N))

        factor = spread[kind]
        high_part = factor.astype(BF16)
        low_part = (factor - high_part.astype(F32)).astype(BF16)

        def eight(r):
            rows = [work[k, pl.ds(r * 8, 8)] for k in range(channels)]
            rows.append(jnp.zeros((2 * N - 8 * channels, N), F32))
            return jnp.concatenate(rows, axis=0).astype(BF16)

        for start in range(0, 9, 2):
            count = min(2, 9 - start)
            rows = jnp.concatenate([eight(start + n) for n in range(count)], axis=1)
            mixed = dot(high_part, rows) + dot(low_part, rows)
            for v in range(channels):
                for n in range(count):
                    work[32 + v, pl.ds((start + n) * 8, 8)] = mixed[v * 8 : v * 8 + 8, n * N : n * N + N]

        for v in range(channels):
            row = jnp.broadcast_to(work[32 + v, pl.ds(HALF, 1)], (16, N))
            bound[kind, v, j, pl.ds(0, HALF)] = work[32 + v, pl.ds(0, HALF)].astype(BF16)
            bound[kind, v, j, pl.ds(HALF, 16)] = row.astype(BF16)
        store(kind, j).start()
    for kind in range(2):
        for j in range(SEC):
            store(kind, j).wait()
            for target in range(3):
                grow_copy(kind, target, j).wait_send()
    for step in (1, 3, 2):
        wave_copy(step).wait_send()


def finish(wave_in, energy_in, left_in, right_in, wave, energy, left, right, wave_held, packed, whole, load_sem, store_sem):
    channels = left_in.shape[0]
    cuts = [channels * n // 6 for n in range(7)]
    parts = [(kind, lo, hi) for lo, hi in zip(cuts[:-1], cuts[1:]) for kind in range(2)]

    def load(n):
        kind, lo, hi = parts[n]
        source = (left_in, right_in)[kind]
        return pltpu.make_async_copy(
            source.at[pl.ds(lo, hi - lo)], packed.at[kind, pl.ds(lo, hi - lo)], load_sem.at[n]
        )

    def store(n):
        kind, lo, hi = parts[n]
        target = (left, right)[kind]
        return pltpu.make_async_copy(
            whole.at[kind, pl.ds(lo, hi - lo)], target.at[pl.ds(lo, hi - lo)], store_sem.at[n]
        )

    wave_load = pltpu.make_async_copy(wave_in, wave_held, load_sem.at[len(parts)])
    wave_store = pltpu.make_async_copy(wave_held, wave, store_sem.at[len(parts)])
    for n in range(len(parts)):
        load(n).start()
        if n == 1:
            wave_load.start()
    energy[0] = energy_in[0, 0]
    bits = triangle_bits(triangle_masks())
    for n, (kind, lo, hi) in enumerate(parts):
        load(n).wait()

        for k, j in [(k, j) for k in range(lo, hi) for j in range(SEC)]:
            row = packed[kind, k, j, pl.ds(HALF, 16)].astype(F32)[:1]
            whole[kind, k, j] = unpack(packed[kind, k, j, pl.ds(0, HALF)], row, bits)
        store(n).start()
        if n == 1:
            wave_load.wait()
            wave_store.start()
    for n in range(len(parts)):
        store(n).wait()
    wave_store.wait()


def body(
    left_boundary,
    right_boundary,
    psi_start,
    left_local,
    right_group,
    right_local,
    left_dims,
    right_dims,
    left_mix,
    right_mix,
):
    channels = left_boundary.shape[1]
    smem = pl.BlockSpec(memory_space=pltpu.SMEM)
    vmem = pl.BlockSpec(memory_space=pltpu.VMEM)
    hbm = pl.BlockSpec(memory_space=pl.ANY)
    table = pl.pallas_call(
        router,
        out_shape=jax.ShapeDtypeStruct((TABLE,), jnp.int32),
        in_specs=[smem] * 5,
        out_specs=smem,
        scratch_shapes=[pltpu.SMEM((16,), jnp.int32)],
        name="router",
    )(
        left_local,
        right_group[:, :, 0],
        right_local,
        left_dims,
        right_dims,
    )
    dma = pltpu.SemaphoreType.DMA
    env = (channels, SEC, N, N)
    region = max(channels * PACK, SEC * (channels * HALF + 32))
    wave, energy, left_grown, right_grown = pl.pallas_call(
        lambda *refs: kernel(channels, *refs),
        out_shape=(
            jax.ShapeDtypeStruct((RUN, N, N), BF16),
            jax.ShapeDtypeStruct((8, N), F32),
            jax.ShapeDtypeStruct((channels, SEC, HALF + 16, N), BF16),
            jax.ShapeDtypeStruct((channels, SEC, HALF + 16, N), BF16),
        ),
        in_specs=[smem, smem, smem, hbm, hbm, vmem],
        out_specs=(vmem, vmem, hbm, hbm),
        scratch_shapes=[
            pltpu.VMEM((2,) + env, BF16),
            pltpu.VMEM((2, SIDE * SEC, channels, N, N), BF16),
            pltpu.VMEM((2, SIDE * region, N), BF16),
            pltpu.VMEM((2, SIDE * region, N), BF16),
            pltpu.VMEM((max(4 * SLOTS, 8 * channels), N, N), F32),
            pltpu.VMEM((SLOTS, N, N), BF16),
            pltpu.VMEM((SLOTS, N, N), BF16),
            pltpu.VMEM((SLOTS, N, N), BF16),
            pltpu.VMEM((SLOTS, N, N), BF16),
            pltpu.VMEM((SLOTS, N, N), BF16),
            pltpu.VMEM((TERMS, channels * HALF, 2 * N), BF16),
            pltpu.VMEM((2, -(-channels // 2) * 16, 2 * N), F32),
            pltpu.VMEM((3, SIDE * SIDE, 8, N), F32),
            pltpu.VMEM((3, 8, N), F32),
            dma((2,)),
            dma((2, SEC)),
            dma((6,)),
            dma((6,)),
            dma((2, channels)),
            dma((2, channels)),
            dma((2, 3, channels)),
            dma((2, 3, channels)),
            dma((3, SIDE * SIDE)),
            dma((3, SIDE * SIDE)),
            dma((2, 3, SEC)),
            dma((2, 3, SEC)),
        ],
        compiler_params=pltpu.CompilerParams(
            collective_id=0, has_side_effects=True, vmem_limit_bytes=62 * 2**20
        ),
        name="davidson",
    )(
        table,
        left_mix,
        right_mix,
        left_boundary[0],
        right_boundary[0],
        psi_start[0],
    )
    wave, energy, left_grown, right_grown = pl.pallas_call(
        finish,
        out_shape=(
            jax.ShapeDtypeStruct(wave.shape, BF16),
            jax.ShapeDtypeStruct((1,), F32),
            jax.ShapeDtypeStruct(env, BF16),
            jax.ShapeDtypeStruct(env, BF16),
        ),
        in_specs=[hbm, vmem, hbm, hbm],
        out_specs=(hbm, smem, hbm, hbm),
        scratch_shapes=[
            pltpu.VMEM(wave.shape, BF16),
            pltpu.VMEM((2, channels, SEC, HALF + 16, N), BF16),
            pltpu.VMEM((2,) + env, BF16),
            dma((13,)),
            dma((13,)),
        ],
        compiler_params=pltpu.CompilerParams(vmem_limit_bytes=62 * 2**20),
        name="finish",
    )(wave, energy, left_grown, right_grown)
    return wave[None], energy, left_grown[None], right_grown[None]


def solution(mesh):
    return jax.shard_map(
        body,
        mesh=mesh,
        in_specs=(
            P("sect", None, "blk", None, None),
            P("sect", None, "blk", None, None),
            P("sect", "blk", None, None),
            P("sect", None),
            P("sect", None, None),
            P("sect", None),
            P("sect", None),
            P("sect", None),
            P(),
            P(),
        ),
        out_specs=(
            P("sect", "blk", None, None),
            P("sect"),
            P("sect", None, "blk", None, None),
            P("sect", None, "blk", None, None),
        ),
        check_vma=False,
    )
```
